32 devices in a mesh: chan: 16 (over z, y, x), src: 2 (over core).
Axes of the slice: x: 2, y: 2, z: 4, core: 2. Of those that a mesh axis runs over, the one named last changes fastest.
Arguments:
- strain: bfloat16 [256, 65536], P('src', 'chan'), may hold values from -6 to 6
- seg_start: int32 [3], replicated, may hold values from 0 to 8704
- src_chan: int32 [256], replicated, may hold values from 0 to 255
Outputs:
- correlation: bfloat16 [256, 2, 128, 512], P('src', None, 'chan')
The draws below stay inside these ranges and needn't reach their ends.
All inputs are finite; a program needn't handle non-finite values.
Results may differ from the reference program's by a relative error of at most 0.0083.
Values may be sent and summed in bfloat16 or wider, within the bound.
No kernel may reach another device: no remote copies, remote signals or barrier semaphores. Data moves between devices by JAX's collectives and lax.ppermute only.
A program may use at most 64 MiB of HBM per device.

```python
import math
import jax
import jax.numpy as jnp
import numpy as np
from jax import lax

NT = 65536
DEC = 4
SEG = 7680
NSEG = 3
BIN_LOW = 61
NBIN = 384
NLAG = 512
NSRC = 256
NTD = 16384
NCH = 256
N_SRC = 2


def touch_ends(array, key, smallest, largest):
    dims = array.shape
    spot = [jax.random.randint(jax.random.fold_in(key, axis), (), 0, dims[axis]) for axis in range(len(dims))]
    array = array.at[tuple(spot)].set(smallest)
    longest = dims.index(max(dims))
    spot[longest] = (spot[longest] + 1) % dims[longest]
    return array.at[tuple(spot)].set(largest)


def shard_levels(own_key, extent, shards, least, largest):
    factor_of, own = 1.0, jax.random.fold_in(own_key, 6)
    for position, shards_of in shards:
        draws = jnp.exp(jax.random.uniform(jax.random.fold_in(own, position), (shards_of,), jnp.float32, least / len(shards), largest / len(shards)))
        factor_of = factor_of * jnp.repeat(draws, extent[position] // shards_of).reshape([-1 if axis == position else 1 for axis in range(len(extent))])
    return factor_of


def bell_draw(own_key, dims, deviation, limit, cuts=(), kind=jnp.bfloat16):
    drawn = jax.random.normal(own_key, dims, jnp.float32) * deviation
    if len(cuts) > 0:
        drawn = shard_levels(own_key, dims, cuts, -0.22, 0.18) * drawn
    return jnp.clip(drawn, min=-limit, max=limit).astype(kind)


def setup_inputs(seed: int = 0) -> dict:
    key_list = jax.random.split(jax.random.key(seed), 4)
    strain = bell_draw(key_list[0], (NCH, NT), 1.0, 6.0, ((0, 2), (1, 16)))
    seg_start = jax.random.randint(key_list[1], (NSEG,), 0, NTD - SEG + 1).astype(jnp.int32)
    src_chan = touch_ends(jax.random.randint(key_list[2], (NSRC,), 0, NCH), jax.random.fold_in(key_list[2], 1), 0, NCH - 1).astype(jnp.int32)
    return dict(strain=strain, seg_start=seg_start, src_chan=src_chan)


def decimation_tables():
    length = 4 * DEC
    offsets = np.arange(length)
    centred = (offsets - (length - 1) / 2.0) / DEC
    coeffs = np.sin(np.pi * centred) / (np.pi * centred) * (0.54 - 0.46 * np.cos(2.0 * np.pi * (offsets + 0.5) / length))
    coeffs = coeffs / coeffs.sum()
    sample_pos = np.arange(128)[:, None]
    output_pos = np.arange(128 // DEC)[None, :]
    tables = []
    for carried in (0, 128):
        tap_pos = sample_pos + carried - DEC * output_pos
        inside = (tap_pos >= 0) & (tap_pos < length)
        values = np.where(inside, coeffs[np.clip(tap_pos, 0, length - 1)], 0.0)
        tables.append(jnp.asarray(values, jnp.float32).astype(jnp.bfloat16))
    return (tables[0], tables[1])

def decimate(series, following, first_tab, second_tab):
    row_count, length = series.shape
    blocks = series.reshape(row_count, length // 128, 128)
    shifted = jnp.concatenate([blocks[:, 1:], following[:, None, :]], axis=1)
    summed = jnp.dot(blocks.reshape(-1, 128), first_tab, preferred_element_type=jnp.float32)
    summed = summed + jnp.dot(shifted.reshape(-1, 128), second_tab, preferred_element_type=jnp.float32)
    return summed.astype(jnp.bfloat16).reshape(row_count, length // DEC)

def whiten(spectrum):
    real_part = spectrum[..., :NBIN]
    imag_part = spectrum[..., NBIN:]
    energy = real_part * real_part + imag_part * imag_part
    offsets = np.arange(NBIN)
    band_mask = jnp.asarray((np.abs(offsets[:, None] - offsets[None, :]) <= 32).astype(np.float32))
    smooth = jnp.matmul(energy, band_mask, precision=lax.Precision.HIGHEST) / 65.0
    inverse = lax.rsqrt(smooth + 1e-05)
    return jnp.concatenate([real_part * inverse, imag_part * inverse], axis=-1).astype(jnp.bfloat16)

def lag_table():
    bin_ids = BIN_LOW + np.arange(NBIN)
    delays = np.arange(NLAG) - NLAG // 2
    angles = 2.0 * np.pi * np.mod(np.outer(bin_ids, delays), SEG) / SEG
    basis = np.concatenate([np.cos(angles), -np.sin(angles)], axis=0) / np.sqrt(NBIN)
    return jnp.asarray(basis, jnp.float32).astype(jnp.bfloat16)

def reference(strain, seg_start, src_chan):
    channels, samples = strain.shape
    block_rows = math.gcd(channels, 64)
    first_tab, second_tab = decimation_tables()

    def spectra_of(strain_block):
        padding = jnp.zeros((block_rows, 128), jnp.bfloat16)
        decimated = decimate(strain_block, padding, first_tab, second_tab)
        pieces = [lax.dynamic_slice_in_dim(decimated, seg_start[number], SEG, 1) for number in range(NSEG)]
        segments = jnp.stack(pieces, axis=1).astype(jnp.float32)
        transform = jnp.fft.rfft(segments, axis=-1)[..., BIN_LOW:BIN_LOW + NBIN] / math.sqrt(SEG)
        spectrum = jnp.concatenate([jnp.real(transform), jnp.imag(transform)], axis=-1)
        return whiten(spectrum)
    spectra = lax.map(spectra_of, strain.reshape(channels // block_rows, block_rows, samples))
    receivers = spectra.reshape(channels, NSEG, 2 * NBIN).astype(jnp.float32)
    sources = receivers[src_chan]
    basis = lag_table()
    recv_re = receivers[..., :NBIN]
    recv_im = receivers[..., NBIN:]
    highest = lax.Precision.HIGHEST

    def per_group(source_block):
        source_re = source_block[..., :NBIN]
        source_im = source_block[..., NBIN:]
        cross_re = jnp.einsum('ksf,rsf->krf', source_re, recv_re, precision=highest)
        cross_re = (cross_re + jnp.einsum('ksf,rsf->krf', source_im, recv_im, precision=highest)) / NSEG
        cross_im = jnp.einsum('ksf,rsf->krf', source_re, recv_im, precision=highest)
        cross_im = (cross_im - jnp.einsum('ksf,rsf->krf', source_im, recv_re, precision=highest)) / NSEG
        merged = jnp.concatenate([cross_re, cross_im], axis=-1).astype(jnp.bfloat16)
        lagged = jnp.dot(merged.reshape(-1, 2 * NBIN), basis, preferred_element_type=jnp.float32)
        return lagged.astype(jnp.bfloat16).reshape(source_block.shape[0], channels, NLAG)
    result = lax.map(per_group, sources.reshape(NSRC // 8, 8, NSEG, 2 * NBIN))
    return result.reshape(NSRC, N_SRC, channels // N_SRC, NLAG)
```

```python
import math

import jax
import jax.numpy as jnp
import numpy as np
from jax import lax
from jax.experimental import pallas as pl
from jax.experimental.pallas import tpu as pltpu
from jax.sharding import PartitionSpec as P

DEC = 4
SEG = 7680
NSEG = 3
BIN_LOW = 61
NBIN = 384
NLAG = 512
LANES = 128
BLOCK = 512
HALVES = 2
CHUNKS = NBIN // LANES
VMEM = pl.BlockSpec(memory_space=pltpu.VMEM)
SMEM = pl.BlockSpec(memory_space=pltpu.SMEM)


def filter_table():
    length = 4 * DEC
    offsets = np.arange(length)
    centred = (offsets - (length - 1) / 2.0) / DEC
    coeffs = (
        np.sin(np.pi * centred)
        / (np.pi * centred)
        * (0.54 - 0.46 * np.cos(2.0 * np.pi * (offsets + 0.5) / length))
    )
    coeffs = coeffs / coeffs.sum()
    tap = np.arange(DEC * LANES + LANES)[:, None] - DEC * np.arange(LANES)[None, :]
    inside = (tap >= 0) & (tap < length)
    values = np.where(inside, coeffs[np.clip(tap, 0, length - 1)], 0.0)
    return jnp.asarray(values, jnp.float32).astype(jnp.bfloat16)


def inner_table():
    bin_ids = BIN_LOW + np.arange(NBIN)
    angle = 2.0 * np.pi * np.mod(np.outer(np.arange(BLOCK), bin_ids), SEG) / SEG
    parts = np.stack([np.cos(angle), -np.sin(angle)], axis=1)
    parts = parts.reshape(BLOCK, 2, CHUNKS, LANES).transpose(0, 2, 1, 3)
    return jnp.asarray(parts.reshape(BLOCK, 2 * NBIN), jnp.float32).astype(jnp.bfloat16)


def phase_table(first, count):
    bin_ids = BIN_LOW + np.arange(NBIN)
    angle = 2.0 * np.pi * np.mod(np.outer(BLOCK * (first + np.arange(count)), bin_ids), SEG) / SEG
    parts = np.stack([np.cos(angle), np.sin(angle)], axis=1) / math.sqrt(SEG)
    return jnp.asarray(parts.reshape(count, 1, 2 * NBIN), jnp.float32)


def lag_table():
    bin_ids = BIN_LOW + np.arange(NBIN)
    delays = np.arange(NLAG) - NLAG // 2
    angles = 2.0 * np.pi * np.mod(np.outer(bin_ids, delays), SEG) / SEG
    basis = np.concatenate([np.cos(angles), -np.sin(angles)], axis=0) / np.sqrt(NBIN)
    return jnp.asarray(basis, jnp.float32).astype(jnp.bfloat16)


def band_table():
    offsets = np.arange(NBIN)
    band = np.abs(offsets[:, None] - offsets[None, :]) <= 32
    return jnp.asarray(band.astype(np.float32)).astype(jnp.bfloat16)


def dot(left, right):
    return jnp.dot(left, right, preferred_element_type=jnp.float32)


def decimate_kernel(strain_ref, table_ref, out_ref):
    halves, rows, length = strain_ref.shape
    group = out_ref.shape[1] // halves
    tiles = length // BLOCK
    x = strain_ref[...].reshape(halves * rows, length)

    def put(values, at):
        for peer in range(rows // group):
            part = [
                values[half * rows + peer * group : half * rows + (peer + 1) * group]
                for half in range(halves)
            ]
            out_ref[peer, :, at : at + LANES] = jnp.concatenate(part, axis=0).astype(jnp.bfloat16)

    for tile in range(tiles):
        stop = min(BLOCK * tile + BLOCK + LANES, length)
        piece = x[:, BLOCK * tile : stop]
        put(dot(piece, table_ref[: piece.shape[1], :]), tile * LANES)
    put(dot(x[:, :LANES], table_ref[BLOCK:, :]), tiles * LANES)


def decimate(strain, peers, group):
    rows, length = strain.shape
    half_rows = rows // HALVES
    width = length // DEC + LANES
    steps = 2
    return pl.pallas_call(
        decimate_kernel,
        out_shape=jax.ShapeDtypeStruct((peers, HALVES * group, width), jnp.bfloat16),
        grid=(steps,),
        in_specs=[
            pl.BlockSpec((HALVES, half_rows // steps, length), lambda i: (0, i, 0)),
            pl.BlockSpec((BLOCK + LANES, LANES), lambda i: (0, 0)),
        ],
        out_specs=pl.BlockSpec((peers // steps, HALVES * group, width), lambda i: (i, 0, 0)),
        name="decimate",
    )(strain.reshape(HALVES, half_rows, length), filter_table())


def spectrum_kernel(place_ref, start_ref, recv_ref, inner_ref, phase_ref, own_ref, send_ref, lhs, edge):
    peers, rows, width = recv_ref.shape
    span = width - LANES
    blocks = peers * span // BLOCK
    base = place_ref[0] * (peers * span)
    first = place_ref[0] * blocks
    starts = [start_ref[number] for number in range(NSEG)]
    lane = lax.broadcasted_iota(jnp.int32, (rows, LANES), 1)

    def windows(values, at):
        pos = lane + at
        return [
            jnp.where((pos >= start) & (pos < start + SEG), values, 0.0).astype(jnp.bfloat16)
            for start in starts
        ]

    for peer in range(peers):
        for tile in range(span // LANES):
            values = recv_ref[peer, :, tile * LANES : (tile + 1) * LANES].astype(jnp.float32)
            if tile == span // LANES - 1 and peer + 1 < peers:
                values = values + recv_ref[peer + 1, :, span:].astype(jnp.float32)
            at = peer * span + tile * LANES
            block, inside = divmod(at, BLOCK)
            for number, part in enumerate(windows(values, base + at)):
                row = (block * NSEG + number) * rows
                lhs[row : row + rows, inside : inside + LANES] = part
    for number, part in enumerate(windows(recv_ref[0, :, span:].astype(jnp.float32), base - LANES)):
        edge[number * rows : (number + 1) * rows, :] = part
    many = NSEG * rows
    for chunk in range(CHUNKS):
        columns = slice(2 * chunk * LANES, 2 * (chunk + 1) * LANES)
        re_at = slice(chunk * LANES, (chunk + 1) * LANES)
        im_at = slice(NBIN + chunk * LANES, NBIN + (chunk + 1) * LANES)
        table = inner_ref[:, columns]
        body = dot(lhs[...], table)
        parts = [dot(edge[...], table[BLOCK - LANES :])]
        parts += [body[block * many : (block + 1) * many] for block in range(blocks)]
        total_re = total_im = 0.0
        for number, part in enumerate(parts):
            cos, sin = phase_ref[first + number, :, re_at], phase_ref[first + number, :, im_at]
            part_re, part_im = part[:, :LANES], part[:, LANES:]
            total_re = total_re + (part_re * cos + part_im * sin)
            total_im = total_im + (part_im * cos - part_re * sin)
        own_ref[:, re_at] = total_re
        own_ref[:, im_at] = total_im
        send_ref[:, re_at] = total_re.astype(jnp.bfloat16)
        send_ref[:, im_at] = total_im.astype(jnp.bfloat16)


def partial_spectrum(place, seg_start, recv):
    peers, rows, width = recv.shape
    blocks = peers * (width - LANES) // BLOCK
    many = NSEG * rows
    return pl.pallas_call(
        spectrum_kernel,
        out_shape=[
            jax.ShapeDtypeStruct((many, 2 * NBIN), jnp.float32),
            jax.ShapeDtypeStruct((many, 2 * NBIN), jnp.bfloat16),
        ],
        in_specs=[SMEM, SMEM, VMEM, VMEM, VMEM],
        out_specs=[VMEM, VMEM],
        scratch_shapes=[
            pltpu.VMEM((blocks * many, BLOCK), jnp.bfloat16),
            pltpu.VMEM((many, LANES), jnp.bfloat16),
        ],
        compiler_params=pltpu.CompilerParams(vmem_limit_bytes=32 * 1024 * 1024),
        name="spectrum",
    )(place, seg_start, recv, inner_table(), phase_table(-1, HALVES * blocks + 1))


def whiten_kernel(own_ref, other_ref, band_ref, out_ref):
    total = own_ref[...] + other_ref[...].astype(jnp.float32)
    real_part, imag_part = total[:, :NBIN], total[:, NBIN:]
    energy = real_part * real_part + imag_part * imag_part
    high = energy.astype(jnp.bfloat16)
    low = (energy - high.astype(jnp.float32)).astype(jnp.bfloat16)
    smooth = (dot(high, band_ref[...]) + dot(low, band_ref[...])) / 65.0
    inverse = lax.rsqrt(smooth + 1e-05)
    white_re = (real_part * inverse).astype(jnp.bfloat16)
    white_im = (imag_part * inverse).astype(jnp.bfloat16)
    for peer in range(out_ref.shape[0]):
        out_ref[peer, :, :NBIN] = white_re
        out_ref[peer, :, NBIN:] = white_im


def whiten(own, other, peers):
    return pl.pallas_call(
        whiten_kernel,
        out_shape=jax.ShapeDtypeStruct((peers, *own.shape), jnp.bfloat16),
        in_specs=[VMEM] * 3,
        out_specs=VMEM,
        compiler_params=pltpu.CompilerParams(vmem_limit_bytes=32 * 1024 * 1024),
        name="whiten",
    )(own, other, band_table())


def correlate_kernel(groups, group, place_ref, chan_ref, *refs):
    spectra, (basis_ref, out_ref, source, receiver, cross) = refs[:groups], refs[groups:]
    peers = spectra[0].shape[0]
    rows = HALVES * group
    channels = peers * rows
    many = source.shape[1]
    block = out_ref.shape[0] // (groups * group)
    half, peer, mine = place_ref[0], place_ref[1], place_ref[2]

    @pl.when(pl.program_id(0) == 0)
    def _():
        wanted = chan_ref[pl.ds(pl.multiple_of(mine * many, many), many), :]
        spot = lax.broadcasted_iota(jnp.int32, (many, channels), 1)
        total = [0.0] * NSEG
        for step, spectrum in enumerate(spectra):
            owner = lax.rem(mine + step, groups)
            local = wanted - owner * channels
            in_half = jnp.bitwise_and(local, channels // HALVES - 1)
            place = (in_half // group) * rows + (local // (channels // HALVES)) * group + in_half % group
            place = jnp.where((local >= 0) & (local < channels), place, -1)
            pick = (spot == place).astype(jnp.float32).astype(jnp.bfloat16)
            for number in range(NSEG):
                held = spectrum[:, number * rows : (number + 1) * rows, :]
                total[number] = total[number] + dot(pick, held.reshape(channels, 2 * NBIN))
                here = spectrum[peer, number * rows : (number + 1) * rows, :].astype(jnp.float32)
                here = jnp.where(half == 0, here[:group], here[group:]) * (1.0 / NSEG)
                receiver[number, owner] = here
        for number in range(NSEG):
            source[number] = total[number]

    start = pl.program_id(0) * block
    for chunk in range(CHUNKS):
        re_at = slice(chunk * LANES, (chunk + 1) * LANES)
        im_at = slice(NBIN + chunk * LANES, NBIN + (chunk + 1) * LANES)
        recv = [receiver[number].reshape(groups * group, 2 * NBIN) for number in range(NSEG)]
        for k in range(block):
            total_re = total_im = 0.0
            for number in range(NSEG):
                row = source[number, pl.ds(start + k, 1), :]
                source_re, source_im = row[:, re_at], row[:, im_at]
                recv_re, recv_im = recv[number][:, re_at], recv[number][:, im_at]
                total_re = total_re + (source_re * recv_re + source_im * recv_im)
                total_im = total_im + (source_re * recv_im - source_im * recv_re)
            at = slice(k * groups * group, (k + 1) * groups * group)
            cross[at, re_at] = total_re.astype(jnp.bfloat16)
            cross[at, im_at] = total_im.astype(jnp.bfloat16)
    out_ref[...] = dot(cross[...], basis_ref[...]).astype(jnp.bfloat16)


def correlate(place, src_chan, spectra, group):
    groups = len(spectra)
    many = src_chan.shape[0] // groups
    rows = groups * group
    block = max(1, 256 // rows)

    def kernel(*refs):
        correlate_kernel(groups, group, *refs)

    whole = lambda array: pl.BlockSpec(array.shape, lambda i: (0,) * array.ndim)
    column = src_chan.reshape(-1, 1)
    basis = lag_table()
    return pl.pallas_call(
        kernel,
        out_shape=jax.ShapeDtypeStruct((many * rows, NLAG), jnp.bfloat16),
        grid=(many // block,),
        in_specs=[SMEM] + [whole(a) for a in (column, *spectra, basis)],
        out_specs=pl.BlockSpec((block * rows, NLAG), lambda i: (i, 0)),
        scratch_shapes=[
            pltpu.VMEM((NSEG, many, 2 * NBIN), jnp.float32),
            pltpu.VMEM((NSEG, groups, group, 2 * NBIN), jnp.float32),
            pltpu.VMEM((block * rows, 2 * NBIN), jnp.bfloat16),
        ],
        compiler_params=pltpu.CompilerParams(vmem_limit_bytes=56 * 1024 * 1024),
        name="correlate",
    )(place, column, *spectra, basis)


def on_device(strain, seg_start, src_chan):
    chan_count = lax.axis_size("chan")
    group_count = lax.axis_size("src")
    peers = chan_count // HALVES
    per_device = strain.shape[0] // chan_count
    index = lax.axis_index("chan")
    place = jnp.stack([index // peers, index % peers, lax.axis_index("src")]).astype(jnp.int32)
    cubes = [[half * peers + peer for peer in range(peers)] for half in range(HALVES)]

    sent = decimate(strain, peers, per_device)
    samples = lax.all_to_all(sent, "chan", 0, 0, tiled=True, axis_index_groups=cubes)
    own, send = partial_spectrum(place, seg_start, samples)
    across = [(i, (i + peers) % chan_count) for i in range(chan_count)]
    white = whiten(own, lax.ppermute(send, "chan", across), peers)
    held = lax.all_to_all(white, "chan", 0, 0, tiled=True, axis_index_groups=cubes)
    spectra = [held]
    for step in range(1, group_count):
        pairs = [((i + step) % group_count, i) for i in range(group_count)]
        spectra.append(lax.ppermute(held, "src", pairs))
    lagged = correlate(place, src_chan, spectra, per_device)
    return lagged.reshape(-1, group_count, per_device, NLAG)


def solution(mesh):
    return jax.shard_map(
        on_device,
        mesh=mesh,
        in_specs=(P("src", "chan"), P(), P()),
        out_specs=P("src", None, "chan", None),
        check_vma=False,
    )
```

```python
import math

import jax
import jax.numpy as jnp
import numpy as np
from jax import lax
from jax.experimental import pallas as pl
from jax.experimental.pallas import tpu as pltpu
from jax.sharding import PartitionSpec as P

DEC = 4
SEG = 7680
NSEG = 3
BIN_LOW = 61
NBIN = 384
NLAG = 512
LANES = 128
BLOCK = 512
HALVES = 2
CHUNKS = NBIN // LANES
VMEM = pl.BlockSpec(memory_space=pltpu.VMEM)
SMEM = pl.BlockSpec(memory_space=pltpu.SMEM)


def filter_table():
    length = 4 * DEC
    offsets = np.arange(length)
    centred = (offsets - (length - 1) / 2.0) / DEC
    coeffs = (
        np.sin(np.pi * centred)
        / (np.pi * centred)
        * (0.54 - 0.46 * np.cos(2.0 * np.pi * (offsets + 0.5) / length))
    )
    coeffs = coeffs / coeffs.sum()
    tap = np.arange(DEC * LANES + LANES)[:, None] - DEC * np.arange(LANES)[None, :]
    inside = (tap >= 0) & (tap < length)
    values = np.where(inside, coeffs[np.clip(tap, 0, length - 1)], 0.0)
    return jnp.asarray(values, jnp.float32).astype(jnp.bfloat16)


def inner_table():
    bin_ids = BIN_LOW + np.arange(NBIN)
    angle = 2.0 * np.pi * np.mod(np.outer(np.arange(BLOCK), bin_ids), SEG) / SEG
    parts = np.stack([np.cos(angle), -np.sin(angle)], axis=1)
    parts = parts.reshape(BLOCK, 2, CHUNKS, LANES).transpose(0, 2, 1, 3)
    return jnp.asarray(parts.reshape(BLOCK, 2 * NBIN), jnp.float32).astype(jnp.bfloat16)


def phase_table(first, count):
    bin_ids = BIN_LOW + np.arange(NBIN)
    angle = 2.0 * np.pi * np.mod(np.outer(BLOCK * (first + np.arange(count)), bin_ids), SEG) / SEG
    parts = np.stack([np.cos(angle), np.sin(angle)], axis=1) / math.sqrt(SEG)
    return jnp.asarray(parts.reshape(count, 1, 2 * NBIN), jnp.float32)


def lag_table():
    bin_ids = BIN_LOW + np.arange(NBIN)
    delays = np.arange(NLAG) - NLAG // 2
    angles = 2.0 * np.pi * np.mod(np.outer(bin_ids, delays), SEG) / SEG
    basis = np.concatenate([np.cos(angles), -np.sin(angles)], axis=0) / np.sqrt(NBIN)
    return jnp.asarray(basis, jnp.float32).astype(jnp.bfloat16)


def band_table():
    offsets = np.arange(NBIN)
    band = np.abs(offsets[:, None] - offsets[None, :]) <= 32
    return jnp.asarray(band.astype(np.float32)).astype(jnp.bfloat16)


def dot(left, right):
    return jnp.dot(left, right, preferred_element_type=jnp.float32)


def decimate_kernel(strain_ref, table_ref, out_ref):
    halves, rows, length = strain_ref.shape
    group = out_ref.shape[1] // halves
    tiles = length // BLOCK
    x = strain_ref[...].reshape(halves * rows, length)

    def put(values, at):
        for peer in range(rows // group):
            part = [
                values[half * rows + peer * group : half * rows + (peer + 1) * group]
                for half in range(halves)
            ]
            out_ref[peer, :, at : at + LANES] = jnp.concatenate(part, axis=0).astype(jnp.bfloat16)

    for tile in range(tiles):
        stop = min(BLOCK * tile + BLOCK + LANES, length)
        piece = x[:, BLOCK * tile : stop]
        put(dot(piece, table_ref[: piece.shape[1], :]), tile * LANES)
    put(dot(x[:, :LANES], table_ref[BLOCK:, :]), tiles * LANES)


def decimate(strain, peers, group):
    rows, length = strain.shape
    half_rows = rows // HALVES
    width = length // DEC + LANES
    steps = 2
    return pl.pallas_call(
        decimate_kernel,
        out_shape=jax.ShapeDtypeStruct((peers, HALVES * group, width), jnp.bfloat16),
        grid=(steps,),
        in_specs=[
            pl.BlockSpec((HALVES, half_rows // steps, length), lambda i: (0, i, 0)),
            pl.BlockSpec((BLOCK + LANES, LANES), lambda i: (0, 0)),
        ],
        out_specs=pl.BlockSpec((peers // steps, HALVES * group, width), lambda i: (i, 0, 0)),
        name="decimate",
    )(strain.reshape(HALVES, half_rows, length), filter_table())


def spectrum_kernel(place_ref, start_ref, recv_ref, inner_ref, phase_ref, own_ref, send_ref, lhs, edge):
    peers, rows, width = recv_ref.shape
    span = width - LANES
    blocks = peers * span // BLOCK
    base = place_ref[0] * (peers * span)
    first = place_ref[0] * blocks
    starts = [start_ref[number] for number in range(NSEG)]
    lane = lax.broadcasted_iota(jnp.int32, (rows, LANES), 1)

    def windows(values, at):
        pos = lane + at
        return [
            jnp.where((pos >= start) & (pos < start + SEG), values, 0.0).astype(jnp.bfloat16)
            for start in starts
        ]

    for peer in range(peers):
        for tile in range(span // LANES):
            values = recv_ref[peer, :, tile * LANES : (tile + 1) * LANES].astype(jnp.float32)
            if tile == span // LANES - 1 and peer + 1 < peers:
                values = values + recv_ref[peer + 1, :, span:].astype(jnp.float32)
            at = peer * span + tile * LANES
            block, inside = divmod(at, BLOCK)
            for number, part in enumerate(windows(values, base + at)):
                row = (block * NSEG + number) * rows
                lhs[row : row + rows, inside : inside + LANES] = part
    for number, part in enumerate(windows(recv_ref[0, :, span:].astype(jnp.float32), base - LANES)):
        edge[number * rows : (number + 1) * rows, :] = part
    many = NSEG * rows
    for chunk in range(CHUNKS):
        columns = slice(2 * chunk * LANES, 2 * (chunk + 1) * LANES)
        re_at = slice(chunk * LANES, (chunk + 1) * LANES)
        im_at = slice(NBIN + chunk * LANES, NBIN + (chunk + 1) * LANES)
        table = inner_ref[:, columns]
        body = dot(lhs[...], table)
        parts = [dot(edge[...], table[BLOCK - LANES :])]
        parts += [body[block * many : (block + 1) * many] for block in range(blocks)]
        total_re = total_im = 0.0
        for number, part in enumerate(parts):
            cos, sin = phase_ref[first + number, :, re_at], phase_ref[first + number, :, im_at]
            part_re, part_im = part[:, :LANES], part[:, LANES:]
            total_re = total_re + (part_re * cos + part_im * sin)
            total_im = total_im + (part_im * cos - part_re * sin)
        own_ref[:, re_at] = total_re
        own_ref[:, im_at] = total_im
        send_ref[:, re_at] = total_re.astype(jnp.bfloat16)
        send_ref[:, im_at] = total_im.astype(jnp.bfloat16)


def partial_spectrum(place, seg_start, recv):
    peers, rows, width = recv.shape
    blocks = peers * (width - LANES) // BLOCK
    many = NSEG * rows
    return pl.pallas_call(
        spectrum_kernel,
        out_shape=[
            jax.ShapeDtypeStruct((many, 2 * NBIN), jnp.float32),
            jax.ShapeDtypeStruct((many, 2 * NBIN), jnp.bfloat16),
        ],
        in_specs=[SMEM, SMEM, VMEM, VMEM, VMEM],
        out_specs=[VMEM, VMEM],
        scratch_shapes=[
            pltpu.VMEM((blocks * many, BLOCK), jnp.bfloat16),
            pltpu.VMEM((many, LANES), jnp.bfloat16),
        ],
        compiler_params=pltpu.CompilerParams(vmem_limit_bytes=32 * 1024 * 1024),
        name="spectrum",
    )(place, seg_start, recv, inner_table(), phase_table(-1, HALVES * blocks + 1))


def whiten_kernel(own_ref, other_ref, band_ref, out_ref):
    total = own_ref[...] + other_ref[...].astype(jnp.float32)
    real_part, imag_part = total[:, :NBIN], total[:, NBIN:]
    energy = real_part * real_part + imag_part * imag_part
    high = energy.astype(jnp.bfloat16)
    low = (energy - high.astype(jnp.float32)).astype(jnp.bfloat16)
    smooth = (dot(high, band_ref[...]) + dot(low, band_ref[...])) / 65.0
    inverse = lax.rsqrt(smooth + 1e-05)
    white_re = (real_part * inverse).astype(jnp.bfloat16)
    white_im = (imag_part * inverse).astype(jnp.bfloat16)
    for peer in range(out_ref.shape[0]):
        out_ref[peer, :, :NBIN] = white_re
        out_ref[peer, :, NBIN:] = white_im


def whiten(own, other, peers):
    return pl.pallas_call(
        whiten_kernel,
        out_shape=jax.ShapeDtypeStruct((peers, *own.shape), jnp.bfloat16),
        in_specs=[VMEM] * 3,
        out_specs=VMEM,
        compiler_params=pltpu.CompilerParams(vmem_limit_bytes=32 * 1024 * 1024),
        name="whiten",
    )(own, other, band_table())


def correlate_kernel(groups, group, block, place_ref, chan_ref, *refs):
    spectra = refs[:groups]
    basis_ref, out_ref, source, receiver, cross_even, cross_odd, lagged, sent = refs[groups:]
    peers = spectra[0].shape[0]
    rows = HALVES * group
    channels = peers * rows
    receivers = groups * group
    many = chan_ref.shape[1]
    blocks = many // block
    half, peer, mine = place_ref[0], place_ref[1], place_ref[2]

    wanted = chan_ref[pl.ds(mine, 1), :]
    spot = lax.broadcasted_iota(jnp.int32, (channels, many), 0)
    picks = []
    for step, spectrum in enumerate(spectra):
        owner = lax.rem(mine + step, groups)
        local = wanted - owner * channels
        in_half = jnp.bitwise_and(local, channels // HALVES - 1)
        row = (in_half // group) * rows + (local // (channels // HALVES)) * group + in_half % group
        row = jnp.where((local >= 0) & (local < channels), row, -1)
        picks.append((spot == row).astype(jnp.float32))
        for number in range(NSEG):
            here = spectrum[peer, number * rows : (number + 1) * rows, :].astype(jnp.float32)
            here = jnp.where(half == 0, here[:group], here[group:]) * (1.0 / NSEG)
            receiver[number, owner] = here
    pick = jnp.concatenate(picks, axis=0).T.astype(jnp.bfloat16)
    for number in range(NSEG):
        at = slice(number * rows, (number + 1) * rows)
        held = [spectrum[:, at, :].reshape(channels, 2 * NBIN) for spectrum in spectra]
        held = jnp.concatenate(held, axis=0)
        for pair in range(CHUNKS):
            found = dot(pick, held[:, 2 * pair * LANES : 2 * (pair + 1) * LANES])
            source[number, 2 * pair] = found[:, :LANES]
            source[number, 2 * pair + 1] = found[:, LANES:]

    def fill(number, cross):
        for chunk in range(CHUNKS):
            re_at = slice(chunk * LANES, (chunk + 1) * LANES)
            im_at = slice(NBIN + chunk * LANES, NBIN + (chunk + 1) * LANES)
            recv = [receiver[seg].reshape(receivers, 2 * NBIN) for seg in range(NSEG)]
            recv_re = [part[:, re_at].astype(jnp.bfloat16) for part in recv]
            recv_im = [part[:, im_at].astype(jnp.bfloat16) for part in recv]
            for k in range(block):
                total_re = total_im = None
                for seg in range(NSEG):
                    same = pl.ds(number * block + k, 8, stride=0)
                    source_re = source[seg, chunk, same, :]
                    source_im = source[seg, CHUNKS + chunk, same, :]
                    source_re = jnp.concatenate([source_re] * (receivers // 8), axis=0)
                    source_im = jnp.concatenate([source_im] * (receivers // 8), axis=0)
                    source_re = source_re.astype(jnp.bfloat16)
                    source_im = source_im.astype(jnp.bfloat16)
                    part_re = source_re * recv_re[seg] + source_im * recv_im[seg]
                    part_im = source_re * recv_im[seg] - source_im * recv_re[seg]
                    total_re = part_re if seg == 0 else total_re + part_re
                    total_im = part_im if seg == 0 else total_im + part_im
                at = slice(k * receivers, (k + 1) * receivers)
                cross[at, re_at] = total_re
                cross[at, im_at] = total_im

    def span(number):
        size = block * receivers
        return pl.ds(pl.multiple_of(number * size, size), size)

    def lag(number, cross):
        lagged[span(number), :] = dot(cross[...], basis_ref[...]).astype(jnp.bfloat16)

    def store(number):
        at = span(number)
        return pltpu.make_async_copy(lagged.at[at], out_ref.at[at], sent.at[number])

    fill(0, cross_even)

    def step(number, carry):
        lag(2 * number, cross_even)
        fill(2 * number + 1, cross_odd)
        store(2 * number).start()
        lag(2 * number + 1, cross_odd)
        fill(jnp.minimum(2 * number + 2, blocks - 1), cross_even)
        store(2 * number + 1).start()
        return carry

    lax.fori_loop(0, blocks // 2, step, 0)

    def finish(number, carry):
        store(number).wait()
        return carry

    lax.fori_loop(0, blocks, finish, 0)


def correlate(place, src_chan, spectra, group):
    groups = len(spectra)
    many = src_chan.shape[0] // groups
    receivers = groups * group
    block = 256 // receivers
    rows = block * receivers

    def kernel(*refs):
        correlate_kernel(groups, group, block, *refs)

    held = sum(spectrum.size * spectrum.dtype.itemsize for spectrum in spectra)
    return pl.pallas_call(
        kernel,
        out_shape=jax.ShapeDtypeStruct((many * receivers, NLAG), jnp.bfloat16),
        in_specs=[SMEM] + [VMEM] * (groups + 2),
        out_specs=pl.BlockSpec(memory_space=pl.ANY),
        scratch_shapes=[
            pltpu.VMEM((NSEG, 2 * CHUNKS, many, LANES), jnp.float32),
            pltpu.VMEM((NSEG, groups, group, 2 * NBIN), jnp.float32),
            pltpu.VMEM((rows, 2 * NBIN), jnp.bfloat16),
            pltpu.VMEM((rows, 2 * NBIN), jnp.bfloat16),
            pltpu.VMEM((many * receivers, NLAG), jnp.bfloat16),
            pltpu.SemaphoreType.DMA((many // block,)),
        ],
        compiler_params=pltpu.CompilerParams(vmem_limit_bytes=16 * 1024 * 1024 + 2 * held),
        name="correlate",
    )(place, src_chan.reshape(groups, many), *spectra, lag_table())


def on_device(strain, seg_start, src_chan):
    chan_count = lax.axis_size("chan")
    group_count = lax.axis_size("src")
    peers = chan_count // HALVES
    per_device = strain.shape[0] // chan_count
    index = lax.axis_index("chan")
    place = jnp.stack([index // peers, index % peers, lax.axis_index("src")]).astype(jnp.int32)
    cubes = [[half * peers + peer for peer in range(peers)] for half in range(HALVES)]

    sent = decimate(strain, peers, per_device)
    samples = lax.all_to_all(sent, "chan", 0, 0, tiled=True, axis_index_groups=cubes)
    own, send = partial_spectrum(place, seg_start, samples)
    across = [(i, (i + peers) % chan_count) for i in range(chan_count)]
    white = whiten(own, lax.ppermute(send, "chan", across), peers)
    held = lax.all_to_all(white, "chan", 0, 0, tiled=True, axis_index_groups=cubes)
    spectra = [held]
    for step in range(1, group_count):
        pairs = [((i + step) % group_count, i) for i in range(group_count)]
        spectra.append(lax.ppermute(held, "src", pairs))
    lagged = correlate(place, src_chan, spectra, per_device)
    return lagged.reshape(-1, group_count, per_device, NLAG)


def solution(mesh):
    return jax.shard_map(
        on_device,
        mesh=mesh,
        in_specs=(P("src", "chan"), P(), P()),
        out_specs=P("src", None, "chan", None),
        check_vma=False,
    )
```

```python
import math

import jax
import jax.numpy as jnp
import numpy as np
from jax import lax
from jax.experimental import pallas as pl
from jax.experimental.pallas import tpu as pltpu
from jax.sharding import PartitionSpec as P

DEC = 4
SEG = 7680
NSEG = 3
BIN_LOW = 61
NBIN = 384
NLAG = 512
LANES = 128
BLOCK = 512
HALVES = 2
CHUNKS = NBIN // LANES
VMEM = pl.BlockSpec(memory_space=pltpu.VMEM)
SMEM = pl.BlockSpec(memory_space=pltpu.SMEM)


def chunked(real, imag):
    parts = np.stack([real, imag], axis=1).reshape(-1, 2, CHUNKS, LANES)
    return parts.transpose(0, 2, 1, 3).reshape(-1, 2 * NBIN)


def places(chunk):
    start = 2 * chunk * LANES
    return slice(start, start + LANES), slice(start + LANES, start + 2 * LANES)


def filter_table():
    length = 4 * DEC
    offsets = np.arange(length)
    centred = (offsets - (length - 1) / 2.0) / DEC
    coeffs = (
        np.sin(np.pi * centred)
        / (np.pi * centred)
        * (0.54 - 0.46 * np.cos(2.0 * np.pi * (offsets + 0.5) / length))
    )
    coeffs = coeffs / coeffs.sum()
    first = np.concatenate([np.arange(LANES), np.arange(LANES) - LANES])
    tap = np.arange(BLOCK)[:, None] - DEC * first[None, :]
    inside = (tap >= 0) & (tap < length)
    values = np.where(inside, coeffs[np.clip(tap, 0, length - 1)], 0.0)
    return jnp.asarray(values, jnp.float32).astype(jnp.bfloat16)


def inner_table():
    bin_ids = BIN_LOW + np.arange(NBIN)
    angle = 2.0 * np.pi * np.mod(np.outer(np.arange(BLOCK), bin_ids), SEG) / SEG
    parts = chunked(np.cos(angle), -np.sin(angle))
    return jnp.asarray(parts, jnp.float32).astype(jnp.bfloat16)


def phase_table(first, count):
    bin_ids = BIN_LOW + np.arange(NBIN)
    angle = 2.0 * np.pi * np.mod(np.outer(BLOCK * (first + np.arange(count)), bin_ids), SEG) / SEG
    parts = chunked(np.cos(angle), np.sin(angle)) / math.sqrt(SEG)
    return jnp.asarray(parts.reshape(count, 1, 2 * NBIN), jnp.float32)


def lag_table():
    bin_ids = BIN_LOW + np.arange(NBIN)
    delays = np.arange(NLAG) - NLAG // 2
    angles = 2.0 * np.pi * np.mod(np.outer(bin_ids, delays), SEG) / SEG
    basis = chunked(np.cos(angles).T, -np.sin(angles).T).T / np.sqrt(NBIN)
    return jnp.asarray(basis, jnp.float32).astype(jnp.bfloat16)


def band_table():
    offsets = np.arange(NBIN)
    band = np.abs(offsets[:, None] - offsets[None, :]) <= 32
    return jnp.asarray(band.astype(np.float32)).astype(jnp.bfloat16)


def dot(left, right):
    return jnp.dot(left, right, preferred_element_type=jnp.float32)


def decimate_kernel(strain_hbm, table_hbm, out_ref, strain, table, arrived):
    halves, rows, length = strain.shape
    group = out_ref.shape[1] // halves
    tiles = length // BLOCK
    many = halves * rows
    reads = [
        pltpu.make_async_copy(table_hbm, table, arrived.at[0]),
        pltpu.make_async_copy(strain_hbm, strain, arrived.at[1]),
    ]
    for read in reads:
        read.start()
    for read in reads:
        read.wait()
    x = strain[...].reshape(many, length)
    stacked = [x[:, tile * BLOCK : (tile + 1) * BLOCK] for tile in range(tiles)]
    sums = dot(jnp.concatenate(stacked, axis=0), table[...])
    for tile in range(tiles + 1):
        if tile == tiles:
            values = sums[:many, LANES:]
        else:
            values = sums[tile * many : (tile + 1) * many, :LANES]
        if tile + 1 < tiles:
            values = values + sums[(tile + 1) * many : (tile + 2) * many, LANES:]
        for peer in range(rows // group):
            part = [
                values[half * rows + peer * group : half * rows + (peer + 1) * group]
                for half in range(halves)
            ]
            part = jnp.concatenate(part, axis=0).astype(jnp.bfloat16)
            out_ref[peer, :, tile * LANES : (tile + 1) * LANES] = part


def decimate(strain, peers, group):
    rows, length = strain.shape
    half_rows = rows // HALVES
    width = length // DEC + LANES
    return pl.pallas_call(
        decimate_kernel,
        out_shape=jax.ShapeDtypeStruct((peers, HALVES * group, width), jnp.bfloat16),
        in_specs=[pl.BlockSpec(memory_space=pl.ANY)] * 2,
        out_specs=VMEM,
        scratch_shapes=[
            pltpu.VMEM((HALVES, half_rows, length), jnp.bfloat16),
            pltpu.VMEM((BLOCK, 2 * LANES), jnp.bfloat16),
            pltpu.SemaphoreType.DMA((2,)),
        ],
        compiler_params=pltpu.CompilerParams(vmem_limit_bytes=16 * 1024 * 1024),
        name="decimate",
    )(strain.reshape(HALVES, half_rows, length), filter_table())


def spectrum_kernel(place_ref, start_ref, recv_ref, inner_ref, phase_ref, own_ref, send_ref, lhs, edge):
    peers, rows, width = recv_ref.shape
    span = width - LANES
    blocks = peers * span // BLOCK
    base = place_ref[0] * (peers * span)
    first = place_ref[0] * blocks
    starts = [start_ref[number] for number in range(NSEG)]
    lane = lax.broadcasted_iota(jnp.int32, (rows, LANES), 1)

    def windows(values, at):
        pos = lane + at
        return [
            jnp.where((pos >= start) & (pos < start + SEG), values, 0.0).astype(jnp.bfloat16)
            for start in starts
        ]

    for peer in range(peers):
        for tile in range(span // LANES):
            values = recv_ref[peer, :, tile * LANES : (tile + 1) * LANES].astype(jnp.float32)
            if tile == span // LANES - 1 and peer + 1 < peers:
                values = values + recv_ref[peer + 1, :, span:].astype(jnp.float32)
            at = peer * span + tile * LANES
            block, inside = divmod(at, BLOCK)
            for number, part in enumerate(windows(values, base + at)):
                row = (block * NSEG + number) * rows
                lhs[row : row + rows, inside : inside + LANES] = part
    for number, part in enumerate(windows(recv_ref[0, :, span:].astype(jnp.float32), base - LANES)):
        edge[number * rows : (number + 1) * rows, :] = part
    many = NSEG * rows
    for chunk in range(CHUNKS):
        re_at, im_at = places(chunk)
        table = inner_ref[:, re_at.start : im_at.stop]
        body = dot(lhs[...], table)
        parts = [dot(edge[...], table[BLOCK - LANES :])]
        parts += [body[block * many : (block + 1) * many] for block in range(blocks)]
        total_re = total_im = 0.0
        for number, part in enumerate(parts):
            cos, sin = phase_ref[first + number, :, re_at], phase_ref[first + number, :, im_at]
            part_re, part_im = part[:, :LANES], part[:, LANES:]
            total_re = total_re + (part_re * cos + part_im * sin)
            total_im = total_im + (part_im * cos - part_re * sin)
        own_ref[:, re_at] = total_re
        own_ref[:, im_at] = total_im
        send_ref[:, re_at] = total_re.astype(jnp.bfloat16)
        send_ref[:, im_at] = total_im.astype(jnp.bfloat16)


def partial_spectrum(place, seg_start, recv):
    peers, rows, width = recv.shape
    blocks = peers * (width - LANES) // BLOCK
    many = NSEG * rows
    return pl.pallas_call(
        spectrum_kernel,
        out_shape=[
            jax.ShapeDtypeStruct((many, 2 * NBIN), jnp.float32),
            jax.ShapeDtypeStruct((many, 2 * NBIN), jnp.bfloat16),
        ],
        in_specs=[SMEM, SMEM, VMEM, VMEM, VMEM],
        out_specs=[VMEM, VMEM],
        scratch_shapes=[
            pltpu.VMEM((blocks * many, BLOCK), jnp.bfloat16),
            pltpu.VMEM((many, LANES), jnp.bfloat16),
        ],
        compiler_params=pltpu.CompilerParams(vmem_limit_bytes=32 * 1024 * 1024),
        name="spectrum",
    )(place, seg_start, recv, inner_table(), phase_table(-1, HALVES * blocks + 1))


def whiten_kernel(own_ref, other_ref, band_ref, out_ref):
    total = own_ref[...] + other_ref[...].astype(jnp.float32)
    real_part = jnp.concatenate([total[:, places(chunk)[0]] for chunk in range(CHUNKS)], axis=1)
    imag_part = jnp.concatenate([total[:, places(chunk)[1]] for chunk in range(CHUNKS)], axis=1)
    energy = real_part * real_part + imag_part * imag_part
    high = energy.astype(jnp.bfloat16)
    low = (energy - high.astype(jnp.float32)).astype(jnp.bfloat16)
    smooth = (dot(high, band_ref[...]) + dot(low, band_ref[...])) / 65.0
    inverse = lax.rsqrt(smooth + 1e-05)
    white = []
    for chunk in range(CHUNKS):
        at = slice(chunk * LANES, (chunk + 1) * LANES)
        white += [real_part[:, at] * inverse[:, at], imag_part[:, at] * inverse[:, at]]
    white = jnp.concatenate(white, axis=1).astype(jnp.bfloat16)
    for peer in range(out_ref.shape[0]):
        out_ref[peer] = white


def whiten(own, other, peers):
    return pl.pallas_call(
        whiten_kernel,
        out_shape=jax.ShapeDtypeStruct((peers, *own.shape), jnp.bfloat16),
        in_specs=[VMEM] * 3,
        out_specs=VMEM,
        compiler_params=pltpu.CompilerParams(vmem_limit_bytes=32 * 1024 * 1024),
        name="whiten",
    )(own, other, band_table())


def correlate_kernel(groups, group, block, place_ref, chan_ref, *refs):
    spectra = refs[:groups]
    basis_ref, out_ref, source, receiver, cross_even, cross_odd, lagged, sent = refs[groups:]
    peers = spectra[0].shape[0]
    rows = HALVES * group
    channels = peers * rows
    receivers = groups * group
    many = chan_ref.shape[1]
    blocks = many // block
    half, peer, mine = place_ref[0], place_ref[1], place_ref[2]

    wanted = chan_ref[pl.ds(mine, 1), :]
    spot = lax.broadcasted_iota(jnp.int32, (channels, many), 0)
    picks = []
    for step, spectrum in enumerate(spectra):
        owner = lax.rem(mine + step, groups)
        local = wanted - owner * channels
        in_half = jnp.bitwise_and(local, channels // HALVES - 1)
        row = (in_half // group) * rows + (local // (channels // HALVES)) * group + in_half % group
        row = jnp.where((local >= 0) & (local < channels), row, -1)
        picks.append((spot == row).astype(jnp.float32))
        for number in range(NSEG):
            here = spectrum[peer, number * rows : (number + 1) * rows, :].astype(jnp.float32)
            here = jnp.where(half == 0, here[:group], here[group:]) * (1.0 / NSEG)
            receiver[number, owner] = here
    pick = jnp.concatenate(picks, axis=0).T.astype(jnp.bfloat16)

    def get(chunk):
        columns = slice(2 * chunk * LANES, 2 * (chunk + 1) * LANES)
        for number in range(NSEG):
            at = slice(number * rows, (number + 1) * rows)
            held = [part[:, at, columns].reshape(channels, 2 * LANES) for part in spectra]
            found = dot(pick, jnp.concatenate(held, axis=0))
            source[number, 2 * chunk] = found[:, :LANES]
            source[number, 2 * chunk + 1] = found[:, LANES:]

    def fill(number, cross, chunks):
        for chunk in chunks:
            re_at, im_at = places(chunk)
            recv = [receiver[seg].reshape(receivers, 2 * NBIN) for seg in range(NSEG)]
            recv_re = [part[:, re_at].astype(jnp.bfloat16) for part in recv]
            recv_im = [part[:, im_at].astype(jnp.bfloat16) for part in recv]
            for k in range(block):
                total_re = total_im = None
                for seg in range(NSEG):
                    same = pl.ds(number * block + k, 8, stride=0)
                    source_re = source[seg, 2 * chunk, same, :]
                    source_im = source[seg, 2 * chunk + 1, same, :]
                    source_re = jnp.concatenate([source_re] * (receivers // 8), axis=0)
                    source_im = jnp.concatenate([source_im] * (receivers // 8), axis=0)
                    source_re = source_re.astype(jnp.bfloat16)
                    source_im = source_im.astype(jnp.bfloat16)
                    part_re = source_re * recv_re[seg] + source_im * recv_im[seg]
                    part_im = source_re * recv_im[seg] - source_im * recv_re[seg]
                    total_re = part_re if seg == 0 else total_re + part_re
                    total_im = part_im if seg == 0 else total_im + part_im
                at = slice(k * receivers, (k + 1) * receivers)
                cross[at, re_at] = total_re
                cross[at, im_at] = total_im

    size = block * receivers

    def span(number):
        return pl.ds(pl.multiple_of(number * size, size), size)

    def lag(number, cross):
        lagged[span(number), :] = dot(cross[...], basis_ref[...]).astype(jnp.bfloat16)

    def store(number):
        at = span(number)
        return pltpu.make_async_copy(lagged.at[at], out_ref.at[at], sent.at[number])

    everything = range(CHUNKS)
    for chunk in everything:
        get(chunk)
        fill(0, cross_even, [chunk])

    def pair(number):
        lag(2 * number, cross_even)
        fill(2 * number + 1, cross_odd, everything)
        store(2 * number).start()

    def step(number, carry):
        pair(number)
        lag(2 * number + 1, cross_odd)
        fill(2 * number + 2, cross_even, everything)
        store(2 * number + 1).start()
        return carry

    last = blocks // 2 - 1
    lax.fori_loop(0, last, step, 0)
    pair(last)
    lag(2 * last + 1, cross_odd)
    store(2 * last + 1).start()

    def finish(number, carry):
        store(number).wait()
        return carry

    lax.fori_loop(0, blocks, finish, 0)


def correlate(place, src_chan, spectra, group):
    groups = len(spectra)
    many = src_chan.shape[0] // groups
    receivers = groups * group
    block = 256 // receivers
    rows = block * receivers

    def kernel(*refs):
        correlate_kernel(groups, group, block, *refs)

    held = sum(spectrum.size * spectrum.dtype.itemsize for spectrum in spectra)
    return pl.pallas_call(
        kernel,
        out_shape=jax.ShapeDtypeStruct((many * receivers, NLAG), jnp.bfloat16),
        in_specs=[SMEM] + [VMEM] * (groups + 2),
        out_specs=pl.BlockSpec(memory_space=pl.ANY),
        scratch_shapes=[
            pltpu.VMEM((NSEG, 2 * CHUNKS, many, LANES), jnp.float32),
            pltpu.VMEM((NSEG, groups, group, 2 * NBIN), jnp.float32),
            pltpu.VMEM((rows, 2 * NBIN), jnp.bfloat16),
            pltpu.VMEM((rows, 2 * NBIN), jnp.bfloat16),
            pltpu.VMEM((many * receivers, NLAG), jnp.bfloat16),
            pltpu.SemaphoreType.DMA((many // block,)),
        ],
        compiler_params=pltpu.CompilerParams(vmem_limit_bytes=16 * 1024 * 1024 + 2 * held),
        name="correlate",
    )(place, src_chan.reshape(groups, many), *spectra, lag_table())


def on_device(strain, seg_start, src_chan):
    chan_count = lax.axis_size("chan")
    group_count = lax.axis_size("src")
    peers = chan_count // HALVES
    per_device = strain.shape[0] // chan_count
    index = lax.axis_index("chan")
    place = jnp.stack([index // peers, index % peers, lax.axis_index("src")]).astype(jnp.int32)
    cubes = [[half * peers + peer for peer in range(peers)] for half in range(HALVES)]

    sent = decimate(strain, peers, per_device)
    samples = lax.all_to_all(sent, "chan", 0, 0, tiled=True, axis_index_groups=cubes)
    own, send = partial_spectrum(place, seg_start, samples)
    across = [(i, (i + peers) % chan_count) for i in range(chan_count)]
    white = whiten(own, lax.ppermute(send, "chan", across), peers)
    held = lax.all_to_all(white, "chan", 0, 0, tiled=True, axis_index_groups=cubes)
    spectra = [held]
    for step in range(1, group_count):
        pairs = [((i + step) % group_count, i) for i in range(group_count)]
        spectra.append(lax.ppermute(held, "src", pairs))
    lagged = correlate(place, src_chan, spectra, per_device)
    return lagged.reshape(-1, group_count, per_device, NLAG)


def solution(mesh):
    return jax.shard_map(
        on_device,
        mesh=mesh,
        in_specs=(P("src", "chan"), P(), P()),
        out_specs=P("src", None, "chan", None),
        check_vma=False,
    )
```

```python
import math

import jax
import jax.numpy as jnp
import numpy as np
from jax import lax
from jax.experimental import pallas as pl
from jax.experimental.pallas import tpu as pltpu
from jax.sharding import PartitionSpec as P

DEC = 4
SEG = 7680
NSEG = 3
BIN_LOW = 61
NBIN = 384
NLAG = 512
LANES = 128
BLOCK = 512
HALVES = 2
CHUNKS = NBIN // LANES
VMEM = pl.BlockSpec(memory_space=pltpu.VMEM)
SMEM = pl.BlockSpec(memory_space=pltpu.SMEM)


def chunked(real, imag):
    parts = np.stack([real, imag], axis=1).reshape(-1, 2, CHUNKS, LANES)
    return parts.transpose(0, 2, 1, 3).reshape(-1, 2 * NBIN)


def places(chunk):
    start = 2 * chunk * LANES
    return slice(start, start + LANES), slice(start + LANES, start + 2 * LANES)


def filter_table():
    length = 4 * DEC
    offsets = np.arange(length)
    centred = (offsets - (length - 1) / 2.0) / DEC
    coeffs = (
        np.sin(np.pi * centred)
        / (np.pi * centred)
        * (0.54 - 0.46 * np.cos(2.0 * np.pi * (offsets + 0.5) / length))
    )
    coeffs = coeffs / coeffs.sum()
    first = np.concatenate([np.arange(LANES), np.arange(LANES) - LANES])
    tap = np.arange(BLOCK)[:, None] - DEC * first[None, :]
    inside = (tap >= 0) & (tap < length)
    values = np.where(inside, coeffs[np.clip(tap, 0, length - 1)], 0.0)
    return jnp.asarray(values, jnp.float32).astype(jnp.bfloat16)


def inner_table():
    bin_ids = BIN_LOW + np.arange(NBIN)
    angle = 2.0 * np.pi * np.mod(np.outer(np.arange(BLOCK), bin_ids), SEG) / SEG
    parts = chunked(np.cos(angle), -np.sin(angle))
    return jnp.asarray(parts, jnp.float32).astype(jnp.bfloat16)


def phase_table(first, count):
    bin_ids = BIN_LOW + np.arange(NBIN)
    angle = 2.0 * np.pi * np.mod(np.outer(BLOCK * (first + np.arange(count)), bin_ids), SEG) / SEG
    parts = chunked(np.cos(angle), np.sin(angle)) / math.sqrt(SEG)
    return jnp.asarray(parts.reshape(count, 1, 2 * NBIN), jnp.float32)


def lag_table():
    bin_ids = BIN_LOW + np.arange(NBIN)
    delays = np.arange(NLAG) - NLAG // 2
    angles = 2.0 * np.pi * np.mod(np.outer(bin_ids, delays), SEG) / SEG
    basis = chunked(np.cos(angles).T, -np.sin(angles).T).T / np.sqrt(NBIN)
    return jnp.asarray(basis, jnp.float32).astype(jnp.bfloat16)


def band_table():
    offsets = np.arange(NBIN)
    band = np.abs(offsets[:, None] - offsets[None, :]) <= 32
    return jnp.asarray(band.astype(np.float32)).astype(jnp.bfloat16)


def dot(left, right):
    return jnp.dot(left, right, preferred_element_type=jnp.float32)


def decimate_kernel(strain_ref, table_ref, out_ref):
    halves, rows, length = strain_ref.shape
    group = out_ref.shape[1] // halves
    tiles = length // BLOCK
    many = halves * rows
    x = strain_ref[...].reshape(many, length)
    stacked = [x[:, tile * BLOCK : (tile + 1) * BLOCK] for tile in range(tiles)]
    sums = dot(jnp.concatenate(stacked, axis=0), table_ref[...])
    for tile in range(tiles + 1):
        if tile == tiles:
            values = sums[:many, LANES:]
        else:
            values = sums[tile * many : (tile + 1) * many, :LANES]
        if tile + 1 < tiles:
            values = values + sums[(tile + 1) * many : (tile + 2) * many, LANES:]
        for peer in range(rows // group):
            part = [
                values[half * rows + peer * group : half * rows + (peer + 1) * group]
                for half in range(halves)
            ]
            part = jnp.concatenate(part, axis=0).astype(jnp.bfloat16)
            out_ref[peer, :, tile * LANES : (tile + 1) * LANES] = part


def decimate(strain, peers, group):
    rows, length = strain.shape
    half_rows = rows // HALVES
    width = length // DEC + LANES
    steps = 2
    return pl.pallas_call(
        decimate_kernel,
        out_shape=jax.ShapeDtypeStruct((peers, HALVES * group, width), jnp.bfloat16),
        grid=(steps,),
        in_specs=[
            pl.BlockSpec((HALVES, half_rows // steps, length), lambda i: (0, i, 0)),
            pl.BlockSpec((BLOCK, 2 * LANES), lambda i: (0, 0)),
        ],
        out_specs=pl.BlockSpec((peers // steps, HALVES * group, width), lambda i: (i, 0, 0)),
        name="decimate",
    )(strain.reshape(HALVES, half_rows, length), filter_table())


def spectrum_kernel(place_ref, start_ref, recv_ref, inner_ref, phase_ref, own_ref, send_ref, lhs, edge):
    peers, rows, width = recv_ref.shape
    span = width - LANES
    blocks = peers * span // BLOCK
    base = place_ref[0] * (peers * span)
    first = place_ref[0] * blocks + 1
    starts = [start_ref[number] - base for number in range(NSEG)]

    for peer in range(peers):
        for tile in range(span // LANES):
            values = recv_ref[peer, :, tile * LANES : (tile + 1) * LANES]
            if tile == span // LANES - 1 and peer + 1 < peers:
                carried = recv_ref[peer + 1, :, span:].astype(jnp.float32)
                values = (values.astype(jnp.float32) + carried).astype(jnp.bfloat16)
            block, inside = divmod(peer * span + tile * LANES, BLOCK)
            lhs[block * rows : (block + 1) * rows, inside : inside + LANES] = values

    cuts = []
    lane = lax.broadcasted_iota(jnp.int32, (rows, BLOCK), 1)
    for number, start in enumerate(starts):
        offset = jnp.bitwise_and(start, BLOCK - 1)
        for side, limit in enumerate((start, start + SEG)):
            block = lax.shift_right_arithmetic(limit, jnp.int32(BLOCK.bit_length() - 1))
            held = jnp.clip(block, 0, blocks - 1)
            cut = (block == held) & (offset != 0)
            kept = jnp.where(side == 0, lane >= offset, lane < offset)
            values = lhs[pl.ds(pl.multiple_of(held * rows, rows), rows), :].astype(jnp.float32)
            values = jnp.where(kept & cut, values, 0.0).astype(jnp.bfloat16)
            row = (blocks + len(cuts)) * rows
            lhs[row : row + rows, :] = values
            cuts.append((number, held))
    before = lax.broadcasted_iota(jnp.int32, (rows, LANES), 1) - LANES
    carried = recv_ref[0, :, span:].astype(jnp.float32)
    for number, start in enumerate(starts):
        kept = (before >= start) & (before < start + SEG)
        values = jnp.where(kept, carried, 0.0).astype(jnp.bfloat16)
        edge[number * rows : (number + 1) * rows, :] = values

    whole = [
        [
            ((start <= block * BLOCK) & ((block + 1) * BLOCK <= start + SEG)).astype(jnp.float32)
            for block in range(blocks)
        ]
        for start in starts
    ]
    for chunk in range(CHUNKS):
        re_at, im_at = places(chunk)

        def turned(part, block):
            cos, sin = phase_ref[first + block, :, re_at], phase_ref[first + block, :, im_at]
            part_re, part_im = part[:, :LANES], part[:, LANES:]
            return part_re * cos + part_im * sin, part_im * cos - part_re * sin

        table = inner_ref[:, re_at.start : im_at.stop]
        body = dot(lhs[...], table)
        tail = dot(edge[...], table[BLOCK - LANES :])
        totals = [turned(tail[number * rows : (number + 1) * rows], -1) for number in range(NSEG)]
        for block in range(blocks):
            part_re, part_im = turned(body[block * rows : (block + 1) * rows], block)
            for number in range(NSEG):
                factor = whole[number][block]
                total_re, total_im = totals[number]
                totals[number] = total_re + factor * part_re, total_im + factor * part_im
        for index, (number, block) in enumerate(cuts):
            at = (blocks + index) * rows
            part_re, part_im = turned(body[at : at + rows], block)
            total_re, total_im = totals[number]
            totals[number] = total_re + part_re, total_im + part_im
        for number, (total_re, total_im) in enumerate(totals):
            at = slice(number * rows, (number + 1) * rows)
            own_ref[at, re_at] = total_re
            own_ref[at, im_at] = total_im
            send_ref[at, re_at] = total_re.astype(jnp.bfloat16)
            send_ref[at, im_at] = total_im.astype(jnp.bfloat16)


def partial_spectrum(place, seg_start, recv):
    peers, rows, width = recv.shape
    blocks = peers * (width - LANES) // BLOCK
    many = NSEG * rows
    return pl.pallas_call(
        spectrum_kernel,
        out_shape=[
            jax.ShapeDtypeStruct((many, 2 * NBIN), jnp.float32),
            jax.ShapeDtypeStruct((many, 2 * NBIN), jnp.bfloat16),
        ],
        in_specs=[SMEM, SMEM, VMEM, VMEM, VMEM],
        out_specs=[VMEM, VMEM],
        scratch_shapes=[
            pltpu.VMEM(((blocks + 2 * NSEG) * rows, BLOCK), jnp.bfloat16),
            pltpu.VMEM((many, LANES), jnp.bfloat16),
        ],
        compiler_params=pltpu.CompilerParams(vmem_limit_bytes=32 * 1024 * 1024),
        name="spectrum",
    )(place, seg_start, recv, inner_table(), phase_table(-1, HALVES * blocks + 1))


def whiten_kernel(own_ref, other_ref, band_ref, out_ref):
    total = own_ref[...] + other_ref[...].astype(jnp.float32)
    real_part = jnp.concatenate([total[:, places(chunk)[0]] for chunk in range(CHUNKS)], axis=1)
    imag_part = jnp.concatenate([total[:, places(chunk)[1]] for chunk in range(CHUNKS)], axis=1)
    energy = real_part * real_part + imag_part * imag_part
    high = energy.astype(jnp.bfloat16)
    low = (energy - high.astype(jnp.float32)).astype(jnp.bfloat16)
    smooth = (dot(high, band_ref[...]) + dot(low, band_ref[...])) / 65.0
    inverse = lax.rsqrt(smooth + 1e-05)
    white = []
    for chunk in range(CHUNKS):
        at = slice(chunk * LANES, (chunk + 1) * LANES)
        white += [real_part[:, at] * inverse[:, at], imag_part[:, at] * inverse[:, at]]
    white = jnp.concatenate(white, axis=1).astype(jnp.bfloat16)
    for peer in range(out_ref.shape[0]):
        out_ref[peer] = white


def whiten(own, other, peers):
    return pl.pallas_call(
        whiten_kernel,
        out_shape=jax.ShapeDtypeStruct((peers, *own.shape), jnp.bfloat16),
        in_specs=[VMEM] * 3,
        out_specs=VMEM,
        compiler_params=pltpu.CompilerParams(vmem_limit_bytes=32 * 1024 * 1024),
        name="whiten",
    )(own, other, band_table())


def correlate_kernel(groups, group, block, place_ref, chan_ref, *refs):
    spectra = refs[:groups]
    basis_ref, out_ref, source, receiver, cross_even, cross_odd, lagged, sent = refs[groups:]
    peers = spectra[0].shape[0]
    rows = HALVES * group
    channels = peers * rows
    receivers = groups * group
    many = chan_ref.shape[1]
    blocks = many // block
    half, peer, mine = place_ref[0], place_ref[1], place_ref[2]

    wanted = chan_ref[pl.ds(mine, 1), :]
    spot = lax.broadcasted_iota(jnp.int32, (channels, many), 0)
    picks = []
    for step, spectrum in enumerate(spectra):
        owner = lax.rem(mine + step, groups)
        local = wanted - owner * channels
        in_half = jnp.bitwise_and(local, channels // HALVES - 1)
        row = (in_half // group) * rows + (local // (channels // HALVES)) * group + in_half % group
        row = jnp.where((local >= 0) & (local < channels), row, -1)
        picks.append((spot == row).astype(jnp.float32))
        for number in range(NSEG):
            here = spectrum[peer, number * rows : (number + 1) * rows, :].astype(jnp.float32)
            here = jnp.where(half == 0, here[:group], here[group:]) * (1.0 / NSEG)
            receiver[number, owner] = here
    pick = jnp.concatenate(picks, axis=0).T.astype(jnp.bfloat16)

    def get(chunk):
        columns = slice(2 * chunk * LANES, 2 * (chunk + 1) * LANES)
        for number in range(NSEG):
            at = slice(number * rows, (number + 1) * rows)
            held = [part[:, at, columns].reshape(channels, 2 * LANES) for part in spectra]
            found = dot(pick, jnp.concatenate(held, axis=0))
            source[number, 2 * chunk] = found[:, :LANES]
            source[number, 2 * chunk + 1] = found[:, LANES:]

    def fill(number, cross, chunks):
        for chunk in chunks:
            re_at, im_at = places(chunk)
            recv = [receiver[seg].reshape(receivers, 2 * NBIN) for seg in range(NSEG)]
            recv_re = [part[:, re_at].astype(jnp.bfloat16) for part in recv]
            recv_im = [part[:, im_at].astype(jnp.bfloat16) for part in recv]
            for k in range(block):
                total_re = total_im = None
                for seg in range(NSEG):
                    same = pl.ds(number * block + k, 8, stride=0)
                    source_re = source[seg, 2 * chunk, same, :]
                    source_im = source[seg, 2 * chunk + 1, same, :]
                    source_re = jnp.concatenate([source_re] * (receivers // 8), axis=0)
                    source_im = jnp.concatenate([source_im] * (receivers // 8), axis=0)
                    source_re = source_re.astype(jnp.bfloat16)
                    source_im = source_im.astype(jnp.bfloat16)
                    part_re = source_re * recv_re[seg] + source_im * recv_im[seg]
                    part_im = source_re * recv_im[seg] - source_im * recv_re[seg]
                    total_re = part_re if seg == 0 else total_re + part_re
                    total_im = part_im if seg == 0 else total_im + part_im
                at = slice(k * receivers, (k + 1) * receivers)
                cross[at, re_at] = total_re
                cross[at, im_at] = total_im

    size = block * receivers

    def span(number):
        return pl.ds(pl.multiple_of(number * size, size), size)

    def lag(number, cross):
        lagged[span(number), :] = dot(cross[...], basis_ref[...]).astype(jnp.bfloat16)

    def store(number):
        at = span(number)
        return pltpu.make_async_copy(lagged.at[at], out_ref.at[at], sent.at[number])

    everything = range(CHUNKS)
    for chunk in everything:
        get(chunk)
        fill(0, cross_even, [chunk])

    def pair(number):
        lag(2 * number, cross_even)
        fill(2 * number + 1, cross_odd, everything)
        store(2 * number).start()

    def step(number, carry):
        pair(number)
        lag(2 * number + 1, cross_odd)
        fill(2 * number + 2, cross_even, everything)
        store(2 * number + 1).start()
        return carry

    last = blocks // 2 - 1
    lax.fori_loop(0, last, step, 0)
    pair(last)
    lag(2 * last + 1, cross_odd)
    store(2 * last + 1).start()

    def finish(number, carry):
        store(number).wait()
        return carry

    lax.fori_loop(0, blocks, finish, 0)


def correlate(place, src_chan, spectra, group):
    groups = len(spectra)
    many = src_chan.shape[0] // groups
    receivers = groups * group
    block = 256 // receivers
    rows = block * receivers

    def kernel(*refs):
        correlate_kernel(groups, group, block, *refs)

    held = sum(spectrum.size * spectrum.dtype.itemsize for spectrum in spectra)
    return pl.pallas_call(
        kernel,
        out_shape=jax.ShapeDtypeStruct((many * receivers, NLAG), jnp.bfloat16),
        in_specs=[SMEM] + [VMEM] * (groups + 2),
        out_specs=pl.BlockSpec(memory_space=pl.ANY),
        scratch_shapes=[
            pltpu.VMEM((NSEG, 2 * CHUNKS, many, LANES), jnp.float32),
            pltpu.VMEM((NSEG, groups, group, 2 * NBIN), jnp.float32),
            pltpu.VMEM((rows, 2 * NBIN), jnp.bfloat16),
            pltpu.VMEM((rows, 2 * NBIN), jnp.bfloat16),
            pltpu.VMEM((many * receivers, NLAG), jnp.bfloat16),
            pltpu.SemaphoreType.DMA((many // block,)),
        ],
        compiler_params=pltpu.CompilerParams(vmem_limit_bytes=16 * 1024 * 1024 + 2 * held),
        name="correlate",
    )(place, src_chan.reshape(groups, many), *spectra, lag_table())


def on_device(strain, seg_start, src_chan):
    chan_count = lax.axis_size("chan")
    group_count = lax.axis_size("src")
    peers = chan_count // HALVES
    per_device = strain.shape[0] // chan_count
    index = lax.axis_index("chan")
    place = jnp.stack([index // peers, index % peers, lax.axis_index("src")]).astype(jnp.int32)
    cubes = [[half * peers + peer for peer in range(peers)] for half in range(HALVES)]

    sent = decimate(strain, peers, per_device)
    samples = lax.all_to_all(sent, "chan", 0, 0, tiled=True, axis_index_groups=cubes)
    own, send = partial_spectrum(place, seg_start, samples)
    across = [(i, (i + peers) % chan_count) for i in range(chan_count)]
    white = whiten(own, lax.ppermute(send, "chan", across), peers)
    held = lax.all_to_all(white, "chan", 0, 0, tiled=True, axis_index_groups=cubes)
    spectra = [held]
    for step in range(1, group_count):
        pairs = [((i + step) % group_count, i) for i in range(group_count)]
        spectra.append(lax.ppermute(held, "src", pairs))
    lagged = correlate(place, src_chan, spectra, per_device)
    return lagged.reshape(-1, group_count, per_device, NLAG)


def solution(mesh):
    return jax.shard_map(
        on_device,
        mesh=mesh,
        in_specs=(P("src", "chan"), P(), P()),
        out_specs=P("src", None, "chan", None),
        check_vma=False,
    )
```

```python
import math

import jax
import jax.numpy as jnp
import numpy as np
from jax import lax
from jax.experimental import pallas as pl
from jax.experimental.pallas import tpu as pltpu
from jax.sharding import PartitionSpec as P

DEC = 4
SEG = 7680
NSEG = 3
BIN_LOW = 61
NBIN = 384
NLAG = 512
LANES = 128
BLOCK = 512
HALVES = 2
CHUNKS = NBIN // LANES
VMEM = pl.BlockSpec(memory_space=pltpu.VMEM)
SMEM = pl.BlockSpec(memory_space=pltpu.SMEM)


def chunked(real, imag):
    parts = np.stack([real, imag], axis=1).reshape(-1, 2, CHUNKS, LANES)
    return parts.transpose(0, 2, 1, 3).reshape(-1, 2 * NBIN)


def places(chunk):
    start = 2 * chunk * LANES
    return slice(start, start + LANES), slice(start + LANES, start + 2 * LANES)


def filter_table():
    length = 4 * DEC
    offsets = np.arange(length)
    centred = (offsets - (length - 1) / 2.0) / DEC
    coeffs = (
        np.sin(np.pi * centred)
        / (np.pi * centred)
        * (0.54 - 0.46 * np.cos(2.0 * np.pi * (offsets + 0.5) / length))
    )
    coeffs = coeffs / coeffs.sum()
    first = np.concatenate([np.arange(LANES), np.arange(LANES) - LANES])
    tap = np.arange(BLOCK)[:, None] - DEC * first[None, :]
    inside = (tap >= 0) & (tap < length)
    values = np.where(inside, coeffs[np.clip(tap, 0, length - 1)], 0.0)
    return jnp.asarray(values, jnp.float32).astype(jnp.bfloat16)


def inner_table():
    bin_ids = BIN_LOW + np.arange(NBIN)
    angle = 2.0 * np.pi * np.mod(np.outer(np.arange(BLOCK), bin_ids), SEG) / SEG
    parts = chunked(np.cos(angle), -np.sin(angle))
    return jnp.asarray(parts, jnp.float32).astype(jnp.bfloat16)


def phase_table(first, count):
    bin_ids = BIN_LOW + np.arange(NBIN)
    angle = 2.0 * np.pi * np.mod(np.outer(BLOCK * (first + np.arange(count)), bin_ids), SEG) / SEG
    parts = chunked(np.cos(angle), np.sin(angle)) / math.sqrt(SEG)
    return jnp.asarray(parts.reshape(count, 1, 2 * NBIN), jnp.float32)


def lag_table():
    bin_ids = BIN_LOW + np.arange(NBIN)
    delays = np.arange(NLAG) - NLAG // 2
    angles = 2.0 * np.pi * np.mod(np.outer(bin_ids, delays), SEG) / SEG
    basis = chunked(np.cos(angles).T, -np.sin(angles).T).T / np.sqrt(NBIN)
    return jnp.asarray(basis, jnp.float32).astype(jnp.bfloat16)


def band_table():
    offsets = np.arange(NBIN)
    band = np.abs(offsets[:, None] - offsets[None, :]) <= 32
    return jnp.asarray(band.astype(np.float32)).astype(jnp.bfloat16)


def dot(left, right):
    return jnp.dot(left, right, preferred_element_type=jnp.float32)


def decimate_kernel(strain_hbm, table_hbm, out_ref, strain, table, arrived):
    tiles, halves, rows, _ = strain.shape
    group = out_ref.shape[1] // halves
    many = halves * rows
    reads = [pltpu.make_async_copy(table_hbm, table, arrived.at[tiles])]
    for tile in range(tiles):
        piece = strain_hbm.at[:, :, tile * BLOCK : (tile + 1) * BLOCK]
        reads.append(pltpu.make_async_copy(piece, strain.at[tile], arrived.at[tile]))
    for read in reads:
        read.start()
    for read in reads:
        read.wait()
    sums = dot(strain[...].reshape(tiles * many, BLOCK), table[...])
    for tile in range(tiles + 1):
        if tile == tiles:
            values = sums[:many, LANES:]
        else:
            values = sums[tile * many : (tile + 1) * many, :LANES]
        if tile + 1 < tiles:
            values = values + sums[(tile + 1) * many : (tile + 2) * many, LANES:]
        for peer in range(rows // group):
            part = [
                values[half * rows + peer * group : half * rows + (peer + 1) * group]
                for half in range(halves)
            ]
            part = jnp.concatenate(part, axis=0).astype(jnp.bfloat16)
            out_ref[peer, :, tile * LANES : (tile + 1) * LANES] = part


def decimate(strain, peers, group):
    rows, length = strain.shape
    half_rows = rows // HALVES
    width = length // DEC + LANES
    tiles = length // BLOCK
    return pl.pallas_call(
        decimate_kernel,
        out_shape=jax.ShapeDtypeStruct((peers, HALVES * group, width), jnp.bfloat16),
        in_specs=[pl.BlockSpec(memory_space=pltpu.HBM)] * 2,
        out_specs=VMEM,
        scratch_shapes=[
            pltpu.VMEM((tiles, HALVES, half_rows, BLOCK), jnp.bfloat16),
            pltpu.VMEM((BLOCK, 2 * LANES), jnp.bfloat16),
            pltpu.SemaphoreType.DMA((tiles + 1,)),
        ],
        compiler_params=pltpu.CompilerParams(vmem_limit_bytes=16 * 1024 * 1024),
        name="decimate",
    )(strain.reshape(HALVES, half_rows, length), filter_table())


def spectrum_kernel(place_ref, start_ref, recv_ref, inner_ref, phase_ref, own_ref, send_ref, lhs, edge):
    peers, rows, width = recv_ref.shape
    span = width - LANES
    blocks = peers * span // BLOCK
    base = place_ref[0] * (peers * span)
    first = place_ref[0] * blocks + 1
    starts = [start_ref[number] - base for number in range(NSEG)]

    for peer in range(peers):
        for tile in range(span // LANES):
            values = recv_ref[peer, :, tile * LANES : (tile + 1) * LANES]
            if tile == span // LANES - 1 and peer + 1 < peers:
                carried = recv_ref[peer + 1, :, span:].astype(jnp.float32)
                values = (values.astype(jnp.float32) + carried).astype(jnp.bfloat16)
            block, inside = divmod(peer * span + tile * LANES, BLOCK)
            lhs[block * rows : (block + 1) * rows, inside : inside + LANES] = values

    cuts = []
    lane = lax.broadcasted_iota(jnp.int32, (rows, BLOCK), 1)
    for number, start in enumerate(starts):
        offset = jnp.bitwise_and(start, BLOCK - 1)
        for side, limit in enumerate((start, start + SEG)):
            block = lax.shift_right_arithmetic(limit, jnp.int32(BLOCK.bit_length() - 1))
            held = jnp.clip(block, 0, blocks - 1)
            cut = (block == held) & (offset != 0)
            kept = jnp.where(side == 0, lane >= offset, lane < offset)
            values = lhs[pl.ds(pl.multiple_of(held * rows, rows), rows), :].astype(jnp.float32)
            values = jnp.where(kept & cut, values, 0.0).astype(jnp.bfloat16)
            row = (blocks + len(cuts)) * rows
            lhs[row : row + rows, :] = values
            cuts.append((number, held))
    before = lax.broadcasted_iota(jnp.int32, (rows, LANES), 1) - LANES
    carried = recv_ref[0, :, span:].astype(jnp.float32)
    for number, start in enumerate(starts):
        kept = (before >= start) & (before < start + SEG)
        values = jnp.where(kept, carried, 0.0).astype(jnp.bfloat16)
        edge[number * rows : (number + 1) * rows, :] = values

    whole = [
        [
            ((start <= block * BLOCK) & ((block + 1) * BLOCK <= start + SEG)).astype(jnp.float32)
            for block in range(blocks)
        ]
        for start in starts
    ]
    for chunk in range(CHUNKS):
        re_at, im_at = places(chunk)

        def turned(part, block):
            cos, sin = phase_ref[first + block, :, re_at], phase_ref[first + block, :, im_at]
            part_re, part_im = part[:, :LANES], part[:, LANES:]
            return part_re * cos + part_im * sin, part_im * cos - part_re * sin

        table = inner_ref[:, re_at.start : im_at.stop]
        body = dot(lhs[...], table)
        tail = dot(edge[...], table[BLOCK - LANES :])
        totals = [turned(tail[number * rows : (number + 1) * rows], -1) for number in range(NSEG)]
        for block in range(blocks):
            part_re, part_im = turned(body[block * rows : (block + 1) * rows], block)
            for number in range(NSEG):
                factor = whole[number][block]
                total_re, total_im = totals[number]
                totals[number] = total_re + factor * part_re, total_im + factor * part_im
        for index, (number, block) in enumerate(cuts):
            at = (blocks + index) * rows
            part_re, part_im = turned(body[at : at + rows], block)
            total_re, total_im = totals[number]
            totals[number] = total_re + part_re, total_im + part_im
        for number, (total_re, total_im) in enumerate(totals):
            at = slice(number * rows, (number + 1) * rows)
            own_ref[at, re_at] = total_re
            own_ref[at, im_at] = total_im
            send_ref[at, re_at] = total_re.astype(jnp.bfloat16)
            send_ref[at, im_at] = total_im.astype(jnp.bfloat16)


def partial_spectrum(place, seg_start, recv):
    peers, rows, width = recv.shape
    blocks = peers * (width - LANES) // BLOCK
    many = NSEG * rows
    return pl.pallas_call(
        spectrum_kernel,
        out_shape=[
            jax.ShapeDtypeStruct((many, 2 * NBIN), jnp.float32),
            jax.ShapeDtypeStruct((many, 2 * NBIN), jnp.bfloat16),
        ],
        in_specs=[SMEM, SMEM, VMEM, VMEM, VMEM],
        out_specs=[VMEM, VMEM],
        scratch_shapes=[
            pltpu.VMEM(((blocks + 2 * NSEG) * rows, BLOCK), jnp.bfloat16),
            pltpu.VMEM((many, LANES), jnp.bfloat16),
        ],
        compiler_params=pltpu.CompilerParams(vmem_limit_bytes=32 * 1024 * 1024),
        name="spectrum",
    )(place, seg_start, recv, inner_table(), phase_table(-1, HALVES * blocks + 1))


def whiten_kernel(own_ref, other_ref, band_ref, out_ref):
    total = own_ref[...] + other_ref[...].astype(jnp.float32)
    real_part = jnp.concatenate([total[:, places(chunk)[0]] for chunk in range(CHUNKS)], axis=1)
    imag_part = jnp.concatenate([total[:, places(chunk)[1]] for chunk in range(CHUNKS)], axis=1)
    energy = real_part * real_part + imag_part * imag_part
    high = energy.astype(jnp.bfloat16)
    low = (energy - high.astype(jnp.float32)).astype(jnp.bfloat16)
    smooth = (dot(high, band_ref[...]) + dot(low, band_ref[...])) / 65.0
    inverse = lax.rsqrt(smooth + 1e-05)
    white = []
    for chunk in range(CHUNKS):
        at = slice(chunk * LANES, (chunk + 1) * LANES)
        white += [real_part[:, at] * inverse[:, at], imag_part[:, at] * inverse[:, at]]
    white = jnp.concatenate(white, axis=1).astype(jnp.bfloat16)
    for peer in range(out_ref.shape[0]):
        out_ref[peer] = white


def whiten(own, other, peers):
    return pl.pallas_call(
        whiten_kernel,
        out_shape=jax.ShapeDtypeStruct((peers, *own.shape), jnp.bfloat16),
        in_specs=[VMEM] * 3,
        out_specs=VMEM,
        compiler_params=pltpu.CompilerParams(vmem_limit_bytes=32 * 1024 * 1024),
        name="whiten",
    )(own, other, band_table())


def correlate_kernel(groups, group, block, place_ref, chan_ref, *refs):
    spectra = refs[:groups]
    basis_ref, out_ref, source, receiver, cross_even, cross_odd, lagged, sent = refs[groups:]
    peers = spectra[0].shape[0]
    rows = HALVES * group
    channels = peers * rows
    receivers = groups * group
    many = chan_ref.shape[1]
    blocks = many // block
    half, peer, mine = place_ref[0], place_ref[1], place_ref[2]

    wanted = chan_ref[pl.ds(mine, 1), :]
    spot = lax.broadcasted_iota(jnp.int32, (channels, many), 0)
    picks = []
    for step, spectrum in enumerate(spectra):
        owner = lax.rem(mine + step, groups)
        local = wanted - owner * channels
        in_half = jnp.bitwise_and(local, channels // HALVES - 1)
        row = (in_half // group) * rows + (local // (channels // HALVES)) * group + in_half % group
        row = jnp.where((local >= 0) & (local < channels), row, -1)
        picks.append((spot == row).astype(jnp.float32))
        for number in range(NSEG):
            here = spectrum[peer, number * rows : (number + 1) * rows, :].astype(jnp.float32)
            here = jnp.where(half == 0, here[:group], here[group:]) * (1.0 / NSEG)
            receiver[number, owner] = here
    pick = jnp.concatenate(picks, axis=0).T.astype(jnp.bfloat16)

    def get(chunk):
        columns = slice(2 * chunk * LANES, 2 * (chunk + 1) * LANES)
        for number in range(NSEG):
            at = slice(number * rows, (number + 1) * rows)
            held = [part[:, at, columns].reshape(channels, 2 * LANES) for part in spectra]
            found = dot(pick, jnp.concatenate(held, axis=0))
            source[number, 2 * chunk] = found[:, :LANES]
            source[number, 2 * chunk + 1] = found[:, LANES:]

    def fill(number, cross, chunks):
        for chunk in chunks:
            re_at, im_at = places(chunk)
            recv = [receiver[seg].reshape(receivers, 2 * NBIN) for seg in range(NSEG)]
            recv_re = [part[:, re_at].astype(jnp.bfloat16) for part in recv]
            recv_im = [part[:, im_at].astype(jnp.bfloat16) for part in recv]
            for k in range(block):
                total_re = total_im = None
                for seg in range(NSEG):
                    same = pl.ds(number * block + k, 8, stride=0)
                    source_re = source[seg, 2 * chunk, same, :]
                    source_im = source[seg, 2 * chunk + 1, same, :]
                    source_re = jnp.concatenate([source_re] * (receivers // 8), axis=0)
                    source_im = jnp.concatenate([source_im] * (receivers // 8), axis=0)
                    source_re = source_re.astype(jnp.bfloat16)
                    source_im = source_im.astype(jnp.bfloat16)
                    part_re = source_re * recv_re[seg] + source_im * recv_im[seg]
                    part_im = source_re * recv_im[seg] - source_im * recv_re[seg]
                    total_re = part_re if seg == 0 else total_re + part_re
                    total_im = part_im if seg == 0 else total_im + part_im
                at = slice(k * receivers, (k + 1) * receivers)
                cross[at, re_at] = total_re
                cross[at, im_at] = total_im

    size = block * receivers

    def span(number):
        return pl.ds(pl.multiple_of(number * size, size), size)

    def lag(number, cross):
        lagged[span(number), :] = dot(cross[...], basis_ref[...]).astype(jnp.bfloat16)

    def store(number):
        at = span(number)
        return pltpu.make_async_copy(lagged.at[at], out_ref.at[at], sent.at[number])

    everything = range(CHUNKS)
    for chunk in everything:
        get(chunk)
        fill(0, cross_even, [chunk])

    def pair(number):
        lag(2 * number, cross_even)
        fill(2 * number + 1, cross_odd, everything)
        store(2 * number).start()

    def step(number, carry):
        pair(number)
        lag(2 * number + 1, cross_odd)
        fill(2 * number + 2, cross_even, everything)
        store(2 * number + 1).start()
        return carry

    last = blocks // 2 - 1
    lax.fori_loop(0, last, step, 0)
    pair(last)
    lag(2 * last + 1, cross_odd)
    store(2 * last + 1).start()

    def finish(number, carry):
        store(number).wait()
        return carry

    lax.fori_loop(0, blocks, finish, 0)


def correlate(place, src_chan, spectra, group):
    groups = len(spectra)
    many = src_chan.shape[0] // groups
    receivers = groups * group
    block = 256 // receivers
    rows = block * receivers

    def kernel(*refs):
        correlate_kernel(groups, group, block, *refs)

    held = sum(spectrum.size * spectrum.dtype.itemsize for spectrum in spectra)
    return pl.pallas_call(
        kernel,
        out_shape=jax.ShapeDtypeStruct((many * receivers, NLAG), jnp.bfloat16),
        in_specs=[SMEM] + [VMEM] * (groups + 2),
        out_specs=pl.BlockSpec(memory_space=pl.ANY),
        scratch_shapes=[
            pltpu.VMEM((NSEG, 2 * CHUNKS, many, LANES), jnp.float32),
            pltpu.VMEM((NSEG, groups, group, 2 * NBIN), jnp.float32),
            pltpu.VMEM((rows, 2 * NBIN), jnp.bfloat16),
            pltpu.VMEM((rows, 2 * NBIN), jnp.bfloat16),
            pltpu.VMEM((many * receivers, NLAG), jnp.bfloat16),
            pltpu.SemaphoreType.DMA((many // block,)),
        ],
        compiler_params=pltpu.CompilerParams(vmem_limit_bytes=16 * 1024 * 1024 + 2 * held),
        name="correlate",
    )(place, src_chan.reshape(groups, many), *spectra, lag_table())


def on_device(strain, seg_start, src_chan):
    chan_count = lax.axis_size("chan")
    group_count = lax.axis_size("src")
    peers = chan_count // HALVES
    per_device = strain.shape[0] // chan_count
    index = lax.axis_index("chan")
    place = jnp.stack([index // peers, index % peers, lax.axis_index("src")]).astype(jnp.int32)
    cubes = [[half * peers + peer for peer in range(peers)] for half in range(HALVES)]

    sent = decimate(strain, peers, per_device)
    samples = lax.all_to_all(sent, "chan", 0, 0, tiled=True, axis_index_groups=cubes)
    own, send = partial_spectrum(place, seg_start, samples)
    across = [(i, (i + peers) % chan_count) for i in range(chan_count)]
    white = whiten(own, lax.ppermute(send, "chan", across), peers)
    held = lax.all_to_all(white, "chan", 0, 0, tiled=True, axis_index_groups=cubes)
    spectra = [held]
    for step in range(1, group_count):
        pairs = [((i + step) % group_count, i) for i in range(group_count)]
        spectra.append(lax.ppermute(held, "src", pairs))
    lagged = correlate(place, src_chan, spectra, per_device)
    return lagged.reshape(-1, group_count, per_device, NLAG)


def solution(mesh):
    return jax.shard_map(
        on_device,
        mesh=mesh,
        in_specs=(P("src", "chan"), P(), P()),
        out_specs=P("src", None, "chan", None),
        check_vma=False,
    )
```

```python
import math

import jax
import jax.numpy as jnp
import numpy as np
from jax import lax
from jax.experimental import pallas as pl
from jax.experimental.pallas import tpu as pltpu
from jax.sharding import PartitionSpec as P

DEC = 4
SEG = 7680
NSEG = 3
BIN_LOW = 61
NBIN = 384
NLAG = 512
LANES = 128
BLOCK = 512
HALVES = 2
CHUNKS = NBIN // LANES
VMEM = pl.BlockSpec(memory_space=pltpu.VMEM)
SMEM = pl.BlockSpec(memory_space=pltpu.SMEM)


def ordered(peers):
    return [place ^ (place >> 1) for place in range(peers)]


def position(peer):
    peer = peer ^ (peer >> 1)
    peer = peer ^ (peer >> 2)
    return peer ^ (peer >> 4)


def chunked(real, imag):
    parts = np.stack([real, imag], axis=1).reshape(-1, 2, CHUNKS, LANES)
    return parts.transpose(0, 2, 1, 3).reshape(-1, 2 * NBIN)


def places(chunk):
    start = 2 * chunk * LANES
    return slice(start, start + LANES), slice(start + LANES, start + 2 * LANES)


def filter_table():
    length = 4 * DEC
    offsets = np.arange(length)
    centred = (offsets - (length - 1) / 2.0) / DEC
    coeffs = (
        np.sin(np.pi * centred)
        / (np.pi * centred)
        * (0.54 - 0.46 * np.cos(2.0 * np.pi * (offsets + 0.5) / length))
    )
    coeffs = coeffs / coeffs.sum()
    first = np.concatenate([np.arange(LANES), np.arange(LANES) - LANES])
    tap = np.arange(BLOCK)[:, None] - DEC * first[None, :]
    inside = (tap >= 0) & (tap < length)
    values = np.where(inside, coeffs[np.clip(tap, 0, length - 1)], 0.0)
    return jnp.asarray(values, jnp.float32).astype(jnp.bfloat16)


def inner_table():
    bin_ids = BIN_LOW + np.arange(NBIN)
    angle = 2.0 * np.pi * np.mod(np.outer(np.arange(BLOCK), bin_ids), SEG) / SEG
    parts = chunked(np.cos(angle), -np.sin(angle))
    return jnp.asarray(parts, jnp.float32).astype(jnp.bfloat16)


def phase_table(first, count):
    bin_ids = BIN_LOW + np.arange(NBIN)
    angle = 2.0 * np.pi * np.mod(np.outer(BLOCK * (first + np.arange(count)), bin_ids), SEG) / SEG
    parts = chunked(np.cos(angle), np.sin(angle)) / math.sqrt(SEG)
    return jnp.asarray(parts.reshape(count, 1, 2 * NBIN), jnp.float32)


def lag_table():
    bin_ids = BIN_LOW + np.arange(NBIN)
    delays = np.arange(NLAG) - NLAG // 2
    angles = 2.0 * np.pi * np.mod(np.outer(bin_ids, delays), SEG) / SEG
    basis = chunked(np.cos(angles).T, -np.sin(angles).T).T / np.sqrt(NBIN)
    return jnp.asarray(basis, jnp.float32).astype(jnp.bfloat16)


def band_table():
    offsets = np.arange(NBIN)
    band = np.abs(offsets[:, None] - offsets[None, :]) <= 32
    return jnp.asarray(band.astype(np.float32)).astype(jnp.bfloat16)


def dot(left, right):
    return jnp.dot(left, right, preferred_element_type=jnp.float32)


def decimate_kernel(strain_ref, table_ref, out_ref):
    halves, rows, length = strain_ref.shape
    group = out_ref.shape[1] // halves
    tiles = length // BLOCK
    many = halves * rows
    first = pl.program_id(0) * (rows // group)
    x = strain_ref[...].reshape(many, length)
    stacked = [x[:, tile * BLOCK : (tile + 1) * BLOCK] for tile in range(tiles)]
    sums = dot(jnp.concatenate(stacked, axis=0), table_ref[...])
    for tile in range(tiles + 1):
        if tile == tiles:
            values = sums[:many, LANES:]
        else:
            values = sums[tile * many : (tile + 1) * many, :LANES]
        if tile + 1 < tiles:
            values = values + sums[(tile + 1) * many : (tile + 2) * many, LANES:]
        for peer in range(rows // group):
            part = [
                values[half * rows + peer * group : half * rows + (peer + 1) * group]
                for half in range(halves)
            ]
            part = jnp.concatenate(part, axis=0).astype(jnp.bfloat16)
            out_ref[position(first + peer) - first, :, tile * LANES : (tile + 1) * LANES] = part


def decimate(strain, peers, group):
    rows, length = strain.shape
    half_rows = rows // HALVES
    width = length // DEC + LANES
    steps = 2
    return pl.pallas_call(
        decimate_kernel,
        out_shape=jax.ShapeDtypeStruct((peers, HALVES * group, width), jnp.bfloat16),
        grid=(steps,),
        in_specs=[
            pl.BlockSpec((HALVES, half_rows // steps, length), lambda i: (0, i, 0)),
            pl.BlockSpec((BLOCK, 2 * LANES), lambda i: (0, 0)),
        ],
        out_specs=pl.BlockSpec((peers // steps, HALVES * group, width), lambda i: (i, 0, 0)),
        name="decimate",
    )(strain.reshape(HALVES, half_rows, length), filter_table())


def spectrum_kernel(place_ref, start_ref, recv_ref, inner_ref, phase_ref, own_ref, send_ref, lhs, edge):
    peers, rows, width = recv_ref.shape
    span = width - LANES
    blocks = peers * span // BLOCK
    base = place_ref[0] * (peers * span)
    first = place_ref[0] * blocks + 1
    starts = [start_ref[number] - base for number in range(NSEG)]

    for peer in range(peers):
        for tile in range(span // LANES):
            values = recv_ref[position(peer), :, tile * LANES : (tile + 1) * LANES]
            if tile == span // LANES - 1 and peer + 1 < peers:
                carried = recv_ref[position(peer + 1), :, span:].astype(jnp.float32)
                values = (values.astype(jnp.float32) + carried).astype(jnp.bfloat16)
            block, inside = divmod(peer * span + tile * LANES, BLOCK)
            lhs[block * rows : (block + 1) * rows, inside : inside + LANES] = values

    cuts = []
    lane = lax.broadcasted_iota(jnp.int32, (rows, BLOCK), 1)
    for number, start in enumerate(starts):
        offset = jnp.bitwise_and(start, BLOCK - 1)
        for side, limit in enumerate((start, start + SEG)):
            block = lax.shift_right_arithmetic(limit, jnp.int32(BLOCK.bit_length() - 1))
            held = jnp.clip(block, 0, blocks - 1)
            cut = (block == held) & (offset != 0)
            kept = jnp.where(side == 0, lane >= offset, lane < offset)
            values = lhs[pl.ds(pl.multiple_of(held * rows, rows), rows), :].astype(jnp.float32)
            values = jnp.where(kept & cut, values, 0.0).astype(jnp.bfloat16)
            row = (blocks + len(cuts)) * rows
            lhs[row : row + rows, :] = values
            cuts.append((number, held))
    before = lax.broadcasted_iota(jnp.int32, (rows, LANES), 1) - LANES
    carried = recv_ref[0, :, span:].astype(jnp.float32)
    for number, start in enumerate(starts):
        kept = (before >= start) & (before < start + SEG)
        values = jnp.where(kept, carried, 0.0).astype(jnp.bfloat16)
        edge[number * rows : (number + 1) * rows, :] = values

    whole = [
        [
            ((start <= block * BLOCK) & ((block + 1) * BLOCK <= start + SEG)).astype(jnp.float32)
            for block in range(blocks)
        ]
        for start in starts
    ]
    for chunk in range(CHUNKS):
        re_at, im_at = places(chunk)

        def turned(part, block):
            cos, sin = phase_ref[first + block, :, re_at], phase_ref[first + block, :, im_at]
            part_re, part_im = part[:, :LANES], part[:, LANES:]
            return part_re * cos + part_im * sin, part_im * cos - part_re * sin

        table = inner_ref[:, re_at.start : im_at.stop]
        body = dot(lhs[...], table)
        tail = dot(edge[...], table[BLOCK - LANES :])
        totals = [turned(tail[number * rows : (number + 1) * rows], -1) for number in range(NSEG)]
        for block in range(blocks):
            part_re, part_im = turned(body[block * rows : (block + 1) * rows], block)
            for number in range(NSEG):
                factor = whole[number][block]
                total_re, total_im = totals[number]
                totals[number] = total_re + factor * part_re, total_im + factor * part_im
        for index, (number, block) in enumerate(cuts):
            at = (blocks + index) * rows
            part_re, part_im = turned(body[at : at + rows], block)
            total_re, total_im = totals[number]
            totals[number] = total_re + part_re, total_im + part_im
        for number, (total_re, total_im) in enumerate(totals):
            at = slice(number * rows, (number + 1) * rows)
            own_ref[at, re_at] = total_re
            own_ref[at, im_at] = total_im
            send_ref[at, re_at] = total_re.astype(jnp.bfloat16)
            send_ref[at, im_at] = total_im.astype(jnp.bfloat16)


def partial_spectrum(place, seg_start, recv):
    peers, rows, width = recv.shape
    blocks = peers * (width - LANES) // BLOCK
    many = NSEG * rows
    return pl.pallas_call(
        spectrum_kernel,
        out_shape=[
            jax.ShapeDtypeStruct((many, 2 * NBIN), jnp.float32),
            jax.ShapeDtypeStruct((many, 2 * NBIN), jnp.bfloat16),
        ],
        in_specs=[SMEM, SMEM, VMEM, VMEM, VMEM],
        out_specs=[VMEM, VMEM],
        scratch_shapes=[
            pltpu.VMEM(((blocks + 2 * NSEG) * rows, BLOCK), jnp.bfloat16),
            pltpu.VMEM((many, LANES), jnp.bfloat16),
        ],
        compiler_params=pltpu.CompilerParams(vmem_limit_bytes=32 * 1024 * 1024),
        name="spectrum",
    )(place, seg_start, recv, inner_table(), phase_table(-1, HALVES * blocks + 1))


def whiten_kernel(own_ref, other_ref, band_ref, out_ref):
    total = own_ref[...] + other_ref[...].astype(jnp.float32)
    real_part = jnp.concatenate([total[:, places(chunk)[0]] for chunk in range(CHUNKS)], axis=1)
    imag_part = jnp.concatenate([total[:, places(chunk)[1]] for chunk in range(CHUNKS)], axis=1)
    energy = real_part * real_part + imag_part * imag_part
    high = energy.astype(jnp.bfloat16)
    low = (energy - high.astype(jnp.float32)).astype(jnp.bfloat16)
    smooth = (dot(high, band_ref[...]) + dot(low, band_ref[...])) / 65.0
    inverse = lax.rsqrt(smooth + 1e-05)
    white = []
    for chunk in range(CHUNKS):
        at = slice(chunk * LANES, (chunk + 1) * LANES)
        white += [real_part[:, at] * inverse[:, at], imag_part[:, at] * inverse[:, at]]
    white = jnp.concatenate(white, axis=1).astype(jnp.bfloat16)
    for peer in range(out_ref.shape[0]):
        out_ref[peer] = white


def whiten(own, other, peers):
    return pl.pallas_call(
        whiten_kernel,
        out_shape=jax.ShapeDtypeStruct((peers, *own.shape), jnp.bfloat16),
        in_specs=[VMEM] * 3,
        out_specs=VMEM,
        compiler_params=pltpu.CompilerParams(vmem_limit_bytes=32 * 1024 * 1024),
        name="whiten",
    )(own, other, band_table())


def correlate_kernel(groups, group, block, place_ref, chan_ref, *refs):
    spectra = refs[:groups]
    basis_ref, out_ref, source, receiver, cross_even, cross_odd, lagged, sent = refs[groups:]
    peers = spectra[0].shape[0]
    rows = HALVES * group
    channels = peers * rows
    receivers = groups * group
    many = chan_ref.shape[1]
    blocks = many // block
    half, peer, mine = place_ref[0], place_ref[1], place_ref[2]

    wanted = chan_ref[pl.ds(mine, 1), :]
    spot = lax.broadcasted_iota(jnp.int32, (channels, many), 0)
    picks = []
    for step, spectrum in enumerate(spectra):
        owner = lax.rem(mine + step, groups)
        local = wanted - owner * channels
        in_half = jnp.bitwise_and(local, channels // HALVES - 1)
        row = position(in_half // group) * rows + (local // (channels // HALVES)) * group + in_half % group
        row = jnp.where((local >= 0) & (local < channels), row, -1)
        picks.append((spot == row).astype(jnp.float32))
        for number in range(NSEG):
            here = spectrum[position(peer), number * rows : (number + 1) * rows, :].astype(jnp.float32)
            here = jnp.where(half == 0, here[:group], here[group:]) * (1.0 / NSEG)
            receiver[number, owner] = here
    pick = jnp.concatenate(picks, axis=0).T.astype(jnp.bfloat16)

    def get(chunk):
        columns = slice(2 * chunk * LANES, 2 * (chunk + 1) * LANES)
        for number in range(NSEG):
            at = slice(number * rows, (number + 1) * rows)
            held = [part[:, at, columns].reshape(channels, 2 * LANES) for part in spectra]
            found = dot(pick, jnp.concatenate(held, axis=0))
            source[number, 2 * chunk] = found[:, :LANES]
            source[number, 2 * chunk + 1] = found[:, LANES:]

    def fill(number, cross, chunks):
        for chunk in chunks:
            re_at, im_at = places(chunk)
            recv = [receiver[seg].reshape(receivers, 2 * NBIN) for seg in range(NSEG)]
            recv_re = [part[:, re_at].astype(jnp.bfloat16) for part in recv]
            recv_im = [part[:, im_at].astype(jnp.bfloat16) for part in recv]
            for k in range(block):
                total_re = total_im = None
                for seg in range(NSEG):
                    same = pl.ds(number * block + k, 8, stride=0)
                    source_re = source[seg, 2 * chunk, same, :]
                    source_im = source[seg, 2 * chunk + 1, same, :]
                    source_re = jnp.concatenate([source_re] * (receivers // 8), axis=0)
                    source_im = jnp.concatenate([source_im] * (receivers // 8), axis=0)
                    source_re = source_re.astype(jnp.bfloat16)
                    source_im = source_im.astype(jnp.bfloat16)
                    part_re = source_re * recv_re[seg] + source_im * recv_im[seg]
                    part_im = source_re * recv_im[seg] - source_im * recv_re[seg]
                    total_re = part_re if seg == 0 else total_re + part_re
                    total_im = part_im if seg == 0 else total_im + part_im
                at = slice(k * receivers, (k + 1) * receivers)
                cross[at, re_at] = total_re
                cross[at, im_at] = total_im

    size = block * receivers

    def span(number):
        return pl.ds(pl.multiple_of(number * size, size), size)

    def lag(number, cross):
        lagged[span(number), :] = dot(cross[...], basis_ref[...]).astype(jnp.bfloat16)

    def store(number):
        at = span(number)
        return pltpu.make_async_copy(lagged.at[at], out_ref.at[at], sent.at[number])

    everything = range(CHUNKS)
    for chunk in everything:
        get(chunk)
        fill(0, cross_even, [chunk])

    def pair(number):
        lag(2 * number, cross_even)
        fill(2 * number + 1, cross_odd, everything)
        store(2 * number).start()

    def step(number, carry):
        pair(number)
        lag(2 * number + 1, cross_odd)
        fill(2 * number + 2, cross_even, everything)
        store(2 * number + 1).start()
        return carry

    last = blocks // 2 - 1
    lax.fori_loop(0, last, step, 0)
    pair(last)
    lag(2 * last + 1, cross_odd)
    store(2 * last + 1).start()

    def finish(number, carry):
        store(number).wait()
        return carry

    lax.fori_loop(0, blocks, finish, 0)


def correlate(place, src_chan, spectra, group):
    groups = len(spectra)
    many = src_chan.shape[0] // groups
    receivers = groups * group
    block = 256 // receivers
    rows = block * receivers

    def kernel(*refs):
        correlate_kernel(groups, group, block, *refs)

    held = sum(spectrum.size * spectrum.dtype.itemsize for spectrum in spectra)
    return pl.pallas_call(
        kernel,
        out_shape=jax.ShapeDtypeStruct((many * receivers, NLAG), jnp.bfloat16),
        in_specs=[SMEM] + [VMEM] * (groups + 2),
        out_specs=pl.BlockSpec(memory_space=pl.ANY),
        scratch_shapes=[
            pltpu.VMEM((NSEG, 2 * CHUNKS, many, LANES), jnp.float32),
            pltpu.VMEM((NSEG, groups, group, 2 * NBIN), jnp.float32),
            pltpu.VMEM((rows, 2 * NBIN), jnp.bfloat16),
            pltpu.VMEM((rows, 2 * NBIN), jnp.bfloat16),
            pltpu.VMEM((many * receivers, NLAG), jnp.bfloat16),
            pltpu.SemaphoreType.DMA((many // block,)),
        ],
        compiler_params=pltpu.CompilerParams(vmem_limit_bytes=16 * 1024 * 1024 + 2 * held),
        name="correlate",
    )(place, src_chan.reshape(groups, many), *spectra, lag_table())


def on_device(strain, seg_start, src_chan):
    chan_count = lax.axis_size("chan")
    group_count = lax.axis_size("src")
    peers = chan_count // HALVES
    per_device = strain.shape[0] // chan_count
    index = lax.axis_index("chan")
    place = jnp.stack([index // peers, index % peers, lax.axis_index("src")]).astype(jnp.int32)
    cubes = [[half * peers + peer for peer in ordered(peers)] for half in range(HALVES)]

    sent = decimate(strain, peers, per_device)
    samples = lax.all_to_all(sent, "chan", 0, 0, tiled=True, axis_index_groups=cubes)
    own, send = partial_spectrum(place, seg_start, samples)
    across = [(i, (i + peers) % chan_count) for i in range(chan_count)]
    white = whiten(own, lax.ppermute(send, "chan", across), peers)
    held = lax.all_to_all(white, "chan", 0, 0, tiled=True, axis_index_groups=cubes)
    spectra = [held]
    for step in range(1, group_count):
        pairs = [((i + step) % group_count, i) for i in range(group_count)]
        spectra.append(lax.ppermute(held, "src", pairs))
    lagged = correlate(place, src_chan, spectra, per_device)
    return lagged.reshape(-1, group_count, per_device, NLAG)


def solution(mesh):
    return jax.shard_map(
        on_device,
        mesh=mesh,
        in_specs=(P("src", "chan"), P(), P()),
        out_specs=P("src", None, "chan", None),
        check_vma=False,
    )
```

```python
import math

import jax
import jax.numpy as jnp
import numpy as np
from jax import lax
from jax.experimental import pallas as pl
from jax.experimental.pallas import tpu as pltpu
from jax.sharding import PartitionSpec as P

DEC = 4
SEG = 7680
NSEG = 3
BIN_LOW = 61
NBIN = 384
NLAG = 512
LANES = 128
BLOCK = 512
HALVES = 2
CHUNKS = NBIN // LANES
VMEM = pl.BlockSpec(memory_space=pltpu.VMEM)
SMEM = pl.BlockSpec(memory_space=pltpu.SMEM)


def ordered(peers):
    return [place ^ (place >> 1) for place in range(peers)]


def position(peer):
    peer = peer ^ (peer >> 1)
    peer = peer ^ (peer >> 2)
    return peer ^ (peer >> 4)


def chunked(real, imag):
    parts = np.stack([real, imag], axis=1).reshape(-1, 2, CHUNKS, LANES)
    return parts.transpose(0, 2, 1, 3).reshape(-1, 2 * NBIN)


def places(chunk):
    start = 2 * chunk * LANES
    return slice(start, start + LANES), slice(start + LANES, start + 2 * LANES)


def filter_table():
    length = 4 * DEC
    offsets = np.arange(length)
    centred = (offsets - (length - 1) / 2.0) / DEC
    coeffs = (
        np.sin(np.pi * centred)
        / (np.pi * centred)
        * (0.54 - 0.46 * np.cos(2.0 * np.pi * (offsets + 0.5) / length))
    )
    coeffs = coeffs / coeffs.sum()
    first = np.concatenate([np.arange(LANES), np.arange(LANES) - LANES])
    tap = np.arange(BLOCK)[:, None] - DEC * first[None, :]
    inside = (tap >= 0) & (tap < length)
    values = np.where(inside, coeffs[np.clip(tap, 0, length - 1)], 0.0)
    return jnp.asarray(values, jnp.float32).astype(jnp.bfloat16)


def inner_table():
    bin_ids = BIN_LOW + np.arange(NBIN)
    angle = 2.0 * np.pi * np.mod(np.outer(np.arange(BLOCK), bin_ids), SEG) / SEG
    parts = chunked(np.cos(angle), -np.sin(angle))
    return jnp.asarray(parts, jnp.float32).astype(jnp.bfloat16)


def phase_table(first, count):
    bin_ids = BIN_LOW + np.arange(NBIN)
    angle = 2.0 * np.pi * np.mod(np.outer(BLOCK * (first + np.arange(count)), bin_ids), SEG) / SEG
    parts = chunked(np.cos(angle), np.sin(angle)) / math.sqrt(SEG)
    return jnp.asarray(parts.reshape(count, 1, 2 * NBIN), jnp.float32)


def lag_table():
    bin_ids = BIN_LOW + np.arange(NBIN)
    delays = np.arange(NLAG) - NLAG // 2
    angles = 2.0 * np.pi * np.mod(np.outer(bin_ids, delays), SEG) / SEG
    basis = chunked(np.cos(angles).T, -np.sin(angles).T).T / np.sqrt(NBIN)
    return jnp.asarray(basis, jnp.float32).astype(jnp.bfloat16)


def band_table():
    offsets = np.arange(NBIN)
    band = np.abs(offsets[:, None] - offsets[None, :]) <= 32
    return jnp.asarray(band.astype(np.float32)).astype(jnp.bfloat16)


def dot(left, right):
    return jnp.dot(left, right, preferred_element_type=jnp.float32)


def decimate_kernel(strain_ref, table_ref, out_ref):
    halves, rows, length = strain_ref.shape
    group = out_ref.shape[1] // halves
    tiles = length // BLOCK
    many = halves * rows
    first = pl.program_id(0) * (rows // group)
    x = strain_ref[...].reshape(many, length)
    stacked = [x[:, tile * BLOCK : (tile + 1) * BLOCK] for tile in range(tiles)]
    sums = dot(jnp.concatenate(stacked, axis=0), table_ref[...])
    for tile in range(tiles + 1):
        if tile == tiles:
            values = sums[:many, LANES:]
        else:
            values = sums[tile * many : (tile + 1) * many, :LANES]
        if tile + 1 < tiles:
            values = values + sums[(tile + 1) * many : (tile + 2) * many, LANES:]
        for peer in range(rows // group):
            part = [
                values[half * rows + peer * group : half * rows + (peer + 1) * group]
                for half in range(halves)
            ]
            part = jnp.concatenate(part, axis=0).astype(jnp.bfloat16)
            out_ref[position(first + peer) - first, :, tile * LANES : (tile + 1) * LANES] = part


def decimate(strain, peers, group):
    rows, length = strain.shape
    half_rows = rows // HALVES
    width = length // DEC + LANES
    steps = 2
    return pl.pallas_call(
        decimate_kernel,
        out_shape=jax.ShapeDtypeStruct((peers, HALVES * group, width), jnp.bfloat16),
        grid=(steps,),
        in_specs=[
            pl.BlockSpec((HALVES, half_rows // steps, length), lambda i: (0, i, 0)),
            pl.BlockSpec((BLOCK, 2 * LANES), lambda i: (0, 0)),
        ],
        out_specs=pl.BlockSpec((peers // steps, HALVES * group, width), lambda i: (i, 0, 0)),
        name="decimate",
    )(strain.reshape(HALVES, half_rows, length), filter_table())


def spectrum_kernel(info_ref, recv_ref, inner_ref, phase_ref, own_ref, send_ref, lhs, edge):
    peers, rows, width = recv_ref.shape
    span = width - LANES
    blocks = peers * span // BLOCK
    base = info_ref[0] * (peers * span)
    first = info_ref[0] * blocks + 1
    starts = [info_ref[1 + number] - base for number in range(NSEG)]

    for peer in range(peers):
        for tile in range(span // LANES):
            values = recv_ref[position(peer), :, tile * LANES : (tile + 1) * LANES]
            if tile == span // LANES - 1 and peer + 1 < peers:
                carried = recv_ref[position(peer + 1), :, span:].astype(jnp.float32)
                values = (values.astype(jnp.float32) + carried).astype(jnp.bfloat16)
            block, inside = divmod(peer * span + tile * LANES, BLOCK)
            lhs[block * rows : (block + 1) * rows, inside : inside + LANES] = values

    cuts = []
    lane = lax.broadcasted_iota(jnp.int32, (rows, BLOCK), 1)
    for number, start in enumerate(starts):
        offset = jnp.bitwise_and(start, BLOCK - 1)
        for side, limit in enumerate((start, start + SEG)):
            block = lax.shift_right_arithmetic(limit, jnp.int32(BLOCK.bit_length() - 1))
            held = jnp.clip(block, 0, blocks - 1)
            cut = (block == held) & (offset != 0)
            kept = jnp.where(side == 0, lane >= offset, lane < offset)
            values = lhs[pl.ds(pl.multiple_of(held * rows, rows), rows), :].astype(jnp.float32)
            values = jnp.where(kept & cut, values, 0.0).astype(jnp.bfloat16)
            row = (blocks + len(cuts)) * rows
            lhs[row : row + rows, :] = values
            cuts.append((number, held))
    before = lax.broadcasted_iota(jnp.int32, (rows, LANES), 1) - LANES
    carried = recv_ref[0, :, span:].astype(jnp.float32)
    for number, start in enumerate(starts):
        kept = (before >= start) & (before < start + SEG)
        values = jnp.where(kept, carried, 0.0).astype(jnp.bfloat16)
        edge[number * rows : (number + 1) * rows, :] = values

    whole = [
        [
            ((start <= block * BLOCK) & ((block + 1) * BLOCK <= start + SEG)).astype(jnp.float32)
            for block in range(blocks)
        ]
        for start in starts
    ]
    for chunk in range(CHUNKS):
        re_at, im_at = places(chunk)

        def turned(part, block):
            cos, sin = phase_ref[first + block, :, re_at], phase_ref[first + block, :, im_at]
            part_re, part_im = part[:, :LANES], part[:, LANES:]
            return part_re * cos + part_im * sin, part_im * cos - part_re * sin

        table = inner_ref[:, re_at.start : im_at.stop]
        body = dot(lhs[...], table)
        tail = dot(edge[...], table[BLOCK - LANES :])
        totals = [turned(tail[number * rows : (number + 1) * rows], -1) for number in range(NSEG)]
        for block in range(blocks):
            part_re, part_im = turned(body[block * rows : (block + 1) * rows], block)
            for number in range(NSEG):
                factor = whole[number][block]
                total_re, total_im = totals[number]
                totals[number] = total_re + factor * part_re, total_im + factor * part_im
        for index, (number, block) in enumerate(cuts):
            at = (blocks + index) * rows
            part_re, part_im = turned(body[at : at + rows], block)
            total_re, total_im = totals[number]
            totals[number] = total_re + part_re, total_im + part_im
        for number, (total_re, total_im) in enumerate(totals):
            at = slice(number * rows, (number + 1) * rows)
            own_ref[at, re_at] = total_re
            own_ref[at, im_at] = total_im
            send_ref[at, re_at] = total_re.astype(jnp.bfloat16)
            send_ref[at, im_at] = total_im.astype(jnp.bfloat16)


def partial_spectrum(info, recv):
    peers, rows, width = recv.shape
    blocks = peers * (width - LANES) // BLOCK
    many = NSEG * rows
    return pl.pallas_call(
        spectrum_kernel,
        out_shape=[
            jax.ShapeDtypeStruct((many, 2 * NBIN), jnp.float32),
            jax.ShapeDtypeStruct((many, 2 * NBIN), jnp.bfloat16),
        ],
        in_specs=[SMEM, VMEM, VMEM, VMEM],
        out_specs=[VMEM, VMEM],
        scratch_shapes=[
            pltpu.VMEM(((blocks + 2 * NSEG) * rows, BLOCK), jnp.bfloat16),
            pltpu.VMEM((many, LANES), jnp.bfloat16),
        ],
        compiler_params=pltpu.CompilerParams(vmem_limit_bytes=32 * 1024 * 1024),
        name="spectrum",
    )(info, recv, inner_table(), phase_table(-1, HALVES * blocks + 1))


def whiten_kernel(own_ref, other_ref, band_ref, out_ref):
    total = own_ref[...] + other_ref[...].astype(jnp.float32)
    real_part = jnp.concatenate([total[:, places(chunk)[0]] for chunk in range(CHUNKS)], axis=1)
    imag_part = jnp.concatenate([total[:, places(chunk)[1]] for chunk in range(CHUNKS)], axis=1)
    energy = real_part * real_part + imag_part * imag_part
    high = energy.astype(jnp.bfloat16)
    low = (energy - high.astype(jnp.float32)).astype(jnp.bfloat16)
    smooth = (dot(high, band_ref[...]) + dot(low, band_ref[...])) / 65.0
    inverse = lax.rsqrt(smooth + 1e-05)
    white = []
    for chunk in range(CHUNKS):
        at = slice(chunk * LANES, (chunk + 1) * LANES)
        white += [real_part[:, at] * inverse[:, at], imag_part[:, at] * inverse[:, at]]
    white = jnp.concatenate(white, axis=1).astype(jnp.bfloat16)
    for peer in range(out_ref.shape[0]):
        out_ref[peer] = white


def whiten(own, other, peers):
    return pl.pallas_call(
        whiten_kernel,
        out_shape=jax.ShapeDtypeStruct((peers, *own.shape), jnp.bfloat16),
        in_specs=[VMEM] * 3,
        out_specs=VMEM,
        compiler_params=pltpu.CompilerParams(vmem_limit_bytes=32 * 1024 * 1024),
        name="whiten",
    )(own, other, band_table())


def correlate_kernel(groups, group, block, info_ref, *refs):
    spectra = refs[:groups]
    basis_ref, out_ref, source, receiver, cross_even, cross_odd, lagged, sent = refs[groups:]
    rows = HALVES * group
    channels = spectra[0].shape[0] * rows
    receivers = groups * group
    blocks = sent.shape[0]
    half, peer, mine = info_ref[0], info_ref[1], info_ref[2]

    for step, spectrum in enumerate(spectra):
        owner = lax.rem(mine + step, groups)
        for number in range(NSEG):
            here = spectrum[position(peer), number * rows : (number + 1) * rows, :].astype(jnp.float32)
            here = jnp.where(half == 0, here[:group], here[group:]) * (1.0 / NSEG)
            receiver[number, owner] = here

    def widen(chunk):
        for step, spectrum in enumerate(spectra):
            for number in range(NSEG):
                for part, columns in enumerate(places(chunk)):
                    held = spectrum[:, number * rows : (number + 1) * rows, columns]
                    held = held.astype(jnp.float32).reshape(channels, LANES)
                    at = slice(step * channels, (step + 1) * channels)
                    source[number, 2 * chunk + part, at, :] = held

    def fill(number, cross, chunks):
        for chunk in chunks:
            re_at, im_at = places(chunk)
            recv = [receiver[seg].reshape(receivers, 2 * NBIN) for seg in range(NSEG)]
            recv_re = [part[:, re_at].astype(jnp.bfloat16) for part in recv]
            recv_im = [part[:, im_at].astype(jnp.bfloat16) for part in recv]
            for k in range(block):
                total_re = total_im = None
                same = pl.ds(info_ref[3 + number * block + k], 8, stride=0)
                for seg in range(NSEG):
                    source_re = source[seg, 2 * chunk, same, :]
                    source_im = source[seg, 2 * chunk + 1, same, :]
                    source_re = jnp.concatenate([source_re] * (receivers // 8), axis=0)
                    source_im = jnp.concatenate([source_im] * (receivers // 8), axis=0)
                    source_re = source_re.astype(jnp.bfloat16)
                    source_im = source_im.astype(jnp.bfloat16)
                    part_re = source_re * recv_re[seg] + source_im * recv_im[seg]
                    part_im = source_re * recv_im[seg] - source_im * recv_re[seg]
                    total_re = part_re if seg == 0 else total_re + part_re
                    total_im = part_im if seg == 0 else total_im + part_im
                at = slice(k * receivers, (k + 1) * receivers)
                cross[at, re_at] = total_re
                cross[at, im_at] = total_im

    size = block * receivers

    def span(number):
        return pl.ds(pl.multiple_of(number * size, size), size)

    def lag(number, cross):
        lagged[span(number), :] = dot(cross[...], basis_ref[...]).astype(jnp.bfloat16)

    def store(number):
        at = span(number)
        return pltpu.make_async_copy(lagged.at[at], out_ref.at[at], sent.at[number])

    everything = range(CHUNKS)
    for chunk in everything:
        widen(chunk)
        fill(0, cross_even, [chunk])

    def pair(number):
        lag(2 * number, cross_even)
        fill(2 * number + 1, cross_odd, everything)
        store(2 * number).start()

    def step(number, carry):
        pair(number)
        lag(2 * number + 1, cross_odd)
        fill(2 * number + 2, cross_even, everything)
        store(2 * number + 1).start()
        return carry

    last = blocks // 2 - 1
    lax.fori_loop(0, last, step, 0)
    pair(last)
    lag(2 * last + 1, cross_odd)
    store(2 * last + 1).start()

    def finish(number, carry):
        store(number).wait()
        return carry

    lax.fori_loop(0, blocks, finish, 0)


def correlate(info, spectra, group):
    groups = len(spectra)
    many = info.shape[0] - 3
    receivers = groups * group
    channels = groups * spectra[0].shape[0] * HALVES * group
    block = 256 // receivers
    rows = block * receivers

    def kernel(*refs):
        correlate_kernel(groups, group, block, *refs)

    held = sum(spectrum.size * spectrum.dtype.itemsize for spectrum in spectra)
    return pl.pallas_call(
        kernel,
        out_shape=jax.ShapeDtypeStruct((many * receivers, NLAG), jnp.bfloat16),
        in_specs=[SMEM] + [VMEM] * (groups + 1),
        out_specs=pl.BlockSpec(memory_space=pl.ANY),
        scratch_shapes=[
            pltpu.VMEM((NSEG, 2 * CHUNKS, channels, LANES), jnp.float32),
            pltpu.VMEM((NSEG, groups, group, 2 * NBIN), jnp.float32),
            pltpu.VMEM((rows, 2 * NBIN), jnp.bfloat16),
            pltpu.VMEM((rows, 2 * NBIN), jnp.bfloat16),
            pltpu.VMEM((many * receivers, NLAG), jnp.bfloat16),
            pltpu.SemaphoreType.DMA((many // block,)),
        ],
        compiler_params=pltpu.CompilerParams(
            vmem_limit_bytes=min(16 * 1024 * 1024 + 3 * held, 63 * 1024 * 1024)
        ),
        name="correlate",
    )(info, *spectra, lag_table())


def source_rows(src_chan, group_count, local_rows, peers, per_device):
    mine = lax.axis_index("src")
    many = src_chan.shape[0] // group_count
    wanted = lax.dynamic_slice_in_dim(src_chan, mine * many, many, 0)
    step = jnp.mod(wanted // local_rows - mine, group_count)
    local = wanted % local_rows
    half, inside = local // (local_rows // HALVES), local % (local_rows // HALVES)
    place = position(inside // per_device) * HALVES + half
    return step * local_rows + place * per_device + inside % per_device


def on_device(strain, seg_start, src_chan):
    chan_count = lax.axis_size("chan")
    group_count = lax.axis_size("src")
    peers = chan_count // HALVES
    per_device = strain.shape[0] // chan_count
    index = lax.axis_index("chan")
    half = (index // peers).reshape(1).astype(jnp.int32)
    place = jnp.stack([index // peers, index % peers, lax.axis_index("src")]).astype(jnp.int32)
    rows = source_rows(src_chan, group_count, strain.shape[0], peers, per_device)
    cubes = [[half * peers + peer for peer in ordered(peers)] for half in range(HALVES)]

    sent = decimate(strain, peers, per_device)
    samples = lax.all_to_all(sent, "chan", 0, 0, tiled=True, axis_index_groups=cubes)
    own, send = partial_spectrum(jnp.concatenate([half, seg_start]), samples)
    across = [(i, (i + peers) % chan_count) for i in range(chan_count)]
    white = whiten(own, lax.ppermute(send, "chan", across), peers)
    held = lax.all_to_all(white, "chan", 0, 0, tiled=True, axis_index_groups=cubes)
    spectra = [held]
    for step in range(1, group_count):
        pairs = [((i + step) % group_count, i) for i in range(group_count)]
        spectra.append(lax.ppermute(held, "src", pairs))
    lagged = correlate(jnp.concatenate([place, rows]), spectra, per_device)
    return lagged.reshape(-1, group_count, per_device, NLAG)


def solution(mesh):
    return jax.shard_map(
        on_device,
        mesh=mesh,
        in_specs=(P("src", "chan"), P(), P()),
        out_specs=P("src", None, "chan", None),
        check_vma=False,
    )
```

```python
import math

import jax
import jax.numpy as jnp
import numpy as np
from jax import lax
from jax.experimental import pallas as pl
from jax.experimental.pallas import tpu as pltpu
from jax.sharding import PartitionSpec as P

DEC = 4
SEG = 7680
NSEG = 3
BIN_LOW = 61
NBIN = 384
NLAG = 512
LANES = 128
BLOCK = 512
HALVES = 2
CHUNKS = NBIN // LANES
VMEM = pl.BlockSpec(memory_space=pltpu.VMEM)
SMEM = pl.BlockSpec(memory_space=pltpu.SMEM)


def ordered(peers):
    return [place ^ (place >> 1) for place in range(peers)]


def position(peer):
    peer = peer ^ (peer >> 1)
    peer = peer ^ (peer >> 2)
    return peer ^ (peer >> 4)


def chunked(real, imag):
    parts = np.stack([real, imag], axis=1).reshape(-1, 2, CHUNKS, LANES)
    return parts.transpose(0, 2, 1, 3).reshape(-1, 2 * NBIN)


def places(chunk):
    start = 2 * chunk * LANES
    return slice(start, start + LANES), slice(start + LANES, start + 2 * LANES)


def filter_table():
    length = 4 * DEC
    offsets = np.arange(length)
    centred = (offsets - (length - 1) / 2.0) / DEC
    coeffs = (
        np.sin(np.pi * centred)
        / (np.pi * centred)
        * (0.54 - 0.46 * np.cos(2.0 * np.pi * (offsets + 0.5) / length))
    )
    coeffs = coeffs / coeffs.sum()
    first = np.concatenate([np.arange(LANES), np.arange(LANES) - LANES])
    tap = np.arange(BLOCK)[:, None] - DEC * first[None, :]
    inside = (tap >= 0) & (tap < length)
    values = np.where(inside, coeffs[np.clip(tap, 0, length - 1)], 0.0)
    return jnp.asarray(values, jnp.float32).astype(jnp.bfloat16)


def inner_table():
    bin_ids = BIN_LOW + np.arange(NBIN)
    angle = 2.0 * np.pi * np.mod(np.outer(np.arange(BLOCK), bin_ids), SEG) / SEG
    parts = chunked(np.cos(angle), -np.sin(angle))
    return jnp.asarray(parts, jnp.float32).astype(jnp.bfloat16)


def phase_table(first, count):
    bin_ids = BIN_LOW + np.arange(NBIN)
    angle = 2.0 * np.pi * np.mod(np.outer(BLOCK * (first + np.arange(count)), bin_ids), SEG) / SEG
    parts = chunked(np.cos(angle), np.sin(angle)) / math.sqrt(SEG)
    return jnp.asarray(parts.reshape(count, 1, 2 * NBIN), jnp.float32)


def lag_table():
    bin_ids = BIN_LOW + np.arange(NBIN)
    delays = np.arange(NLAG) - NLAG // 2
    angles = 2.0 * np.pi * np.mod(np.outer(bin_ids, delays), SEG) / SEG
    basis = chunked(np.cos(angles).T, -np.sin(angles).T).T / np.sqrt(NBIN)
    return jnp.asarray(basis, jnp.float32).astype(jnp.bfloat16)


def band_table():
    offsets = np.arange(NBIN)
    band = np.abs(offsets[:, None] - offsets[None, :]) <= 32
    return jnp.asarray(band.astype(np.float32)).astype(jnp.bfloat16)


def dot(left, right):
    return jnp.dot(left, right, preferred_element_type=jnp.float32)


def decimate_kernel(strain_ref, table_ref, out_ref):
    halves, rows, length = strain_ref.shape
    group = out_ref.shape[1] // halves
    tiles = length // BLOCK
    many = halves * rows
    first = pl.program_id(0) * (rows // group)
    x = strain_ref[...].reshape(many, length)
    stacked = [x[:, tile * BLOCK : (tile + 1) * BLOCK] for tile in range(tiles)]
    sums = dot(jnp.concatenate(stacked, axis=0), table_ref[...])
    for tile in range(tiles + 1):
        if tile == tiles:
            values = sums[:many, LANES:]
        else:
            values = sums[tile * many : (tile + 1) * many, :LANES]
        if tile + 1 < tiles:
            values = values + sums[(tile + 1) * many : (tile + 2) * many, LANES:]
        for peer in range(rows // group):
            part = [
                values[half * rows + peer * group : half * rows + (peer + 1) * group]
                for half in range(halves)
            ]
            part = jnp.concatenate(part, axis=0).astype(jnp.bfloat16)
            out_ref[position(first + peer) - first, :, tile * LANES : (tile + 1) * LANES] = part


def decimate(strain, peers, group):
    rows, length = strain.shape
    half_rows = rows // HALVES
    width = length // DEC + LANES
    steps = 2
    return pl.pallas_call(
        decimate_kernel,
        out_shape=jax.ShapeDtypeStruct((peers, HALVES * group, width), jnp.bfloat16),
        grid=(steps,),
        in_specs=[
            pl.BlockSpec((HALVES, half_rows // steps, length), lambda i: (0, i, 0)),
            pl.BlockSpec((BLOCK, 2 * LANES), lambda i: (0, 0)),
        ],
        out_specs=pl.BlockSpec((peers // steps, HALVES * group, width), lambda i: (i, 0, 0)),
        name="decimate",
    )(strain.reshape(HALVES, half_rows, length), filter_table())


def spectrum_kernel(info_ref, recv_ref, inner_ref, phase_ref, own_ref, send_ref, lhs, edge):
    peers, rows, width = recv_ref.shape
    span = width - LANES
    blocks = peers * span // BLOCK
    base = info_ref[0] * (peers * span)
    first = info_ref[0] * blocks + 1
    starts = [info_ref[1 + number] - base for number in range(NSEG)]

    for peer in range(peers):
        for tile in range(span // LANES):
            values = recv_ref[position(peer), :, tile * LANES : (tile + 1) * LANES]
            if tile == span // LANES - 1 and peer + 1 < peers:
                carried = recv_ref[position(peer + 1), :, span:].astype(jnp.float32)
                values = (values.astype(jnp.float32) + carried).astype(jnp.bfloat16)
            block, inside = divmod(peer * span + tile * LANES, BLOCK)
            lhs[block * rows : (block + 1) * rows, inside : inside + LANES] = values

    cuts = []
    lane = lax.broadcasted_iota(jnp.int32, (rows, BLOCK), 1)
    for number, start in enumerate(starts):
        offset = jnp.bitwise_and(start, BLOCK - 1)
        for side, limit in enumerate((start, start + SEG)):
            block = lax.shift_right_arithmetic(limit, jnp.int32(BLOCK.bit_length() - 1))
            held = jnp.clip(block, 0, blocks - 1)
            cut = (block == held) & (offset != 0)
            kept = jnp.where(side == 0, lane >= offset, lane < offset)
            values = lhs[pl.ds(pl.multiple_of(held * rows, rows), rows), :].astype(jnp.float32)
            values = jnp.where(kept & cut, values, 0.0).astype(jnp.bfloat16)
            row = (blocks + len(cuts)) * rows
            lhs[row : row + rows, :] = values
            cuts.append((number, held))
    before = lax.broadcasted_iota(jnp.int32, (rows, LANES), 1) - LANES
    carried = recv_ref[0, :, span:].astype(jnp.float32)
    for number, start in enumerate(starts):
        kept = (before >= start) & (before < start + SEG)
        values = jnp.where(kept, carried, 0.0).astype(jnp.bfloat16)
        edge[number * rows : (number + 1) * rows, :] = values

    whole = [
        [
            ((start <= block * BLOCK) & ((block + 1) * BLOCK <= start + SEG)).astype(jnp.float32)
            for block in range(blocks)
        ]
        for start in starts
    ]
    for chunk in range(CHUNKS):
        re_at, im_at = places(chunk)

        def turned(part, block):
            cos, sin = phase_ref[first + block, :, re_at], phase_ref[first + block, :, im_at]
            part_re, part_im = part[:, :LANES], part[:, LANES:]
            return part_re * cos + part_im * sin, part_im * cos - part_re * sin

        table = inner_ref[:, re_at.start : im_at.stop]
        body = dot(lhs[...], table)
        tail = dot(edge[...], table[BLOCK - LANES :])
        totals = [turned(tail[number * rows : (number + 1) * rows], -1) for number in range(NSEG)]
        for block in range(blocks):
            part_re, part_im = turned(body[block * rows : (block + 1) * rows], block)
            for number in range(NSEG):
                factor = whole[number][block]
                total_re, total_im = totals[number]
                totals[number] = total_re + factor * part_re, total_im + factor * part_im
        for index, (number, block) in enumerate(cuts):
            at = (blocks + index) * rows
            part_re, part_im = turned(body[at : at + rows], block)
            total_re, total_im = totals[number]
            totals[number] = total_re + part_re, total_im + part_im
        for number, (total_re, total_im) in enumerate(totals):
            at = slice(number * rows, (number + 1) * rows)
            own_ref[at, re_at] = total_re
            own_ref[at, im_at] = total_im
            send_ref[at, re_at] = total_re.astype(jnp.bfloat16)
            send_ref[at, im_at] = total_im.astype(jnp.bfloat16)


def partial_spectrum(info, recv):
    peers, rows, width = recv.shape
    blocks = peers * (width - LANES) // BLOCK
    many = NSEG * rows
    return pl.pallas_call(
        spectrum_kernel,
        out_shape=[
            jax.ShapeDtypeStruct((many, 2 * NBIN), jnp.float32),
            jax.ShapeDtypeStruct((many, 2 * NBIN), jnp.bfloat16),
        ],
        in_specs=[SMEM, VMEM, VMEM, VMEM],
        out_specs=[VMEM, VMEM],
        scratch_shapes=[
            pltpu.VMEM(((blocks + 2 * NSEG) * rows, BLOCK), jnp.bfloat16),
            pltpu.VMEM((many, LANES), jnp.bfloat16),
        ],
        compiler_params=pltpu.CompilerParams(vmem_limit_bytes=32 * 1024 * 1024),
        name="spectrum",
    )(info, recv, inner_table(), phase_table(-1, HALVES * blocks + 1))


def whiten_kernel(own_ref, other_ref, band_ref, out_ref):
    total = own_ref[...] + other_ref[...].astype(jnp.float32)
    real_part = jnp.concatenate([total[:, places(chunk)[0]] for chunk in range(CHUNKS)], axis=1)
    imag_part = jnp.concatenate([total[:, places(chunk)[1]] for chunk in range(CHUNKS)], axis=1)
    energy = real_part * real_part + imag_part * imag_part
    high = energy.astype(jnp.bfloat16)
    low = (energy - high.astype(jnp.float32)).astype(jnp.bfloat16)
    smooth = (dot(high, band_ref[...]) + dot(low, band_ref[...])) / 65.0
    inverse = lax.rsqrt(smooth + 1e-05)
    white = []
    for chunk in range(CHUNKS):
        at = slice(chunk * LANES, (chunk + 1) * LANES)
        white += [real_part[:, at] * inverse[:, at], imag_part[:, at] * inverse[:, at]]
    white = jnp.concatenate(white, axis=1).astype(jnp.bfloat16)
    for peer in range(out_ref.shape[0]):
        out_ref[peer] = white


def whiten(own, other, peers):
    return pl.pallas_call(
        whiten_kernel,
        out_shape=jax.ShapeDtypeStruct((peers, *own.shape), jnp.bfloat16),
        in_specs=[VMEM] * 3,
        out_specs=VMEM,
        compiler_params=pltpu.CompilerParams(vmem_limit_bytes=32 * 1024 * 1024),
        name="whiten",
    )(own, other, band_table())


def correlate_kernel(groups, group, block, info_ref, *refs):
    spectra = refs[:groups]
    basis_ref, out_ref, source, near, receiver, cross_even, cross_odd, lagged, sent = refs[groups:]
    rows = HALVES * group
    channels = spectra[0].shape[0] * rows
    receivers = groups * group
    blocks = sent.shape[0]
    half, peer, mine = info_ref[0], info_ref[1], info_ref[2]

    for step, spectrum in enumerate(spectra):
        owner = lax.rem(mine + step, groups)
        for number in range(NSEG):
            here = spectrum[position(peer), number * rows : (number + 1) * rows, :].astype(jnp.float32)
            here = jnp.where(half == 0, here[:group], here[group:]) * (1.0 / NSEG)
            near[number, owner] = here

    for number in range(NSEG):
        receiver[number] = near[number].reshape(receivers, 2 * NBIN).astype(jnp.bfloat16)

    def widen(chunk):
        for step, spectrum in enumerate(spectra):
            for number in range(NSEG):
                for part, columns in enumerate(places(chunk)):
                    held = spectrum[:, number * rows : (number + 1) * rows, columns]
                    held = held.astype(jnp.float32).reshape(channels, LANES)
                    at = slice(step * channels, (step + 1) * channels)
                    source[number, 2 * chunk + part, at, :] = held

    def fill(number, cross, chunks):
        for chunk in chunks:
            re_at, im_at = places(chunk)
            recv_re = [receiver[seg, :, re_at] for seg in range(NSEG)]
            recv_im = [receiver[seg, :, im_at] for seg in range(NSEG)]
            for k in range(block):
                total_re = total_im = None
                same = pl.ds(info_ref[3 + number * block + k], 8, stride=0)
                for seg in range(NSEG):
                    source_re = source[seg, 2 * chunk, same, :]
                    source_im = source[seg, 2 * chunk + 1, same, :]
                    source_re = jnp.concatenate([source_re] * (receivers // 8), axis=0)
                    source_im = jnp.concatenate([source_im] * (receivers // 8), axis=0)
                    source_re = source_re.astype(jnp.bfloat16)
                    source_im = source_im.astype(jnp.bfloat16)
                    part_re = source_re * recv_re[seg] + source_im * recv_im[seg]
                    part_im = source_re * recv_im[seg] - source_im * recv_re[seg]
                    total_re = part_re if seg == 0 else total_re + part_re
                    total_im = part_im if seg == 0 else total_im + part_im
                at = slice(k * receivers, (k + 1) * receivers)
                cross[at, re_at] = total_re
                cross[at, im_at] = total_im

    size = block * receivers

    def span(number):
        return pl.ds(pl.multiple_of(number * size, size), size)

    def lag(number, cross):
        lagged[span(number), :] = dot(cross[...], basis_ref[...]).astype(jnp.bfloat16)

    def store(number):
        at = span(number)
        return pltpu.make_async_copy(lagged.at[at], out_ref.at[at], sent.at[number])

    everything = range(CHUNKS)
    for chunk in everything:
        widen(chunk)
    fill(0, cross_even, everything)

    def pair(number):
        lag(2 * number, cross_even)
        fill(2 * number + 1, cross_odd, everything)
        store(2 * number).start()

    def step(number, carry):
        pair(number)
        lag(2 * number + 1, cross_odd)
        fill(2 * number + 2, cross_even, everything)
        store(2 * number + 1).start()
        return carry

    last = blocks // 2 - 1
    lax.fori_loop(0, last, step, 0)
    pair(last)
    lag(2 * last + 1, cross_odd)
    store(2 * last + 1).start()

    def finish(number, carry):
        store(number).wait()
        return carry

    lax.fori_loop(0, blocks, finish, 0)


def correlate(info, spectra, group):
    groups = len(spectra)
    many = info.shape[0] - 3
    receivers = groups * group
    channels = groups * spectra[0].shape[0] * HALVES * group
    block = 256 // receivers
    rows = block * receivers

    def kernel(*refs):
        correlate_kernel(groups, group, block, *refs)

    held = sum(spectrum.size * spectrum.dtype.itemsize for spectrum in spectra)
    return pl.pallas_call(
        kernel,
        out_shape=jax.ShapeDtypeStruct((many * receivers, NLAG), jnp.bfloat16),
        in_specs=[SMEM] + [VMEM] * (groups + 1),
        out_specs=pl.BlockSpec(memory_space=pl.ANY),
        scratch_shapes=[
            pltpu.VMEM((NSEG, 2 * CHUNKS, channels + 8, LANES), jnp.float32),
            pltpu.VMEM((NSEG, groups, group, 2 * NBIN), jnp.float32),
            pltpu.VMEM((NSEG, receivers, 2 * NBIN), jnp.bfloat16),
            pltpu.VMEM((rows, 2 * NBIN), jnp.bfloat16),
            pltpu.VMEM((rows, 2 * NBIN), jnp.bfloat16),
            pltpu.VMEM((many * receivers, NLAG), jnp.bfloat16),
            pltpu.SemaphoreType.DMA((many // block,)),
        ],
        compiler_params=pltpu.CompilerParams(
            vmem_limit_bytes=min(16 * 1024 * 1024 + 3 * held, 63 * 1024 * 1024)
        ),
        name="correlate",
    )(info, *spectra, lag_table())


def source_rows(src_chan, group_count, local_rows, peers, per_device):
    mine = lax.axis_index("src")
    many = src_chan.shape[0] // group_count
    wanted = lax.dynamic_slice_in_dim(src_chan, mine * many, many, 0)
    step = jnp.mod(wanted // local_rows - mine, group_count)
    local = wanted % local_rows
    half, inside = local // (local_rows // HALVES), local % (local_rows // HALVES)
    place = position(inside // per_device) * HALVES + half
    return step * local_rows + place * per_device + inside % per_device


def on_device(strain, seg_start, src_chan):
    chan_count = lax.axis_size("chan")
    group_count = lax.axis_size("src")
    peers = chan_count // HALVES
    per_device = strain.shape[0] // chan_count
    index = lax.axis_index("chan")
    half = (index // peers).reshape(1).astype(jnp.int32)
    place = jnp.stack([index // peers, index % peers, lax.axis_index("src")]).astype(jnp.int32)
    rows = source_rows(src_chan, group_count, strain.shape[0], peers, per_device)
    cubes = [[half * peers + peer for peer in ordered(peers)] for half in range(HALVES)]

    sent = decimate(strain, peers, per_device)
    samples = lax.all_to_all(sent, "chan", 0, 0, tiled=True, axis_index_groups=cubes)
    own, send = partial_spectrum(jnp.concatenate([half, seg_start]), samples)
    across = [(i, (i + peers) % chan_count) for i in range(chan_count)]
    white = whiten(own, lax.ppermute(send, "chan", across), peers)
    held = lax.all_to_all(white, "chan", 0, 0, tiled=True, axis_index_groups=cubes)
    spectra = [held]
    for step in range(1, group_count):
        pairs = [((i + step) % group_count, i) for i in range(group_count)]
        spectra.append(lax.ppermute(held, "src", pairs))
    lagged = correlate(jnp.concatenate([place, rows]), spectra, per_device)
    return lagged.reshape(-1, group_count, per_device, NLAG)


def solution(mesh):
    return jax.shard_map(
        on_device,
        mesh=mesh,
        in_specs=(P("src", "chan"), P(), P()),
        out_specs=P("src", None, "chan", None),
        check_vma=False,
    )
```

```python
import math

import jax
import jax.numpy as jnp
import numpy as np
from jax import lax
from jax.experimental import pallas as pl
from jax.experimental.pallas import tpu as pltpu
from jax.sharding import PartitionSpec as P

DEC = 4
SEG = 7680
NSEG = 3
BIN_LOW = 61
NBIN = 384
NLAG = 512
LANES = 128
BLOCK = 512
HALVES = 2
CHUNKS = NBIN // LANES
VMEM = pl.BlockSpec(memory_space=pltpu.VMEM)
SMEM = pl.BlockSpec(memory_space=pltpu.SMEM)


def ordered(peers):
    return [place ^ (place >> 1) for place in range(peers)]


def position(peer):
    peer = peer ^ (peer >> 1)
    peer = peer ^ (peer >> 2)
    return peer ^ (peer >> 4)


def chunked(real, imag):
    parts = np.stack([real, imag], axis=1).reshape(-1, 2, CHUNKS, LANES)
    return parts.transpose(0, 2, 1, 3).reshape(-1, 2 * NBIN)


def places(chunk):
    start = 2 * chunk * LANES
    return slice(start, start + LANES), slice(start + LANES, start + 2 * LANES)


def filter_table():
    length = 4 * DEC
    offsets = np.arange(length)
    centred = (offsets - (length - 1) / 2.0) / DEC
    coeffs = (
        np.sin(np.pi * centred)
        / (np.pi * centred)
        * (0.54 - 0.46 * np.cos(2.0 * np.pi * (offsets + 0.5) / length))
    )
    coeffs = coeffs / coeffs.sum()
    first = np.concatenate([np.arange(LANES), np.arange(LANES) - LANES])
    tap = np.arange(BLOCK)[:, None] - DEC * first[None, :]
    inside = (tap >= 0) & (tap < length)
    values = np.where(inside, coeffs[np.clip(tap, 0, length - 1)], 0.0)
    return jnp.asarray(values, jnp.float32).astype(jnp.bfloat16)


def inner_table():
    bin_ids = BIN_LOW + np.arange(NBIN)
    angle = 2.0 * np.pi * np.mod(np.outer(np.arange(BLOCK), bin_ids), SEG) / SEG
    parts = chunked(np.cos(angle), -np.sin(angle))
    return jnp.asarray(parts, jnp.float32).astype(jnp.bfloat16)


def phase_table(first, count):
    bin_ids = BIN_LOW + np.arange(NBIN)
    angle = 2.0 * np.pi * np.mod(np.outer(BLOCK * (first + np.arange(count)), bin_ids), SEG) / SEG
    parts = chunked(np.cos(angle), np.sin(angle)) / math.sqrt(SEG)
    return jnp.asarray(parts.reshape(count, 1, 2 * NBIN), jnp.float32)


def lag_table():
    bin_ids = BIN_LOW + np.arange(NBIN)
    delays = np.arange(NLAG) - NLAG // 2
    angles = 2.0 * np.pi * np.mod(np.outer(bin_ids, delays), SEG) / SEG
    basis = chunked(np.cos(angles).T, -np.sin(angles).T).T / np.sqrt(NBIN)
    return jnp.asarray(basis, jnp.float32).astype(jnp.bfloat16)


def band_table():
    offsets = np.arange(NBIN)
    band = np.abs(offsets[:, None] - offsets[None, :]) <= 32
    return jnp.asarray(band.astype(np.float32)).astype(jnp.bfloat16)


def dot(left, right):
    return jnp.dot(left, right, preferred_element_type=jnp.float32)


def decimate_kernel(strain_ref, table_ref, out_ref):
    halves, rows, length = strain_ref.shape
    group = out_ref.shape[1] // halves
    tiles = length // BLOCK
    many = halves * rows
    first = pl.program_id(0) * (rows // group)
    x = strain_ref[...].reshape(many, length)
    stacked = [x[:, tile * BLOCK : (tile + 1) * BLOCK] for tile in range(tiles)]
    sums = dot(jnp.concatenate(stacked, axis=0), table_ref[...])
    for tile in range(tiles + 1):
        if tile == tiles:
            values = sums[:many, LANES:]
        else:
            values = sums[tile * many : (tile + 1) * many, :LANES]
        if tile + 1 < tiles:
            values = values + sums[(tile + 1) * many : (tile + 2) * many, LANES:]
        for peer in range(rows // group):
            part = [
                values[half * rows + peer * group : half * rows + (peer + 1) * group]
                for half in range(halves)
            ]
            part = jnp.concatenate(part, axis=0).astype(jnp.bfloat16)
            out_ref[position(first + peer) - first, :, tile * LANES : (tile + 1) * LANES] = part


def decimate(strain, peers, group):
    rows, length = strain.shape
    half_rows = rows // HALVES
    width = length // DEC + LANES
    steps = 2
    return pl.pallas_call(
        decimate_kernel,
        out_shape=jax.ShapeDtypeStruct((peers, HALVES * group, width), jnp.bfloat16),
        grid=(steps,),
        in_specs=[
            pl.BlockSpec((HALVES, half_rows // steps, length), lambda i: (0, i, 0)),
            pl.BlockSpec((BLOCK, 2 * LANES), lambda i: (0, 0)),
        ],
        out_specs=pl.BlockSpec((peers // steps, HALVES * group, width), lambda i: (i, 0, 0)),
        name="decimate",
    )(strain.reshape(HALVES, half_rows, length), filter_table())


def spectrum_kernel(info_vmem, recv_ref, inner_ref, phase_ref, own_ref, send_ref, lhs, edge, info_ref, told):
    peers, rows, width = recv_ref.shape
    span = width - LANES
    blocks = peers * span // BLOCK
    tell = pltpu.make_async_copy(info_vmem, info_ref, told)
    tell.start()

    for peer in range(peers):
        for tile in range(span // LANES):
            values = recv_ref[position(peer), :, tile * LANES : (tile + 1) * LANES]
            if tile == span // LANES - 1 and peer + 1 < peers:
                carried = recv_ref[position(peer + 1), :, span:].astype(jnp.float32)
                values = (values.astype(jnp.float32) + carried).astype(jnp.bfloat16)
            block, inside = divmod(peer * span + tile * LANES, BLOCK)
            lhs[block * rows : (block + 1) * rows, inside : inside + LANES] = values

    tell.wait()
    base = info_ref[0] * (peers * span)
    first = info_ref[0] * blocks + 1
    starts = [info_ref[1 + number] - base for number in range(NSEG)]

    cuts = []
    lane = lax.broadcasted_iota(jnp.int32, (rows, BLOCK), 1)
    for number, start in enumerate(starts):
        offset = jnp.bitwise_and(start, BLOCK - 1)
        for side, limit in enumerate((start, start + SEG)):
            block = lax.shift_right_arithmetic(limit, jnp.int32(BLOCK.bit_length() - 1))
            held = jnp.clip(block, 0, blocks - 1)
            cut = (block == held) & (offset != 0)
            kept = jnp.where(side == 0, lane >= offset, lane < offset)
            values = lhs[pl.ds(pl.multiple_of(held * rows, rows), rows), :].astype(jnp.float32)
            values = jnp.where(kept & cut, values, 0.0).astype(jnp.bfloat16)
            row = (blocks + len(cuts)) * rows
            lhs[row : row + rows, :] = values
            cuts.append((number, held))
    before = lax.broadcasted_iota(jnp.int32, (rows, LANES), 1) - LANES
    carried = recv_ref[0, :, span:].astype(jnp.float32)
    for number, start in enumerate(starts):
        kept = (before >= start) & (before < start + SEG)
        values = jnp.where(kept, carried, 0.0).astype(jnp.bfloat16)
        edge[number * rows : (number + 1) * rows, :] = values

    whole = [
        [
            ((start <= block * BLOCK) & ((block + 1) * BLOCK <= start + SEG)).astype(jnp.float32)
            for block in range(blocks)
        ]
        for start in starts
    ]
    for chunk in range(CHUNKS):
        re_at, im_at = places(chunk)

        def turned(part, block):
            cos, sin = phase_ref[first + block, :, re_at], phase_ref[first + block, :, im_at]
            part_re, part_im = part[:, :LANES], part[:, LANES:]
            return part_re * cos + part_im * sin, part_im * cos - part_re * sin

        table = inner_ref[:, re_at.start : im_at.stop]
        body = dot(lhs[...], table)
        tail = dot(edge[...], table[BLOCK - LANES :])
        totals = [turned(tail[number * rows : (number + 1) * rows], -1) for number in range(NSEG)]
        for block in range(blocks):
            part_re, part_im = turned(body[block * rows : (block + 1) * rows], block)
            for number in range(NSEG):
                factor = whole[number][block]
                total_re, total_im = totals[number]
                totals[number] = total_re + factor * part_re, total_im + factor * part_im
        for index, (number, block) in enumerate(cuts):
            at = (blocks + index) * rows
            part_re, part_im = turned(body[at : at + rows], block)
            total_re, total_im = totals[number]
            totals[number] = total_re + part_re, total_im + part_im
        for number, (total_re, total_im) in enumerate(totals):
            at = slice(number * rows, (number + 1) * rows)
            own_ref[at, re_at] = total_re
            own_ref[at, im_at] = total_im
            send_ref[at, re_at] = total_re.astype(jnp.bfloat16)
            send_ref[at, im_at] = total_im.astype(jnp.bfloat16)


def partial_spectrum(info, recv):
    peers, rows, width = recv.shape
    blocks = peers * (width - LANES) // BLOCK
    many = NSEG * rows
    return pl.pallas_call(
        spectrum_kernel,
        out_shape=[
            jax.ShapeDtypeStruct((many, 2 * NBIN), jnp.float32),
            jax.ShapeDtypeStruct((many, 2 * NBIN), jnp.bfloat16),
        ],
        in_specs=[VMEM] * 4,
        out_specs=[VMEM, VMEM],
        scratch_shapes=[
            pltpu.VMEM(((blocks + 2 * NSEG) * rows, BLOCK), jnp.bfloat16),
            pltpu.VMEM((many, LANES), jnp.bfloat16),
            pltpu.SMEM(info.shape, jnp.int32),
            pltpu.SemaphoreType.DMA,
        ],
        compiler_params=pltpu.CompilerParams(vmem_limit_bytes=32 * 1024 * 1024),
        name="spectrum",
    )(info, recv, inner_table(), phase_table(-1, HALVES * blocks + 1))


def whiten_kernel(own_ref, other_ref, band_ref, out_ref):
    total = own_ref[...] + other_ref[...].astype(jnp.float32)
    real_part = jnp.concatenate([total[:, places(chunk)[0]] for chunk in range(CHUNKS)], axis=1)
    imag_part = jnp.concatenate([total[:, places(chunk)[1]] for chunk in range(CHUNKS)], axis=1)
    energy = real_part * real_part + imag_part * imag_part
    high = energy.astype(jnp.bfloat16)
    low = (energy - high.astype(jnp.float32)).astype(jnp.bfloat16)
    smooth = (dot(high, band_ref[...]) + dot(low, band_ref[...])) / 65.0
    inverse = lax.rsqrt(smooth + 1e-05)
    white = []
    for chunk in range(CHUNKS):
        at = slice(chunk * LANES, (chunk + 1) * LANES)
        white += [real_part[:, at] * inverse[:, at], imag_part[:, at] * inverse[:, at]]
    white = jnp.concatenate(white, axis=1).astype(jnp.bfloat16)
    for peer in range(out_ref.shape[0]):
        out_ref[peer] = white


def whiten(own, other, peers):
    return pl.pallas_call(
        whiten_kernel,
        out_shape=jax.ShapeDtypeStruct((peers, *own.shape), jnp.bfloat16),
        in_specs=[VMEM] * 3,
        out_specs=VMEM,
        compiler_params=pltpu.CompilerParams(vmem_limit_bytes=32 * 1024 * 1024),
        name="whiten",
    )(own, other, band_table())


def correlate_kernel(groups, group, block, info_vmem, *refs):
    spectra = refs[:groups]
    basis_ref, out_ref, source, near, receiver, cross_even, cross_odd, lagged, sent, info_ref, told = refs[groups:]
    rows = HALVES * group
    channels = spectra[0].shape[0] * rows
    receivers = groups * group
    blocks = sent.shape[0]
    tell = pltpu.make_async_copy(info_vmem, info_ref, told)
    tell.start()

    def widen(chunk):
        for step, spectrum in enumerate(spectra):
            for number in range(NSEG):
                for part, columns in enumerate(places(chunk)):
                    held = spectrum[:, number * rows : (number + 1) * rows, columns]
                    held = held.astype(jnp.float32).reshape(channels, LANES)
                    at = slice(step * channels, (step + 1) * channels)
                    source[number, 2 * chunk + part, at, :] = held

    for chunk in range(CHUNKS):
        widen(chunk)
    tell.wait()
    half, peer, mine = info_ref[0], info_ref[1], info_ref[2]

    for step, spectrum in enumerate(spectra):
        owner = lax.rem(mine + step, groups)
        for number in range(NSEG):
            here = spectrum[position(peer), number * rows : (number + 1) * rows, :].astype(jnp.float32)
            here = jnp.where(half == 0, here[:group], here[group:]) * (1.0 / NSEG)
            near[number, owner] = here

    for number in range(NSEG):
        receiver[number] = near[number].reshape(receivers, 2 * NBIN).astype(jnp.bfloat16)

    def fill(number, cross, chunks):
        for chunk in chunks:
            re_at, im_at = places(chunk)
            recv_re = [receiver[seg, :, re_at] for seg in range(NSEG)]
            recv_im = [receiver[seg, :, im_at] for seg in range(NSEG)]
            for k in range(block):
                total_re = total_im = None
                same = pl.ds(info_ref[3 + number * block + k], 8, stride=0)
                for seg in range(NSEG):
                    source_re = source[seg, 2 * chunk, same, :]
                    source_im = source[seg, 2 * chunk + 1, same, :]
                    source_re = jnp.concatenate([source_re] * (receivers // 8), axis=0)
                    source_im = jnp.concatenate([source_im] * (receivers // 8), axis=0)
                    source_re = source_re.astype(jnp.bfloat16)
                    source_im = source_im.astype(jnp.bfloat16)
                    part_re = source_re * recv_re[seg] + source_im * recv_im[seg]
                    part_im = source_re * recv_im[seg] - source_im * recv_re[seg]
                    total_re = part_re if seg == 0 else total_re + part_re
                    total_im = part_im if seg == 0 else total_im + part_im
                at = slice(k * receivers, (k + 1) * receivers)
                cross[at, re_at] = total_re
                cross[at, im_at] = total_im

    size = block * receivers

    def span(number):
        return pl.ds(pl.multiple_of(number * size, size), size)

    def lag(number, cross):
        lagged[span(number), :] = dot(cross[...], basis_ref[...]).astype(jnp.bfloat16)

    def store(number):
        at = span(number)
        return pltpu.make_async_copy(lagged.at[at], out_ref.at[at], sent.at[number])

    everything = range(CHUNKS)
    fill(0, cross_even, everything)

    def pair(number):
        lag(2 * number, cross_even)
        fill(2 * number + 1, cross_odd, everything)
        store(2 * number).start()

    def step(number, carry):
        pair(number)
        lag(2 * number + 1, cross_odd)
        fill(2 * number + 2, cross_even, everything)
        store(2 * number + 1).start()
        return carry

    last = blocks // 2 - 1
    lax.fori_loop(0, last, step, 0)
    pair(last)
    lag(2 * last + 1, cross_odd)
    store(2 * last + 1).start()

    def finish(number, carry):
        store(number).wait()
        return carry

    lax.fori_loop(0, blocks, finish, 0)


def correlate(info, spectra, group):
    groups = len(spectra)
    many = info.shape[0] - 3
    receivers = groups * group
    channels = groups * spectra[0].shape[0] * HALVES * group
    block = 256 // receivers
    rows = block * receivers

    def kernel(*refs):
        correlate_kernel(groups, group, block, *refs)

    held = sum(spectrum.size * spectrum.dtype.itemsize for spectrum in spectra)
    return pl.pallas_call(
        kernel,
        out_shape=jax.ShapeDtypeStruct((many * receivers, NLAG), jnp.bfloat16),
        in_specs=[VMEM] * (groups + 2),
        out_specs=pl.BlockSpec(memory_space=pl.ANY),
        scratch_shapes=[
            pltpu.VMEM((NSEG, 2 * CHUNKS, channels + 8, LANES), jnp.float32),
            pltpu.VMEM((NSEG, groups, group, 2 * NBIN), jnp.float32),
            pltpu.VMEM((NSEG, receivers, 2 * NBIN), jnp.bfloat16),
            pltpu.VMEM((rows, 2 * NBIN), jnp.bfloat16),
            pltpu.VMEM((rows, 2 * NBIN), jnp.bfloat16),
            pltpu.VMEM((many * receivers, NLAG), jnp.bfloat16),
            pltpu.SemaphoreType.DMA((many // block,)),
            pltpu.SMEM(info.shape, jnp.int32),
            pltpu.SemaphoreType.DMA,
        ],
        compiler_params=pltpu.CompilerParams(
            vmem_limit_bytes=min(16 * 1024 * 1024 + 3 * held, 63 * 1024 * 1024)
        ),
        name="correlate",
    )(info, *spectra, lag_table())


def source_rows(src_chan, group_count, local_rows, peers, per_device):
    mine = lax.axis_index("src")
    many = src_chan.shape[0] // group_count
    wanted = lax.dynamic_slice_in_dim(src_chan, mine * many, many, 0)
    step = jnp.mod(wanted // local_rows - mine, group_count)
    local = wanted % local_rows
    half, inside = local // (local_rows // HALVES), local % (local_rows // HALVES)
    place = position(inside // per_device) * HALVES + half
    return step * local_rows + place * per_device + inside % per_device


def on_device(strain, seg_start, src_chan):
    chan_count = lax.axis_size("chan")
    group_count = lax.axis_size("src")
    peers = chan_count // HALVES
    per_device = strain.shape[0] // chan_count
    index = lax.axis_index("chan")
    half = (index // peers).reshape(1).astype(jnp.int32)
    place = jnp.stack([index // peers, index % peers, lax.axis_index("src")]).astype(jnp.int32)
    rows = source_rows(src_chan, group_count, strain.shape[0], peers, per_device)
    cubes = [[half * peers + peer for peer in ordered(peers)] for half in range(HALVES)]

    sent = decimate(strain, peers, per_device)
    samples = lax.all_to_all(sent, "chan", 0, 0, tiled=True, axis_index_groups=cubes)
    own, send = partial_spectrum(jnp.concatenate([half, seg_start]), samples)
    across = [(i, (i + peers) % chan_count) for i in range(chan_count)]
    white = whiten(own, lax.ppermute(send, "chan", across), peers)
    held = lax.all_to_all(white, "chan", 0, 0, tiled=True, axis_index_groups=cubes)
    spectra = [held]
    for step in range(1, group_count):
        pairs = [((i + step) % group_count, i) for i in range(group_count)]
        spectra.append(lax.ppermute(held, "src", pairs))
    lagged = correlate(jnp.concatenate([place, rows]), spectra, per_device)
    return lagged.reshape(-1, group_count, per_device, NLAG)


def solution(mesh):
    return jax.shard_map(
        on_device,
        mesh=mesh,
        in_specs=(P("src", "chan"), P(), P()),
        out_specs=P("src", None, "chan", None),
        check_vma=False,
    )
```

```python
import math

import jax
import jax.numpy as jnp
import numpy as np
from jax import lax
from jax.experimental import pallas as pl
from jax.experimental.pallas import tpu as pltpu
from jax.sharding import PartitionSpec as P

DEC = 4
SEG = 7680
NSEG = 3
BIN_LOW = 61
NBIN = 384
NLAG = 512
LANES = 128
BLOCK = 512
HALVES = 2
CHUNKS = NBIN // LANES
VMEM = pl.BlockSpec(memory_space=pltpu.VMEM)
SMEM = pl.BlockSpec(memory_space=pltpu.SMEM)


def ordered(peers):
    return [place ^ (place >> 1) for place in range(peers)]


def position(peer):
    peer = peer ^ (peer >> 1)
    peer = peer ^ (peer >> 2)
    return peer ^ (peer >> 4)


def chunked(real, imag):
    parts = np.stack([real, imag], axis=1).reshape(-1, 2, CHUNKS, LANES)
    return parts.transpose(0, 2, 1, 3).reshape(-1, 2 * NBIN)


def places(chunk):
    start = 2 * chunk * LANES
    return slice(start, start + LANES), slice(start + LANES, start + 2 * LANES)


def filter_table():
    length = 4 * DEC
    offsets = np.arange(length)
    centred = (offsets - (length - 1) / 2.0) / DEC
    coeffs = (
        np.sin(np.pi * centred)
        / (np.pi * centred)
        * (0.54 - 0.46 * np.cos(2.0 * np.pi * (offsets + 0.5) / length))
    )
    coeffs = coeffs / coeffs.sum()
    first = np.concatenate([np.arange(LANES), np.arange(LANES) - LANES])
    tap = np.arange(BLOCK)[:, None] - DEC * first[None, :]
    inside = (tap >= 0) & (tap < length)
    values = np.where(inside, coeffs[np.clip(tap, 0, length - 1)], 0.0)
    return jnp.asarray(values, jnp.float32).astype(jnp.bfloat16)


def inner_table():
    bin_ids = BIN_LOW + np.arange(NBIN)
    angle = 2.0 * np.pi * np.mod(np.outer(np.arange(BLOCK), bin_ids), SEG) / SEG
    parts = chunked(np.cos(angle), -np.sin(angle))
    return jnp.asarray(parts, jnp.float32).astype(jnp.bfloat16)


def phase_table(first, count):
    bin_ids = BIN_LOW + np.arange(NBIN)
    angle = 2.0 * np.pi * np.mod(np.outer(BLOCK * (first + np.arange(count)), bin_ids), SEG) / SEG
    parts = chunked(np.cos(angle), np.sin(angle)) / math.sqrt(SEG)
    return jnp.asarray(parts.reshape(count, 1, 2 * NBIN), jnp.float32)


def lag_table():
    bin_ids = BIN_LOW + np.arange(NBIN)
    delays = np.arange(NLAG) - NLAG // 2
    angles = 2.0 * np.pi * np.mod(np.outer(bin_ids, delays), SEG) / SEG
    basis = chunked(np.cos(angles).T, -np.sin(angles).T).T / np.sqrt(NBIN)
    return jnp.asarray(basis, jnp.float32).astype(jnp.bfloat16)


def band_table():
    offsets = np.arange(NBIN)
    band = np.abs(offsets[:, None] - offsets[None, :]) <= 32
    return jnp.asarray(band.astype(np.float32)).astype(jnp.bfloat16)


def dot(left, right):
    return jnp.dot(left, right, preferred_element_type=jnp.float32)


def decimate_kernel(strain_ref, table_ref, out_ref):
    halves, rows, length = strain_ref.shape
    tiles = length // BLOCK
    group = out_ref.shape[1] // (halves * tiles + 1)
    wide = halves * group
    many = halves * rows
    first = pl.program_id(0) * (rows // group)
    x = strain_ref[...].reshape(many, length)
    stacked = [x[:, tile * BLOCK : (tile + 1) * BLOCK] for tile in range(tiles)]
    sums = dot(jnp.concatenate(stacked, axis=0), table_ref[...])
    for tile in range(tiles + 1):
        if tile == tiles:
            values = sums[:many, LANES:]
        else:
            values = sums[tile * many : (tile + 1) * many, :LANES]
        if tile + 1 < tiles:
            values = values + sums[(tile + 1) * many : (tile + 2) * many, LANES:]
        for peer in range(rows // group):
            part = [
                values[half * rows + peer * group : half * rows + (peer + 1) * group]
                for half in range(halves)
            ]
            place = position(first + peer) - first
            if tile < tiles:
                part = jnp.concatenate(part, axis=0).astype(jnp.bfloat16)
                out_ref[place, tile * wide : (tile + 1) * wide, :] = part
            else:
                part = part[0] + pltpu.roll(part[1], LANES // 2, axis=1)
                out_ref[place, tiles * wide :, :] = part.astype(jnp.bfloat16)


def decimate(strain, peers, group):
    rows, length = strain.shape
    half_rows = rows // HALVES
    many = length // BLOCK * HALVES * group + group
    steps = 2
    return pl.pallas_call(
        decimate_kernel,
        out_shape=jax.ShapeDtypeStruct((peers, many, LANES), jnp.bfloat16),
        grid=(steps,),
        in_specs=[
            pl.BlockSpec((HALVES, half_rows // steps, length), lambda i: (0, i, 0)),
            pl.BlockSpec((BLOCK, 2 * LANES), lambda i: (0, 0)),
        ],
        out_specs=pl.BlockSpec((peers // steps, many, LANES), lambda i: (i, 0, 0)),
        name="decimate",
    )(strain.reshape(HALVES, half_rows, length), filter_table())


def spectrum_kernel(info_vmem, recv_ref, inner_ref, phase_ref, own_ref, send_ref, lhs, edge, info_ref, told):
    peers, many, _ = recv_ref.shape
    rows = own_ref.shape[0] // NSEG
    group = rows // HALVES
    tiles = (many - group) // rows
    span = tiles * LANES
    blocks = peers * span // BLOCK
    spot = lax.broadcasted_iota(jnp.int32, (rows, LANES), 1)

    def tail(peer):
        held = recv_ref[position(peer), tiles * rows :, :].astype(jnp.float32)
        held = jnp.concatenate([held, pltpu.roll(held, LANES // 2, axis=1)], axis=0)
        return jnp.where(spot >= LANES // 2, held, 0.0)

    tell = pltpu.make_async_copy(info_vmem, info_ref, told)
    tell.start()

    for peer in range(peers):
        for tile in range(span // LANES):
            values = recv_ref[position(peer), tile * rows : (tile + 1) * rows, :]
            if tile == span // LANES - 1 and peer + 1 < peers:
                values = (values.astype(jnp.float32) + tail(peer + 1)).astype(jnp.bfloat16)
            block, inside = divmod(peer * span + tile * LANES, BLOCK)
            lhs[block * rows : (block + 1) * rows, inside : inside + LANES] = values

    tell.wait()
    base = info_ref[0] * (peers * span)
    first = info_ref[0] * blocks + 1
    starts = [info_ref[1 + number] - base for number in range(NSEG)]

    cuts = []
    lane = lax.broadcasted_iota(jnp.int32, (rows, BLOCK), 1)
    for number, start in enumerate(starts):
        offset = jnp.bitwise_and(start, BLOCK - 1)
        for side, limit in enumerate((start, start + SEG)):
            block = lax.shift_right_arithmetic(limit, jnp.int32(BLOCK.bit_length() - 1))
            held = jnp.clip(block, 0, blocks - 1)
            cut = (block == held) & (offset != 0)
            kept = jnp.where(side == 0, lane >= offset, lane < offset)
            values = lhs[pl.ds(pl.multiple_of(held * rows, rows), rows), :].astype(jnp.float32)
            values = jnp.where(kept & cut, values, 0.0).astype(jnp.bfloat16)
            row = (blocks + len(cuts)) * rows
            lhs[row : row + rows, :] = values
            cuts.append((number, held))
    before = lax.broadcasted_iota(jnp.int32, (rows, LANES), 1) - LANES
    carried = tail(0)
    for number, start in enumerate(starts):
        kept = (before >= start) & (before < start + SEG)
        values = jnp.where(kept, carried, 0.0).astype(jnp.bfloat16)
        edge[number * rows : (number + 1) * rows, :] = values

    whole = [
        [
            ((start <= block * BLOCK) & ((block + 1) * BLOCK <= start + SEG)).astype(jnp.float32)
            for block in range(blocks)
        ]
        for start in starts
    ]
    for chunk in range(CHUNKS):
        re_at, im_at = places(chunk)

        def turned(part, block):
            cos, sin = phase_ref[first + block, :, re_at], phase_ref[first + block, :, im_at]
            part_re, part_im = part[:, :LANES], part[:, LANES:]
            return part_re * cos + part_im * sin, part_im * cos - part_re * sin

        table = inner_ref[:, re_at.start : im_at.stop]
        body = dot(lhs[...], table)
        ends = dot(edge[...], table[BLOCK - LANES :])
        totals = [turned(ends[number * rows : (number + 1) * rows], -1) for number in range(NSEG)]
        for block in range(blocks):
            part_re, part_im = turned(body[block * rows : (block + 1) * rows], block)
            for number in range(NSEG):
                factor = whole[number][block]
                total_re, total_im = totals[number]
                totals[number] = total_re + factor * part_re, total_im + factor * part_im
        for index, (number, block) in enumerate(cuts):
            at = (blocks + index) * rows
            part_re, part_im = turned(body[at : at + rows], block)
            total_re, total_im = totals[number]
            totals[number] = total_re + part_re, total_im + part_im
        for number, (total_re, total_im) in enumerate(totals):
            at = slice(number * rows, (number + 1) * rows)
            own_ref[at, re_at] = total_re
            own_ref[at, im_at] = total_im
            send_ref[at, re_at] = total_re.astype(jnp.bfloat16)
            send_ref[at, im_at] = total_im.astype(jnp.bfloat16)


def partial_spectrum(info, recv, group):
    rows = HALVES * group
    peers = recv.shape[0]
    blocks = peers * (recv.shape[1] - group) // rows * LANES // BLOCK
    many = NSEG * rows
    return pl.pallas_call(
        spectrum_kernel,
        out_shape=[
            jax.ShapeDtypeStruct((many, 2 * NBIN), jnp.float32),
            jax.ShapeDtypeStruct((many, 2 * NBIN), jnp.bfloat16),
        ],
        in_specs=[VMEM] * 4,
        out_specs=[VMEM, VMEM],
        scratch_shapes=[
            pltpu.VMEM(((blocks + 2 * NSEG) * rows, BLOCK), jnp.bfloat16),
            pltpu.VMEM((many, LANES), jnp.bfloat16),
            pltpu.SMEM(info.shape, jnp.int32),
            pltpu.SemaphoreType.DMA,
        ],
        compiler_params=pltpu.CompilerParams(vmem_limit_bytes=32 * 1024 * 1024),
        name="spectrum",
    )(info, recv, inner_table(), phase_table(-1, HALVES * blocks + 1))


def whiten_kernel(own_ref, other_ref, band_ref, out_ref):
    total = own_ref[...] + other_ref[...].astype(jnp.float32)
    real_part = jnp.concatenate([total[:, places(chunk)[0]] for chunk in range(CHUNKS)], axis=1)
    imag_part = jnp.concatenate([total[:, places(chunk)[1]] for chunk in range(CHUNKS)], axis=1)
    energy = real_part * real_part + imag_part * imag_part
    high = energy.astype(jnp.bfloat16)
    low = (energy - high.astype(jnp.float32)).astype(jnp.bfloat16)
    smooth = (dot(high, band_ref[...]) + dot(low, band_ref[...])) / 65.0
    inverse = lax.rsqrt(smooth + 1e-05)
    white = []
    for chunk in range(CHUNKS):
        at = slice(chunk * LANES, (chunk + 1) * LANES)
        white += [real_part[:, at] * inverse[:, at], imag_part[:, at] * inverse[:, at]]
    white = jnp.concatenate(white, axis=1).astype(jnp.bfloat16)
    for peer in range(out_ref.shape[0]):
        out_ref[peer] = white


def whiten(own, other, peers):
    return pl.pallas_call(
        whiten_kernel,
        out_shape=jax.ShapeDtypeStruct((peers, *own.shape), jnp.bfloat16),
        in_specs=[VMEM] * 3,
        out_specs=VMEM,
        compiler_params=pltpu.CompilerParams(vmem_limit_bytes=32 * 1024 * 1024),
        name="whiten",
    )(own, other, band_table())


def correlate_kernel(groups, group, block, info_vmem, *refs):
    spectra = refs[:groups]
    basis_ref, out_ref, source, near, receiver, cross_even, cross_odd, lagged, sent, info_ref, told = refs[groups:]
    rows = HALVES * group
    channels = spectra[0].shape[0] * rows
    receivers = groups * group
    blocks = sent.shape[0]
    tell = pltpu.make_async_copy(info_vmem, info_ref, told)
    tell.start()

    def widen(chunk):
        for step, spectrum in enumerate(spectra):
            for number in range(NSEG):
                for part, columns in enumerate(places(chunk)):
                    held = spectrum[:, number * rows : (number + 1) * rows, columns]
                    held = held.astype(jnp.float32).reshape(channels, LANES)
                    at = slice(step * channels, (step + 1) * channels)
                    source[number, 2 * chunk + part, at, :] = held

    for chunk in range(CHUNKS):
        widen(chunk)
    tell.wait()
    half, peer, mine = info_ref[0], info_ref[1], info_ref[2]

    for step, spectrum in enumerate(spectra):
        owner = lax.rem(mine + step, groups)
        for number in range(NSEG):
            here = spectrum[position(peer), number * rows : (number + 1) * rows, :].astype(jnp.float32)
            here = jnp.where(half == 0, here[:group], here[group:]) * (1.0 / NSEG)
            near[number, owner] = here

    for number in range(NSEG):
        receiver[number] = near[number].reshape(receivers, 2 * NBIN).astype(jnp.bfloat16)

    def fill(number, cross, chunks):
        for chunk in chunks:
            re_at, im_at = places(chunk)
            recv_re = [receiver[seg, :, re_at] for seg in range(NSEG)]
            recv_im = [receiver[seg, :, im_at] for seg in range(NSEG)]
            for k in range(block):
                total_re = total_im = None
                same = pl.ds(info_ref[3 + number * block + k], 8, stride=0)
                for seg in range(NSEG):
                    source_re = source[seg, 2 * chunk, same, :]
                    source_im = source[seg, 2 * chunk + 1, same, :]
                    source_re = jnp.concatenate([source_re] * (receivers // 8), axis=0)
                    source_im = jnp.concatenate([source_im] * (receivers // 8), axis=0)
                    source_re = source_re.astype(jnp.bfloat16)
                    source_im = source_im.astype(jnp.bfloat16)
                    part_re = source_re * recv_re[seg] + source_im * recv_im[seg]
                    part_im = source_re * recv_im[seg] - source_im * recv_re[seg]
                    total_re = part_re if seg == 0 else total_re + part_re
                    total_im = part_im if seg == 0 else total_im + part_im
                at = slice(k * receivers, (k + 1) * receivers)
                cross[at, re_at] = total_re
                cross[at, im_at] = total_im

    size = block * receivers

    def span(number):
        return pl.ds(pl.multiple_of(number * size, size), size)

    def lag(number, cross):
        lagged[span(number), :] = dot(cross[...], basis_ref[...]).astype(jnp.bfloat16)

    def store(number):
        at = span(number)
        return pltpu.make_async_copy(lagged.at[at], out_ref.at[at], sent.at[number])

    everything = range(CHUNKS)
    fill(0, cross_even, everything)

    def pair(number):
        lag(2 * number, cross_even)
        fill(2 * number + 1, cross_odd, everything)
        store(2 * number).start()

    def step(number, carry):
        pair(number)
        lag(2 * number + 1, cross_odd)
        fill(2 * number + 2, cross_even, everything)
        store(2 * number + 1).start()
        return carry

    last = blocks // 2 - 1
    lax.fori_loop(0, last, step, 0)
    pair(last)
    lag(2 * last + 1, cross_odd)
    store(2 * last + 1).start()

    def finish(number, carry):
        store(number).wait()
        return carry

    lax.fori_loop(0, blocks, finish, 0)


def correlate(info, spectra, group):
    groups = len(spectra)
    many = info.shape[0] - 3
    receivers = groups * group
    channels = groups * spectra[0].shape[0] * HALVES * group
    block = 256 // receivers
    rows = block * receivers

    def kernel(*refs):
        correlate_kernel(groups, group, block, *refs)

    held = sum(spectrum.size * spectrum.dtype.itemsize for spectrum in spectra)
    return pl.pallas_call(
        kernel,
        out_shape=jax.ShapeDtypeStruct((many * receivers, NLAG), jnp.bfloat16),
        in_specs=[VMEM] * (groups + 2),
        out_specs=pl.BlockSpec(memory_space=pl.ANY),
        scratch_shapes=[
            pltpu.VMEM((NSEG, 2 * CHUNKS, channels + 8, LANES), jnp.float32),
            pltpu.VMEM((NSEG, groups, group, 2 * NBIN), jnp.float32),
            pltpu.VMEM((NSEG, receivers, 2 * NBIN), jnp.bfloat16),
            pltpu.VMEM((rows, 2 * NBIN), jnp.bfloat16),
            pltpu.VMEM((rows, 2 * NBIN), jnp.bfloat16),
            pltpu.VMEM((many * receivers, NLAG), jnp.bfloat16),
            pltpu.SemaphoreType.DMA((many // block,)),
            pltpu.SMEM(info.shape, jnp.int32),
            pltpu.SemaphoreType.DMA,
        ],
        compiler_params=pltpu.CompilerParams(
            vmem_limit_bytes=min(16 * 1024 * 1024 + 3 * held, 63 * 1024 * 1024)
        ),
        name="correlate",
    )(info, *spectra, lag_table())


def source_rows(src_chan, group_count, local_rows, peers, per_device):
    mine = lax.axis_index("src")
    many = src_chan.shape[0] // group_count
    wanted = lax.dynamic_slice_in_dim(src_chan, mine * many, many, 0)
    step = jnp.mod(wanted // local_rows - mine, group_count)
    local = wanted % local_rows
    half, inside = local // (local_rows // HALVES), local % (local_rows // HALVES)
    place = position(inside // per_device) * HALVES + half
    return step * local_rows + place * per_device + inside % per_device


def on_device(strain, seg_start, src_chan):
    chan_count = lax.axis_size("chan")
    group_count = lax.axis_size("src")
    peers = chan_count // HALVES
    per_device = strain.shape[0] // chan_count
    index = lax.axis_index("chan")
    half = (index // peers).reshape(1).astype(jnp.int32)
    place = jnp.stack([index // peers, index % peers, lax.axis_index("src")]).astype(jnp.int32)
    rows = source_rows(src_chan, group_count, strain.shape[0], peers, per_device)
    cubes = [[half * peers + peer for peer in ordered(peers)] for half in range(HALVES)]

    sent = decimate(strain, peers, per_device)
    samples = lax.all_to_all(sent, "chan", 0, 0, tiled=True, axis_index_groups=cubes)
    own, send = partial_spectrum(jnp.concatenate([half, seg_start]), samples, per_device)
    across = [(i, (i + peers) % chan_count) for i in range(chan_count)]
    white = whiten(own, lax.ppermute(send, "chan", across), peers)
    held = lax.all_to_all(white, "chan", 0, 0, tiled=True, axis_index_groups=cubes)
    spectra = [held]
    for step in range(1, group_count):
        pairs = [((i + step) % group_count, i) for i in range(group_count)]
        spectra.append(lax.ppermute(held, "src", pairs))
    lagged = correlate(jnp.concatenate([place, rows]), spectra, per_device)
    return lagged.reshape(-1, group_count, per_device, NLAG)


def solution(mesh):
    return jax.shard_map(
        on_device,
        mesh=mesh,
        in_specs=(P("src", "chan"), P(), P()),
        out_specs=P("src", None, "chan", None),
        check_vma=False,
    )
```

```python
import math

import jax
import jax.numpy as jnp
import numpy as np
from jax import lax
from jax.experimental import pallas as pl
from jax.experimental.pallas import tpu as pltpu
from jax.sharding import PartitionSpec as P

DEC = 4
SEG = 7680
NSEG = 3
BIN_LOW = 61
NBIN = 384
NLAG = 512
LANES = 128
BLOCK = 512
HALVES = 2
CHUNKS = NBIN // LANES
VMEM = pl.BlockSpec(memory_space=pltpu.VMEM)
SMEM = pl.BlockSpec(memory_space=pltpu.SMEM)


def ordered(peers):
    return [place ^ (place >> 1) for place in range(peers)]


def position(peer):
    peer = peer ^ (peer >> 1)
    peer = peer ^ (peer >> 2)
    return peer ^ (peer >> 4)


def chunked(real, imag):
    parts = np.stack([real, imag], axis=1).reshape(-1, 2, CHUNKS, LANES)
    return parts.transpose(0, 2, 1, 3).reshape(-1, 2 * NBIN)


def places(chunk):
    start = 2 * chunk * LANES
    return slice(start, start + LANES), slice(start + LANES, start + 2 * LANES)


def filter_table():
    length = 4 * DEC
    offsets = np.arange(length)
    centred = (offsets - (length - 1) / 2.0) / DEC
    coeffs = (
        np.sin(np.pi * centred)
        / (np.pi * centred)
        * (0.54 - 0.46 * np.cos(2.0 * np.pi * (offsets + 0.5) / length))
    )
    coeffs = coeffs / coeffs.sum()
    first = np.concatenate([np.arange(LANES), np.arange(LANES) - LANES])
    tap = np.arange(BLOCK)[:, None] - DEC * first[None, :]
    inside = (tap >= 0) & (tap < length)
    values = np.where(inside, coeffs[np.clip(tap, 0, length - 1)], 0.0)
    return jnp.asarray(values, jnp.float32).astype(jnp.bfloat16)


def inner_table():
    bin_ids = BIN_LOW + np.arange(NBIN)
    angle = 2.0 * np.pi * np.mod(np.outer(np.arange(BLOCK), bin_ids), SEG) / SEG
    parts = chunked(np.cos(angle), -np.sin(angle))
    return jnp.asarray(parts, jnp.float32).astype(jnp.bfloat16)


def phase_table(first, count):
    bin_ids = BIN_LOW + np.arange(NBIN)
    angle = 2.0 * np.pi * np.mod(np.outer(BLOCK * (first + np.arange(count)), bin_ids), SEG) / SEG
    parts = chunked(np.cos(angle), np.sin(angle)) / math.sqrt(SEG)
    return jnp.asarray(parts.reshape(count, 1, 2 * NBIN), jnp.float32)


def lag_table():
    bin_ids = BIN_LOW + np.arange(NBIN)
    delays = np.arange(NLAG) - NLAG // 2
    angles = 2.0 * np.pi * np.mod(np.outer(bin_ids, delays), SEG) / SEG
    basis = chunked(np.cos(angles).T, -np.sin(angles).T).T / np.sqrt(NBIN)
    return jnp.asarray(basis, jnp.float32).astype(jnp.bfloat16)


def band_table():
    offsets = np.arange(NBIN)
    band = np.abs(offsets[:, None] - offsets[None, :]) <= 32
    return jnp.asarray(band.astype(np.float32)).astype(jnp.bfloat16)


def dot(left, right):
    return jnp.dot(left, right, preferred_element_type=jnp.float32)


def decimate_kernel(strain_ref, table_ref, out_ref):
    halves, rows, length = strain_ref.shape
    tiles = length // BLOCK
    group = out_ref.shape[1] // (halves * tiles + 1)
    wide = halves * group
    many = halves * rows
    first = pl.program_id(0) * (rows // group)
    x = strain_ref[...].reshape(many, length)
    stacked = [x[:, tile * BLOCK : (tile + 1) * BLOCK] for tile in range(tiles)]
    sums = dot(jnp.concatenate(stacked, axis=0), table_ref[...])
    for tile in range(tiles + 1):
        if tile == tiles:
            values = sums[:many, LANES:]
        else:
            values = sums[tile * many : (tile + 1) * many, :LANES]
        if tile + 1 < tiles:
            values = values + sums[(tile + 1) * many : (tile + 2) * many, LANES:]
        for peer in range(rows // group):
            part = [
                values[half * rows + peer * group : half * rows + (peer + 1) * group]
                for half in range(halves)
            ]
            place = position(first + peer) - first
            if tile < tiles:
                part = jnp.concatenate(part, axis=0).astype(jnp.bfloat16)
                out_ref[place, tile * wide : (tile + 1) * wide, :] = part
            else:
                part = part[0] + pltpu.roll(part[1], LANES // 2, axis=1)
                out_ref[place, tiles * wide :, :] = part.astype(jnp.bfloat16)


def decimate(strain, peers, group):
    rows, length = strain.shape
    half_rows = rows // HALVES
    many = length // BLOCK * HALVES * group + group
    steps = 2
    return pl.pallas_call(
        decimate_kernel,
        out_shape=jax.ShapeDtypeStruct((peers, many, LANES), jnp.bfloat16),
        grid=(steps,),
        in_specs=[
            pl.BlockSpec((HALVES, half_rows // steps, length), lambda i: (0, i, 0)),
            pl.BlockSpec((BLOCK, 2 * LANES), lambda i: (0, 0)),
        ],
        out_specs=pl.BlockSpec((peers // steps, many, LANES), lambda i: (i, 0, 0)),
        name="decimate",
    )(strain.reshape(HALVES, half_rows, length), filter_table())


def spectrum_kernel(info_vmem, recv_ref, inner_ref, phase_ref, own_ref, send_ref, lhs, edge, info_ref, told):
    peers, many, _ = recv_ref.shape
    rows = own_ref.shape[0] // NSEG
    group = rows // HALVES
    tiles = (many - group) // rows
    span = tiles * LANES
    blocks = peers * span // BLOCK
    spot = lax.broadcasted_iota(jnp.int32, (rows, LANES), 1)

    def tail(peer):
        held = recv_ref[position(peer), tiles * rows :, :].astype(jnp.float32)
        held = jnp.concatenate([held, pltpu.roll(held, LANES // 2, axis=1)], axis=0)
        return jnp.where(spot >= LANES // 2, held, 0.0)

    tell = pltpu.make_async_copy(info_vmem, info_ref, told)
    tell.start()

    for peer in range(peers):
        for tile in range(span // LANES):
            values = recv_ref[position(peer), tile * rows : (tile + 1) * rows, :]
            if tile == span // LANES - 1 and peer + 1 < peers:
                values = (values.astype(jnp.float32) + tail(peer + 1)).astype(jnp.bfloat16)
            block, inside = divmod(peer * span + tile * LANES, BLOCK)
            lhs[block * rows : (block + 1) * rows, inside : inside + LANES] = values

    tell.wait()
    base = info_ref[0] * (peers * span)
    first = info_ref[0] * blocks + 1
    starts = [info_ref[1 + number] - base for number in range(NSEG)]

    cuts = []
    lane = lax.broadcasted_iota(jnp.int32, (rows, BLOCK), 1)
    for number, start in enumerate(starts):
        offset = jnp.bitwise_and(start, BLOCK - 1)
        for side, limit in enumerate((start, start + SEG)):
            block = lax.shift_right_arithmetic(limit, jnp.int32(BLOCK.bit_length() - 1))
            held = jnp.clip(block, 0, blocks - 1)
            cut = (block == held) & (offset != 0)
            kept = jnp.where(side == 0, lane >= offset, lane < offset)
            values = lhs[pl.ds(pl.multiple_of(held * rows, rows), rows), :].astype(jnp.float32)
            values = jnp.where(kept & cut, values, 0.0).astype(jnp.bfloat16)
            row = (blocks + len(cuts)) * rows
            lhs[row : row + rows, :] = values
            cuts.append((number, held))
    before = lax.broadcasted_iota(jnp.int32, (rows, LANES), 1) - LANES
    carried = tail(0)
    for number, start in enumerate(starts):
        kept = (before >= start) & (before < start + SEG)
        values = jnp.where(kept, carried, 0.0).astype(jnp.bfloat16)
        edge[number * rows : (number + 1) * rows, :] = values

    whole = [
        [
            ((start <= block * BLOCK) & ((block + 1) * BLOCK <= start + SEG)).astype(jnp.float32)
            for block in range(blocks)
        ]
        for start in starts
    ]
    for chunk in range(CHUNKS):
        re_at, im_at = places(chunk)

        def turned(part, block):
            cos, sin = phase_ref[first + block, :, re_at], phase_ref[first + block, :, im_at]
            part_re, part_im = part[:, :LANES], part[:, LANES:]
            return part_re * cos + part_im * sin, part_im * cos - part_re * sin

        table = inner_ref[:, re_at.start : im_at.stop]
        body = dot(lhs[...], table)
        ends = dot(edge[...], table[BLOCK - LANES :])
        totals = [turned(ends[number * rows : (number + 1) * rows], -1) for number in range(NSEG)]
        for block in range(blocks):
            part_re, part_im = turned(body[block * rows : (block + 1) * rows], block)
            for number in range(NSEG):
                factor = whole[number][block]
                total_re, total_im = totals[number]
                totals[number] = total_re + factor * part_re, total_im + factor * part_im
        for index, (number, block) in enumerate(cuts):
            at = (blocks + index) * rows
            part_re, part_im = turned(body[at : at + rows], block)
            total_re, total_im = totals[number]
            totals[number] = total_re + part_re, total_im + part_im
        for number, (total_re, total_im) in enumerate(totals):
            at = slice(number * rows, (number + 1) * rows)
            own_ref[at, re_at] = total_re
            own_ref[at, im_at] = total_im
            send_ref[at, re_at] = total_re.astype(jnp.bfloat16)
            send_ref[at, im_at] = total_im.astype(jnp.bfloat16)


def partial_spectrum(info, recv, group):
    rows = HALVES * group
    peers = recv.shape[0]
    blocks = peers * (recv.shape[1] - group) // rows * LANES // BLOCK
    many = NSEG * rows
    return pl.pallas_call(
        spectrum_kernel,
        out_shape=[
            jax.ShapeDtypeStruct((many, 2 * NBIN), jnp.float32),
            jax.ShapeDtypeStruct((many, 2 * NBIN), jnp.bfloat16),
        ],
        in_specs=[VMEM] * 4,
        out_specs=[VMEM, VMEM],
        scratch_shapes=[
            pltpu.VMEM(((blocks + 2 * NSEG) * rows, BLOCK), jnp.bfloat16),
            pltpu.VMEM((many, LANES), jnp.bfloat16),
            pltpu.SMEM(info.shape, jnp.int32),
            pltpu.SemaphoreType.DMA,
        ],
        compiler_params=pltpu.CompilerParams(vmem_limit_bytes=12 * 1024 * 1024),
        name="spectrum",
    )(info, recv, inner_table(), phase_table(-1, HALVES * blocks + 1))


def whiten_kernel(own_ref, other_ref, band_ref, out_ref):
    total = own_ref[...] + other_ref[...].astype(jnp.float32)
    real_part = jnp.concatenate([total[:, places(chunk)[0]] for chunk in range(CHUNKS)], axis=1)
    imag_part = jnp.concatenate([total[:, places(chunk)[1]] for chunk in range(CHUNKS)], axis=1)
    energy = real_part * real_part + imag_part * imag_part
    high = energy.astype(jnp.bfloat16)
    low = (energy - high.astype(jnp.float32)).astype(jnp.bfloat16)
    smooth = (dot(high, band_ref[...]) + dot(low, band_ref[...])) / 65.0
    inverse = lax.rsqrt(smooth + 1e-05)
    white = []
    for chunk in range(CHUNKS):
        at = slice(chunk * LANES, (chunk + 1) * LANES)
        white += [real_part[:, at] * inverse[:, at], imag_part[:, at] * inverse[:, at]]
    white = jnp.concatenate(white, axis=1).astype(jnp.bfloat16)
    for peer in range(out_ref.shape[0]):
        out_ref[peer] = white


def whiten(own, other, peers):
    return pl.pallas_call(
        whiten_kernel,
        out_shape=jax.ShapeDtypeStruct((peers, *own.shape), jnp.bfloat16),
        in_specs=[VMEM] * 3,
        out_specs=VMEM,
        compiler_params=pltpu.CompilerParams(vmem_limit_bytes=12 * 1024 * 1024),
        name="whiten",
    )(own, other, band_table())


def correlate_kernel(groups, group, block, info_vmem, *refs):
    spectra = refs[:groups]
    basis_ref, out_ref, source, near, receiver, cross_even, cross_odd, lagged, sent, info_ref, told = refs[groups:]
    rows = HALVES * group
    channels = spectra[0].shape[0] * rows
    receivers = groups * group
    blocks = sent.shape[0]
    tell = pltpu.make_async_copy(info_vmem, info_ref, told)
    tell.start()

    def widen(chunk):
        for step, spectrum in enumerate(spectra):
            for number in range(NSEG):
                for part, columns in enumerate(places(chunk)):
                    held = spectrum[:, number * rows : (number + 1) * rows, columns]
                    held = held.astype(jnp.float32).reshape(channels, LANES)
                    at = slice(step * channels, (step + 1) * channels)
                    source[number, 2 * chunk + part, at, :] = held

    for chunk in range(CHUNKS):
        widen(chunk)
    tell.wait()
    half, peer, mine = info_ref[0], info_ref[1], info_ref[2]

    for step, spectrum in enumerate(spectra):
        owner = lax.rem(mine + step, groups)
        for number in range(NSEG):
            here = spectrum[position(peer), number * rows : (number + 1) * rows, :].astype(jnp.float32)
            here = jnp.where(half == 0, here[:group], here[group:]) * (1.0 / NSEG)
            near[number, owner] = here

    for number in range(NSEG):
        receiver[number] = near[number].reshape(receivers, 2 * NBIN).astype(jnp.bfloat16)

    def fill(number, cross, chunks):
        for chunk in chunks:
            re_at, im_at = places(chunk)
            recv_re = [receiver[seg, :, re_at] for seg in range(NSEG)]
            recv_im = [receiver[seg, :, im_at] for seg in range(NSEG)]
            for k in range(block):
                total_re = total_im = None
                same = pl.ds(info_ref[3 + number * block + k], 8, stride=0)
                for seg in range(NSEG):
                    source_re = source[seg, 2 * chunk, same, :]
                    source_im = source[seg, 2 * chunk + 1, same, :]
                    source_re = jnp.concatenate([source_re] * (receivers // 8), axis=0)
                    source_im = jnp.concatenate([source_im] * (receivers // 8), axis=0)
                    source_re = source_re.astype(jnp.bfloat16)
                    source_im = source_im.astype(jnp.bfloat16)
                    part_re = source_re * recv_re[seg] + source_im * recv_im[seg]
                    part_im = source_re * recv_im[seg] - source_im * recv_re[seg]
                    total_re = part_re if seg == 0 else total_re + part_re
                    total_im = part_im if seg == 0 else total_im + part_im
                at = slice(k * receivers, (k + 1) * receivers)
                cross[at, re_at] = total_re
                cross[at, im_at] = total_im

    size = block * receivers

    def span(number):
        return pl.ds(pl.multiple_of(number * size, size), size)

    def lag(number, cross):
        lagged[span(number), :] = dot(cross[...], basis_ref[...]).astype(jnp.bfloat16)

    def store(number):
        at = span(number)
        return pltpu.make_async_copy(lagged.at[at], out_ref.at[at], sent.at[number])

    everything = range(CHUNKS)
    fill(0, cross_even, everything)

    def pair(number):
        lag(2 * number, cross_even)
        fill(2 * number + 1, cross_odd, everything)
        store(2 * number).start()

    def step(number, carry):
        pair(number)
        lag(2 * number + 1, cross_odd)
        fill(2 * number + 2, cross_even, everything)
        store(2 * number + 1).start()
        return carry

    last = blocks // 2 - 1
    lax.fori_loop(0, last, step, 0)
    pair(last)
    lag(2 * last + 1, cross_odd)
    store(2 * last + 1).start()

    def finish(number, carry):
        store(number).wait()
        return carry

    lax.fori_loop(0, blocks, finish, 0)


def correlate(info, spectra, group):
    groups = len(spectra)
    many = info.shape[0] - 3
    receivers = groups * group
    channels = groups * spectra[0].shape[0] * HALVES * group
    block = 256 // receivers
    rows = block * receivers

    def kernel(*refs):
        correlate_kernel(groups, group, block, *refs)

    held = sum(spectrum.size * spectrum.dtype.itemsize for spectrum in spectra)
    return pl.pallas_call(
        kernel,
        out_shape=jax.ShapeDtypeStruct((many * receivers, NLAG), jnp.bfloat16),
        in_specs=[VMEM] * (groups + 2),
        out_specs=pl.BlockSpec(memory_space=pl.ANY),
        scratch_shapes=[
            pltpu.VMEM((NSEG, 2 * CHUNKS, channels + 8, LANES), jnp.float32),
            pltpu.VMEM((NSEG, groups, group, 2 * NBIN), jnp.float32),
            pltpu.VMEM((NSEG, receivers, 2 * NBIN), jnp.bfloat16),
            pltpu.VMEM((rows, 2 * NBIN), jnp.bfloat16),
            pltpu.VMEM((rows, 2 * NBIN), jnp.bfloat16),
            pltpu.VMEM((many * receivers, NLAG), jnp.bfloat16),
            pltpu.SemaphoreType.DMA((many // block,)),
            pltpu.SMEM(info.shape, jnp.int32),
            pltpu.SemaphoreType.DMA,
        ],
        compiler_params=pltpu.CompilerParams(
            vmem_limit_bytes=min(10 * 1024 * 1024 + 3 * held, 63 * 1024 * 1024)
        ),
        name="correlate",
    )(info, *spectra, lag_table())


def source_rows(src_chan, group_count, local_rows, peers, per_device):
    mine = lax.axis_index("src")
    many = src_chan.shape[0] // group_count
    wanted = lax.dynamic_slice_in_dim(src_chan, mine * many, many, 0)
    step = jnp.mod(wanted // local_rows - mine, group_count)
    local = wanted % local_rows
    half, inside = local // (local_rows // HALVES), local % (local_rows // HALVES)
    place = position(inside // per_device) * HALVES + half
    return step * local_rows + place * per_device + inside % per_device


def on_device(strain, seg_start, src_chan):
    chan_count = lax.axis_size("chan")
    group_count = lax.axis_size("src")
    peers = chan_count // HALVES
    per_device = strain.shape[0] // chan_count
    index = lax.axis_index("chan")
    half = (index // peers).reshape(1).astype(jnp.int32)
    place = jnp.stack([index // peers, index % peers, lax.axis_index("src")]).astype(jnp.int32)
    rows = source_rows(src_chan, group_count, strain.shape[0], peers, per_device)
    cubes = [[half * peers + peer for peer in ordered(peers)] for half in range(HALVES)]

    sent = decimate(strain, peers, per_device)
    samples = lax.all_to_all(sent, "chan", 0, 0, tiled=True, axis_index_groups=cubes)
    own, send = partial_spectrum(jnp.concatenate([half, seg_start]), samples, per_device)
    across = [(i, (i + peers) % chan_count) for i in range(chan_count)]
    white = whiten(own, lax.ppermute(send, "chan", across), peers)
    held = lax.all_to_all(white, "chan", 0, 0, tiled=True, axis_index_groups=cubes)
    spectra = [held]
    for step in range(1, group_count):
        pairs = [((i + step) % group_count, i) for i in range(group_count)]
        spectra.append(lax.ppermute(held, "src", pairs))
    lagged = correlate(jnp.concatenate([place, rows]), spectra, per_device)
    return lagged.reshape(-1, group_count, per_device, NLAG)


def solution(mesh):
    return jax.shard_map(
        on_device,
        mesh=mesh,
        in_specs=(P("src", "chan"), P(), P()),
        out_specs=P("src", None, "chan", None),
        check_vma=False,
    )
```

```python
import math

import jax
import jax.numpy as jnp
import numpy as np
from jax import lax
from jax.experimental import pallas as pl
from jax.experimental.pallas import tpu as pltpu
from jax.sharding import PartitionSpec as P

DEC = 4
SEG = 7680
NSEG = 3
BIN_LOW = 61
NBIN = 384
NLAG = 512
LANES = 128
BLOCK = 512
HALVES = 2
CHUNKS = NBIN // LANES
VMEM = pl.BlockSpec(memory_space=pltpu.VMEM)
SMEM = pl.BlockSpec(memory_space=pltpu.SMEM)


def ordered(peers):
    return [place ^ (place >> 1) for place in range(peers)]


def position(peer):
    peer = peer ^ (peer >> 1)
    peer = peer ^ (peer >> 2)
    return peer ^ (peer >> 4)


def chunked(real, imag):
    parts = np.stack([real, imag], axis=1).reshape(-1, 2, CHUNKS, LANES)
    return parts.transpose(0, 2, 1, 3).reshape(-1, 2 * NBIN)


def places(chunk):
    start = 2 * chunk * LANES
    return slice(start, start + LANES), slice(start + LANES, start + 2 * LANES)


def filter_table():
    length = 4 * DEC
    offsets = np.arange(length)
    centred = (offsets - (length - 1) / 2.0) / DEC
    coeffs = (
        np.sin(np.pi * centred)
        / (np.pi * centred)
        * (0.54 - 0.46 * np.cos(2.0 * np.pi * (offsets + 0.5) / length))
    )
    coeffs = coeffs / coeffs.sum()
    first = np.concatenate([np.arange(LANES), np.arange(LANES) - LANES])
    tap = np.arange(BLOCK)[:, None] - DEC * first[None, :]
    inside = (tap >= 0) & (tap < length)
    values = np.where(inside, coeffs[np.clip(tap, 0, length - 1)], 0.0)
    return jnp.asarray(values, jnp.float32).astype(jnp.bfloat16)


def inner_table():
    bin_ids = BIN_LOW + np.arange(NBIN)
    angle = 2.0 * np.pi * np.mod(np.outer(np.arange(BLOCK), bin_ids), SEG) / SEG
    parts = chunked(np.cos(angle), -np.sin(angle))
    return jnp.asarray(parts, jnp.float32).astype(jnp.bfloat16)


def phase_table(first, count):
    bin_ids = BIN_LOW + np.arange(NBIN)
    angle = 2.0 * np.pi * np.mod(np.outer(BLOCK * (first + np.arange(count)), bin_ids), SEG) / SEG
    parts = chunked(np.cos(angle), np.sin(angle)) / math.sqrt(SEG)
    return jnp.asarray(parts.reshape(count, 1, 2 * NBIN), jnp.float32)


def lag_table():
    bin_ids = BIN_LOW + np.arange(NBIN)
    delays = np.arange(NLAG) - NLAG // 2
    angles = 2.0 * np.pi * np.mod(np.outer(bin_ids, delays), SEG) / SEG
    basis = chunked(np.cos(angles).T, -np.sin(angles).T).T / np.sqrt(NBIN)
    return jnp.asarray(basis, jnp.float32).astype(jnp.bfloat16)


def band_table():
    offsets = np.arange(NBIN)
    band = np.abs(offsets[:, None] - offsets[None, :]) <= 32
    return jnp.asarray(band.astype(np.float32)).astype(jnp.bfloat16)


def dot(left, right):
    return jnp.dot(left, right, preferred_element_type=jnp.float32)


def decimate_kernel(strain_ref, table_ref, out_ref):
    halves, rows, length = strain_ref.shape
    tiles = length // BLOCK
    group = out_ref.shape[1] // (halves * tiles + 1)
    wide = halves * group
    many = halves * rows
    first = pl.program_id(0) * (rows // group)
    x = strain_ref[...].reshape(many, length)
    stacked = [x[:, tile * BLOCK : (tile + 1) * BLOCK] for tile in range(tiles)]
    sums = dot(jnp.concatenate(stacked, axis=0), table_ref[...])
    for tile in range(tiles + 1):
        if tile == tiles:
            values = sums[:many, LANES:]
        else:
            values = sums[tile * many : (tile + 1) * many, :LANES]
        if tile + 1 < tiles:
            values = values + sums[(tile + 1) * many : (tile + 2) * many, LANES:]
        for peer in range(rows // group):
            part = [
                values[half * rows + peer * group : half * rows + (peer + 1) * group]
                for half in range(halves)
            ]
            place = position(first + peer) - first
            if tile < tiles:
                part = jnp.concatenate(part, axis=0).astype(jnp.bfloat16)
                out_ref[place, tile * wide : (tile + 1) * wide, :] = part
            else:
                part = part[0] + pltpu.roll(part[1], LANES // 2, axis=1)
                out_ref[place, tiles * wide :, :] = part.astype(jnp.bfloat16)


def decimate(strain, peers, group):
    rows, length = strain.shape
    half_rows = rows // HALVES
    many = length // BLOCK * HALVES * group + group
    steps = 2
    return pl.pallas_call(
        decimate_kernel,
        out_shape=jax.ShapeDtypeStruct((peers, many, LANES), jnp.bfloat16),
        grid=(steps,),
        in_specs=[
            pl.BlockSpec((HALVES, half_rows // steps, length), lambda i: (0, i, 0)),
            pl.BlockSpec((BLOCK, 2 * LANES), lambda i: (0, 0)),
        ],
        out_specs=pl.BlockSpec((peers // steps, many, LANES), lambda i: (i, 0, 0)),
        name="decimate",
    )(strain.reshape(HALVES, half_rows, length), filter_table())


def spectrum_kernel(info_vmem, recv_ref, inner_ref, phase_ref, own_ref, send_ref, lhs, edge, info_ref, told):
    peers, many, _ = recv_ref.shape
    rows = own_ref.shape[0] // NSEG
    group = rows // HALVES
    tiles = (many - group) // rows
    span = tiles * LANES
    blocks = peers * span // BLOCK
    spot = lax.broadcasted_iota(jnp.int32, (rows, LANES), 1)

    def tail(peer):
        held = recv_ref[position(peer), tiles * rows :, :].astype(jnp.float32)
        held = jnp.concatenate([held, pltpu.roll(held, LANES // 2, axis=1)], axis=0)
        return jnp.where(spot >= LANES // 2, held, 0.0)

    tell = pltpu.make_async_copy(info_vmem, info_ref, told)
    tell.start()

    for peer in range(peers):
        for tile in range(span // LANES):
            values = recv_ref[position(peer), tile * rows : (tile + 1) * rows, :]
            if tile == span // LANES - 1 and peer + 1 < peers:
                values = (values.astype(jnp.float32) + tail(peer + 1)).astype(jnp.bfloat16)
            block, inside = divmod(peer * span + tile * LANES, BLOCK)
            lhs[block * rows : (block + 1) * rows, inside : inside + LANES] = values

    tell.wait()
    base = info_ref[0] * (peers * span)
    first = info_ref[0] * blocks + 1
    starts = [info_ref[1 + number] - base for number in range(NSEG)]

    cuts = []
    lane = lax.broadcasted_iota(jnp.int32, (rows, BLOCK), 1)
    for number, start in enumerate(starts):
        offset = jnp.bitwise_and(start, BLOCK - 1)
        for side, limit in enumerate((start, start + SEG)):
            block = lax.shift_right_arithmetic(limit, jnp.int32(BLOCK.bit_length() - 1))
            held = jnp.clip(block, 0, blocks - 1)
            cut = (block == held) & (offset != 0)
            kept = jnp.where(side == 0, lane >= offset, lane < offset)
            values = lhs[pl.ds(pl.multiple_of(held * rows, rows), rows), :].astype(jnp.float32)
            values = jnp.where(kept & cut, values, 0.0).astype(jnp.bfloat16)
            row = (blocks + len(cuts)) * rows
            lhs[row : row + rows, :] = values
            cuts.append((number, held))
    before = lax.broadcasted_iota(jnp.int32, (rows, LANES), 1) - LANES
    carried = tail(0)
    for number, start in enumerate(starts):
        kept = (before >= start) & (before < start + SEG)
        values = jnp.where(kept, carried, 0.0).astype(jnp.bfloat16)
        edge[number * rows : (number + 1) * rows, :] = values

    whole = [
        [
            ((start <= block * BLOCK) & ((block + 1) * BLOCK <= start + SEG)).astype(jnp.float32)
            for block in range(blocks)
        ]
        for start in starts
    ]
    for chunk in range(CHUNKS):
        re_at, im_at = places(chunk)

        def turned(part, block):
            cos, sin = phase_ref[first + block, :, re_at], phase_ref[first + block, :, im_at]
            part_re, part_im = part[:, :LANES], part[:, LANES:]
            return part_re * cos + part_im * sin, part_im * cos - part_re * sin

        table = inner_ref[:, re_at.start : im_at.stop]
        body = dot(lhs[...], table)
        ends = dot(edge[...], table[BLOCK - LANES :])
        totals = [turned(ends[number * rows : (number + 1) * rows], -1) for number in range(NSEG)]
        for block in range(blocks):
            part_re, part_im = turned(body[block * rows : (block + 1) * rows], block)
            for number in range(NSEG):
                factor = whole[number][block]
                total_re, total_im = totals[number]
                totals[number] = total_re + factor * part_re, total_im + factor * part_im
        for index, (number, block) in enumerate(cuts):
            at = (blocks + index) * rows
            part_re, part_im = turned(body[at : at + rows], block)
            total_re, total_im = totals[number]
            totals[number] = total_re + part_re, total_im + part_im
        for number, (total_re, total_im) in enumerate(totals):
            at = slice(number * rows, (number + 1) * rows)
            own_ref[at, re_at] = total_re
            own_ref[at, im_at] = total_im
            send_ref[at, re_at] = total_re.astype(jnp.bfloat16)
            send_ref[at, im_at] = total_im.astype(jnp.bfloat16)


def partial_spectrum(info, recv, group):
    rows = HALVES * group
    peers = recv.shape[0]
    blocks = peers * (recv.shape[1] - group) // rows * LANES // BLOCK
    many = NSEG * rows
    return pl.pallas_call(
        spectrum_kernel,
        out_shape=[
            jax.ShapeDtypeStruct((many, 2 * NBIN), jnp.float32),
            jax.ShapeDtypeStruct((many, 2 * NBIN), jnp.bfloat16),
        ],
        in_specs=[VMEM] * 4,
        out_specs=[VMEM, VMEM],
        scratch_shapes=[
            pltpu.VMEM(((blocks + 2 * NSEG) * rows, BLOCK), jnp.bfloat16),
            pltpu.VMEM((many, LANES), jnp.bfloat16),
            pltpu.SMEM(info.shape, jnp.int32),
            pltpu.SemaphoreType.DMA,
        ],
        compiler_params=pltpu.CompilerParams(vmem_limit_bytes=12 * 1024 * 1024),
        name="spectrum",
    )(info, recv, inner_table(), phase_table(-1, HALVES * blocks + 1))


def whiten_kernel(own_ref, other_ref, band_ref, out_ref):
    total = own_ref[...] + other_ref[...].astype(jnp.float32)
    real_part = jnp.concatenate([total[:, places(chunk)[0]] for chunk in range(CHUNKS)], axis=1)
    imag_part = jnp.concatenate([total[:, places(chunk)[1]] for chunk in range(CHUNKS)], axis=1)
    energy = real_part * real_part + imag_part * imag_part
    high = energy.astype(jnp.bfloat16)
    low = (energy - high.astype(jnp.float32)).astype(jnp.bfloat16)
    smooth = (dot(high, band_ref[...]) + dot(low, band_ref[...])) / 65.0
    inverse = lax.rsqrt(smooth + 1e-05)
    white = []
    for chunk in range(CHUNKS):
        at = slice(chunk * LANES, (chunk + 1) * LANES)
        white += [real_part[:, at] * inverse[:, at], imag_part[:, at] * inverse[:, at]]
    white = jnp.concatenate(white, axis=1).astype(jnp.bfloat16)
    for peer in range(out_ref.shape[0]):
        out_ref[peer] = white


def whiten(own, other, peers):
    return pl.pallas_call(
        whiten_kernel,
        out_shape=jax.ShapeDtypeStruct((peers, *own.shape), jnp.bfloat16),
        in_specs=[VMEM] * 3,
        out_specs=VMEM,
        compiler_params=pltpu.CompilerParams(vmem_limit_bytes=12 * 1024 * 1024),
        name="whiten",
    )(own, other, band_table())


def correlate_kernel(groups, group, block, info_vmem, *refs):
    spectra = refs[:groups]
    basis_ref, out_ref, source, near, receiver, cross_even, cross_odd, lagged, sent, info_ref, told = refs[groups:]
    rows = HALVES * group
    channels = spectra[0].shape[0] * rows
    receivers = groups * group
    blocks = sent.shape[0] - 1
    tell = pltpu.make_async_copy(info_vmem, info_ref, told)
    tell.start()

    def widen(chunk):
        for step, spectrum in enumerate(spectra):
            for number in range(NSEG):
                for part, columns in enumerate(places(chunk)):
                    held = spectrum[:, number * rows : (number + 1) * rows, columns]
                    held = held.astype(jnp.float32).reshape(channels, LANES)
                    at = slice(step * channels, (step + 1) * channels)
                    source[number, 2 * chunk + part, at, :] = held

    for chunk in range(CHUNKS):
        widen(chunk)
    tell.wait()
    half, peer, mine = info_ref[0], info_ref[1], info_ref[2]

    for step, spectrum in enumerate(spectra):
        owner = lax.rem(mine + step, groups)
        for number in range(NSEG):
            here = spectrum[position(peer), number * rows : (number + 1) * rows, :].astype(jnp.float32)
            here = jnp.where(half == 0, here[:group], here[group:]) * (1.0 / NSEG)
            near[number, owner] = here

    for number in range(NSEG):
        receiver[number] = near[number].reshape(receivers, 2 * NBIN).astype(jnp.bfloat16)

    def fill(number, cross, chunks):
        for chunk in chunks:
            re_at, im_at = places(chunk)
            recv_re = [receiver[seg, :, re_at] for seg in range(NSEG)]
            recv_im = [receiver[seg, :, im_at] for seg in range(NSEG)]
            for k in range(block):
                total_re = total_im = None
                same = pl.ds(info_ref[3 + number * block + k], 8, stride=0)
                for seg in range(NSEG):
                    source_re = source[seg, 2 * chunk, same, :]
                    source_im = source[seg, 2 * chunk + 1, same, :]
                    source_re = jnp.concatenate([source_re] * (receivers // 8), axis=0)
                    source_im = jnp.concatenate([source_im] * (receivers // 8), axis=0)
                    source_re = source_re.astype(jnp.bfloat16)
                    source_im = source_im.astype(jnp.bfloat16)
                    part_re = source_re * recv_re[seg] + source_im * recv_im[seg]
                    part_im = source_re * recv_im[seg] - source_im * recv_re[seg]
                    total_re = part_re if seg == 0 else total_re + part_re
                    total_im = part_im if seg == 0 else total_im + part_im
                at = slice(k * receivers, (k + 1) * receivers)
                cross[at, re_at] = total_re
                cross[at, im_at] = total_im

    size = block * receivers

    def span(number):
        return pl.ds(pl.multiple_of(number * size, size), size)

    def lag(number, cross):
        lagged[span(number), :] = dot(cross[...], basis_ref[...]).astype(jnp.bfloat16)

    def store(number):
        at = span(number)
        return pltpu.make_async_copy(lagged.at[at], out_ref.at[at], sent.at[number])

    everything = range(CHUNKS)
    fill(0, cross_even, everything)

    def pair(number):
        lag(2 * number, cross_even)
        fill(2 * number + 1, cross_odd, everything)
        store(2 * number).start()

    def step(number, carry):
        pair(number)
        lag(2 * number + 1, cross_odd)
        fill(2 * number + 2, cross_even, everything)
        store(2 * number + 1).start()
        return carry

    last = blocks // 2 - 1
    lax.fori_loop(0, last, step, 0)
    pair(last)
    lag(2 * last + 1, cross_odd)
    parts = []
    for part in range(2):
        at = pl.ds((blocks - 1) * size + part * (size // 2), size // 2)
        parts.append(pltpu.make_async_copy(lagged.at[at], out_ref.at[at], sent.at[blocks - 1 + part]))
        parts[-1].start()

    def finish(number, carry):
        store(number).wait()
        return carry

    lax.fori_loop(0, blocks - 1, finish, 0)
    for part in parts:
        part.wait()


def correlate(info, spectra, group):
    groups = len(spectra)
    many = info.shape[0] - 3
    receivers = groups * group
    channels = groups * spectra[0].shape[0] * HALVES * group
    block = 256 // receivers
    rows = block * receivers

    def kernel(*refs):
        correlate_kernel(groups, group, block, *refs)

    held = sum(spectrum.size * spectrum.dtype.itemsize for spectrum in spectra)
    return pl.pallas_call(
        kernel,
        out_shape=jax.ShapeDtypeStruct((many * receivers, NLAG), jnp.bfloat16),
        in_specs=[VMEM] * (groups + 2),
        out_specs=pl.BlockSpec(memory_space=pl.ANY),
        scratch_shapes=[
            pltpu.VMEM((NSEG, 2 * CHUNKS, channels + 8, LANES), jnp.float32),
            pltpu.VMEM((NSEG, groups, group, 2 * NBIN), jnp.float32),
            pltpu.VMEM((NSEG, receivers, 2 * NBIN), jnp.bfloat16),
            pltpu.VMEM((rows, 2 * NBIN), jnp.bfloat16),
            pltpu.VMEM((rows, 2 * NBIN), jnp.bfloat16),
            pltpu.VMEM((many * receivers, NLAG), jnp.bfloat16),
            pltpu.SemaphoreType.DMA((many // block + 1,)),
            pltpu.SMEM(info.shape, jnp.int32),
            pltpu.SemaphoreType.DMA,
        ],
        compiler_params=pltpu.CompilerParams(
            vmem_limit_bytes=min(10 * 1024 * 1024 + 3 * held, 63 * 1024 * 1024)
        ),
        name="correlate",
    )(info, *spectra, lag_table())


def source_rows(src_chan, group_count, local_rows, peers, per_device):
    mine = lax.axis_index("src")
    many = src_chan.shape[0] // group_count
    wanted = lax.dynamic_slice_in_dim(src_chan, mine * many, many, 0)
    step = jnp.mod(wanted // local_rows - mine, group_count)
    local = wanted % local_rows
    half, inside = local // (local_rows // HALVES), local % (local_rows // HALVES)
    place = position(inside // per_device) * HALVES + half
    return step * local_rows + place * per_device + inside % per_device


def on_device(strain, seg_start, src_chan):
    chan_count = lax.axis_size("chan")
    group_count = lax.axis_size("src")
    peers = chan_count // HALVES
    per_device = strain.shape[0] // chan_count
    index = lax.axis_index("chan")
    half = (index // peers).reshape(1).astype(jnp.int32)
    place = jnp.stack([index // peers, index % peers, lax.axis_index("src")]).astype(jnp.int32)
    rows = source_rows(src_chan, group_count, strain.shape[0], peers, per_device)
    cubes = [[half * peers + peer for peer in ordered(peers)] for half in range(HALVES)]

    sent = decimate(strain, peers, per_device)
    samples = lax.all_to_all(sent, "chan", 0, 0, tiled=True, axis_index_groups=cubes)
    own, send = partial_spectrum(jnp.concatenate([half, seg_start]), samples, per_device)
    across = [(i, (i + peers) % chan_count) for i in range(chan_count)]
    white = whiten(own, lax.ppermute(send, "chan", across), peers)
    held = lax.all_to_all(white, "chan", 0, 0, tiled=True, axis_index_groups=cubes)
    spectra = [held]
    for step in range(1, group_count):
        pairs = [((i + step) % group_count, i) for i in range(group_count)]
        spectra.append(lax.ppermute(held, "src", pairs))
    lagged = correlate(jnp.concatenate([place, rows]), spectra, per_device)
    return lagged.reshape(-1, group_count, per_device, NLAG)


def solution(mesh):
    return jax.shard_map(
        on_device,
        mesh=mesh,
        in_specs=(P("src", "chan"), P(), P()),
        out_specs=P("src", None, "chan", None),
        check_vma=False,
    )
```
